256 devices in a mesh: tok: 64 (over z, x, core), head: 4 (over y).
Axes of the slice: x: 4, y: 4, z: 8, core: 2. Of those that a mesh axis runs over, the one named last changes fastest.
Arguments:
- atom_single: bfloat16 [30720, 128], P('tok'), may hold values from -80 to 80
- atom_bias: bfloat16 [30720, 4, 128], P('tok'), may hold values from -5 to 320
- atom_token: int32 [30720], P('tok'), may hold values from 0 to 3071, as said below
- atom_count: int32 [3072], P('tok'), may hold values from 1 to 19, as said below
- token_single: bfloat16 [3072, 384], P('tok'), may hold values from -80 to 80
- pair: bfloat16 [3072, 128, 3072], P('tok', 'head'), may hold values from -5 to 24
- atom_qkv: bfloat16 [128, 3, 128], replicated, may hold values from -0.5 to 0.5
- atom_wo: bfloat16 [128, 128], replicated, may hold values from -0.5 to 0.5
- atom_agg: bfloat16 [128, 384], replicated, may hold values from -0.5 to 0.5
- token_qkvg: bfloat16 [384, 4, 384], replicated, may hold values from -0.3125 to 0.3125
- pair_weight: bfloat16 [128, 16], P('head'), may hold values from -0.75 to 0.75
- token_wo: bfloat16 [384, 384], P('head'), may hold values from -0.3125 to 0.3125
Outputs:
- atom_out: bfloat16 [30720, 128], P('tok')
- token_out: bfloat16 [3072, 384], P('tok', 'head')
The draws below stay inside these ranges and needn't reach their ends.
Inputs may be any that keep to these rules, and one draw needn't show every extreme that they name: `atom_count`: the tokens of each aligned block of 192 tokens have 4 * 480 atoms together. `atom_token`: never falls; token t is named atom_count[t] times.
All inputs are finite; a program needn't handle non-finite values.
Results may differ from the reference program's by a relative error of at most 0.006.
Values may be sent and summed in bfloat16 or wider, within the bound.
A program may use at most 128 MiB of HBM per device.

```python
import math
import jax
import jax.numpy as jnp
from jax import lax

ATOM_W = 128
TOKEN_W = 384
HEADS = 16
PAIR_W = 128
ATOM_HEADS = 4
WQ = 32
WK = 128
BLOCK_DEVS = 4
TOK_DEV = 48
HEAD_SIZE = 24
ATOM_HEAD_SIZE = 32
TOKENS = 3072
ATOMS = 30720


def scaled(key, base, low, high):
    row_key, col_key = jax.random.split(key)
    rows, cols = base.shape
    row_scale = jnp.exp(jax.random.uniform(row_key, (rows, 1), jnp.float32, math.log(low), math.log(high)))
    col_scale = jnp.exp(jax.random.uniform(col_key, (1, cols), jnp.float32, math.log(low), math.log(high)))
    return base * row_scale * col_scale


def atom_layout(key):
    groups = TOKENS // (BLOCK_DEVS * TOK_DEV)
    half = BLOCK_DEVS // 2 * TOK_DEV
    level_key, light_key, perm_key, flip_key = jax.random.split(key, 4)
    level = jax.random.randint(level_key, (groups, BLOCK_DEVS // 2, 1), 1, 11)
    level = jnp.broadcast_to(level, (groups, BLOCK_DEVS // 2, TOK_DEV)).reshape(groups, half)
    light = jax.random.randint(light_key, (groups, half), 1, 2 * level)
    light = light.at[:, 0].set(1)
    orders = jax.vmap(lambda k: jax.random.permutation(k, half))(jax.random.split(perm_key, groups))
    heavy = 20 - jnp.take_along_axis(light, orders, axis=1)
    flip = jax.random.randint(flip_key, (groups, 1), 0, 2)
    first = jnp.where(flip == 1, heavy, light)
    second = jnp.where(flip == 1, light, heavy)
    return jnp.concatenate([first, second], axis=1).reshape(TOKENS).astype(jnp.int32)


def draw_atom_count(key, part):
    return atom_layout(key)


def draw_atom_token(key, part):
    counts = atom_layout(key)
    return jnp.repeat(jnp.arange(TOKENS, dtype=jnp.int32), counts, total_repeat_length=ATOMS).astype(jnp.int32)


def draw_atom_single(key, part):
    key = jax.random.fold_in(key, 13)
    base_key, scale_key = jax.random.split(key, 2)
    shape = (ATOMS, ATOM_W)
    base = jnp.clip(jax.random.normal(base_key, shape, jnp.float32), -4.0, 4.0)
    return scaled(scale_key, base, 0.3, 3.0).astype(jnp.bfloat16)


def draw_token_single(key, part):
    key = jax.random.fold_in(key, 17)
    base_key, scale_key = jax.random.split(key, 2)
    shape = (TOKENS, TOKEN_W)
    base = jnp.clip(jax.random.normal(base_key, shape, jnp.float32), -4.0, 4.0)
    return scaled(scale_key, base, 0.3, 3.0).astype(jnp.bfloat16)


def draw_atom_bias(key, part):
    key = jax.random.fold_in(key, 3)
    shape = (ATOMS, ATOM_HEADS, WK)
    return jnp.clip(jax.random.normal(key, shape, jnp.float32), -5.0, 5.0).astype(jnp.bfloat16)


def draw_pair(key, part):
    key = jax.random.fold_in(key, 5)
    shape = (TOKENS, PAIR_W, TOKENS)
    return jnp.clip(jax.random.normal(key, shape, jnp.float32), -5.0, 5.0).astype(jnp.bfloat16)


def draw_pair_weight(key, part):
    key = jax.random.fold_in(key, 7)
    shape = (PAIR_W, HEADS)
    return jnp.clip(0.25 * jax.random.normal(key, shape, jnp.float32), -0.75, 0.75).astype(jnp.bfloat16)


def block_levels(key, extent, shards, smallest, high):
    loudness, own = 1.0, jax.random.fold_in(key, 6)
    for position, parts in shards:
        draws = jnp.exp(jax.random.uniform(jax.random.fold_in(own, position), (parts,), jnp.float32, smallest / len(shards), high / len(shards)))
        loudness = loudness * jnp.repeat(draws, extent[position] // parts).reshape([-1 if axis == position else 1 for axis in range(len(extent))])
    return loudness


def bell_draw(key, dims, deviation, reach, cuts=(), held_as=jnp.bfloat16):
    drawn = deviation * jax.random.normal(key, dims, jnp.float32)
    if cuts:
        drawn = drawn * block_levels(key, dims, cuts, -0.22, 0.18)
    return jnp.clip(drawn, -reach, reach).astype(held_as)


def setup_inputs(seed: int = 0) -> dict:
    key_of = jax.random.split(jax.random.key(seed), 13)
    atom_single = draw_atom_single(jax.random.fold_in(key_of[12], 71), 0)
    atom_bias = draw_atom_bias(jax.random.fold_in(key_of[12], 71), 0)
    atom_token = draw_atom_token(jax.random.fold_in(key_of[12], 71), 0)
    atom_count = draw_atom_count(jax.random.fold_in(key_of[12], 71), 0)
    token_single = draw_token_single(jax.random.fold_in(key_of[12], 71), 0)
    pair = draw_pair(jax.random.fold_in(key_of[12], 71), 0)
    atom_qkv = bell_draw(key_of[6], (ATOM_W, 3, ATOM_W), ATOM_W ** -0.5, 0.5)
    atom_wo = bell_draw(key_of[7], (ATOM_W, ATOM_W), ATOM_W ** -0.5, 0.5)
    atom_agg = bell_draw(key_of[8], (ATOM_W, TOKEN_W), ATOM_W ** -0.5, 0.5)
    token_qkvg = bell_draw(key_of[9], (TOKEN_W, 4, TOKEN_W), TOKEN_W ** -0.5, 0.3125)
    pair_weight = draw_pair_weight(jax.random.fold_in(key_of[12], 71), 0)
    token_wo = bell_draw(key_of[11], (TOKEN_W, TOKEN_W), TOKEN_W ** -0.5, 0.3125, ((0, 4),))
    return {"atom_single": atom_single, "atom_bias": atom_bias, "atom_token": atom_token, "atom_count": atom_count, "token_single": token_single, "pair": pair, "atom_qkv": atom_qkv, "atom_wo": atom_wo, "atom_agg": atom_agg, "token_qkvg": token_qkvg, "pair_weight": pair_weight, "token_wo": token_wo}


EPS = 1e-05
BLOCK_ROWS = 64

def normalize(rows):
    rows = rows.astype(jnp.float32)
    mean = lax.optimization_barrier(jnp.mean(rows, axis=-1, keepdims=True))
    centered = rows - mean
    spread = lax.optimization_barrier(jnp.mean(centered * centered, axis=-1, keepdims=True))
    return centered * lax.rsqrt(spread + EPS)

def window_keys(padded, windows):
    blocks = padded.reshape(windows + WK // WQ - 1, WQ, padded.shape[-1])
    return jnp.concatenate([blocks[i:i + windows] for i in range(WK // WQ)], axis=1)

def atom_block(atom_single, atom_bias, atom_qkv, atom_wo):
    total_atoms, width = atom_single.shape
    windows = total_atoms // WQ
    rim = (WK - WQ) // 2
    normed = normalize(atom_single).astype(jnp.bfloat16)
    proj = jnp.dot(normed, atom_qkv.reshape(width, 3 * width), preferred_element_type=jnp.float32)
    query = (proj[:, :width] * (1.0 / math.sqrt(ATOM_HEAD_SIZE))).astype(jnp.bfloat16)
    pairs = proj[:, width:].astype(jnp.bfloat16)
    padded = jnp.pad(pairs, ((rim, rim), (0, 0)))
    keyed = window_keys(padded, windows)
    spot = WQ * jnp.arange(windows, dtype=jnp.int32)[:, None] + jnp.arange(WK, dtype=jnp.int32)[None, :] - rim
    valid = (spot >= 0) & (spot < total_atoms)
    q_heads = query.reshape(windows, WQ, ATOM_HEADS, ATOM_HEAD_SIZE).astype(jnp.float32)
    k_heads = keyed[:, :, :width].reshape(windows, WK, ATOM_HEADS, ATOM_HEAD_SIZE).astype(jnp.float32)
    v_heads = keyed[:, :, width:].reshape(windows, WK, ATOM_HEADS, ATOM_HEAD_SIZE).astype(jnp.float32)
    score = jnp.einsum('wqhe,wkhe->whqk', q_heads, k_heads, precision=lax.Precision.HIGHEST)
    score = score + atom_bias.reshape(windows, WQ, ATOM_HEADS, WK).transpose(0, 2, 1, 3).astype(jnp.float32)
    score = jnp.where(valid[:, None, None, :], score, -1e+30)
    peak = lax.optimization_barrier(jnp.max(score, axis=-1, keepdims=True))
    expd = jnp.exp(score - peak)
    weight = (expd / lax.optimization_barrier(jnp.sum(expd, axis=-1, keepdims=True))).astype(jnp.bfloat16)
    mix = jnp.einsum('whqk,wkhe->wqhe', weight.astype(jnp.float32), v_heads, precision=lax.Precision.HIGHEST)
    mix = mix.reshape(total_atoms, width).astype(jnp.bfloat16)
    out = atom_single.astype(jnp.float32) + jnp.dot(mix, atom_wo, preferred_element_type=jnp.float32)
    return out.astype(jnp.bfloat16)

def reference(atom_single, atom_bias, atom_token, atom_count, token_single, pair, atom_qkv, atom_wo, atom_agg, token_qkvg, pair_weight, token_wo):
    atom_out = atom_block(atom_single, atom_bias, atom_qkv, atom_wo)
    feat = jax.nn.relu(jnp.dot(atom_out, atom_agg, preferred_element_type=jnp.float32)).astype(jnp.bfloat16)
    sums = jax.ops.segment_sum(feat.astype(jnp.float32), atom_token, num_segments=TOKENS)
    token_mid = token_single.astype(jnp.float32) + sums / atom_count.astype(jnp.float32)[:, None]
    normed = normalize(token_mid).astype(jnp.bfloat16)
    proj = jnp.dot(normed, token_qkvg.reshape(TOKEN_W, 4 * TOKEN_W), preferred_element_type=jnp.float32)
    proj = proj.reshape(TOKENS, 4, TOKEN_W)
    query = (proj[:, 0] * (1.0 / math.sqrt(HEAD_SIZE))).astype(jnp.bfloat16)
    keys = proj[:, 1].astype(jnp.bfloat16).astype(jnp.float32).reshape(TOKENS, HEADS, HEAD_SIZE)
    values = proj[:, 2].astype(jnp.bfloat16).astype(jnp.float32).reshape(TOKENS, HEADS, HEAD_SIZE)
    gate = jax.nn.sigmoid(proj[:, 3])
    weights_pair = pair_weight.astype(jnp.float32)
    blocks = TOKENS // BLOCK_ROWS

    def token_rows(block):
        pair_rows, query_rows, gate_rows = block
        bias = jnp.einsum('ick,ch->hik', pair_rows.astype(jnp.float32), weights_pair, precision=lax.Precision.HIGHEST)
        score = jnp.einsum('ihe,khe->hik', query_rows.astype(jnp.float32), keys, precision=lax.Precision.HIGHEST) + bias
        peak = lax.optimization_barrier(jnp.max(score, axis=-1, keepdims=True))
        expd = jnp.exp(score - peak)
        weight = expd / lax.optimization_barrier(jnp.sum(expd, axis=-1, keepdims=True))
        mix = jnp.einsum('hik,khe->ihe', weight, values, precision=lax.Precision.HIGHEST)
        return (mix.reshape(BLOCK_ROWS, TOKEN_W) * gate_rows).astype(jnp.bfloat16)
    mixed = lax.map(token_rows, (pair.reshape(blocks, BLOCK_ROWS, PAIR_W, TOKENS), query.reshape(blocks, BLOCK_ROWS, HEADS, HEAD_SIZE), gate.reshape(blocks, BLOCK_ROWS, TOKEN_W)))
    mixed = mixed.reshape(TOKENS, TOKEN_W)
    token_out = token_mid + jnp.dot(mixed, token_wo, preferred_element_type=jnp.float32)
    return (atom_out, token_out.astype(jnp.bfloat16))
```

```python
import functools
import math

import jax
import jax.numpy as jnp
from jax import lax
from jax.experimental import pallas as pl
from jax.experimental.pallas import tpu as pltpu
from jax.sharding import PartitionSpec as P

ATOM_HEADS = 4
WQ = 32
WK = 128
RIM = (WK - WQ) // 2
BLOCK_DEVS = 4
HEAD_SIZE = 24
ATOM_HEAD_SIZE = 32
EPS = 1e-05

Y = 4
CORES = 2
ROWS = 8
CH = 32
HL = 4
CHUNK = HL * ROWS
LANES = 128

PAIR_MID = 9.5
PAIR_HALF = 14.5
CODE_MAX = 32700.0

F32 = jnp.float32
BF16 = jnp.bfloat16
I16 = jnp.int16
MESH = pl.DeviceIdType.MESH

OPP_UP, OPP_DN, DIR_UP, DIR_DN, FWD_UP, FWD_DN = range(6)


def iota(shape, dim):
    return lax.broadcasted_iota(jnp.int32, shape, dim)


def dot(a, b):
    return jnp.dot(a, b, preferred_element_type=F32)


def dot_nt(a, b):
    return lax.dot_general(a, b, (((1,), (1,)), ((), ())), preferred_element_type=F32)


def mask(cond):
    return jnp.where(cond, 1.0, 0.0).astype(F32)


def normalize(rows):
    mean = jnp.mean(rows, axis=-1, keepdims=True)
    centered = rows - mean
    spread = jnp.mean(centered * centered, axis=-1, keepdims=True)
    return centered * lax.rsqrt(spread + EPS)


def fused(
    zs,
    xs,
    atom_single,
    atom_bias,
    atom_token,
    atom_count,
    token_single,
    pair,
    atom_qkv,
    atom_wo,
    atom_agg,
    token_qkvg,
    pair_weight,
    token_wo,
    atom_out,
    token_out,
    single_v,
    bias_v,
    tok_v,
    pair_v,
    aqkv_v,
    awo_v,
    agg_v,
    qkvg_v,
    two_v,
    kv_pad,
    weights,
    own,
    hold_up,
    hold_dn,
    opp_up_s,
    opp_dn_s,
    dir_up_s,
    dir_dn_s,
    fwd_up_s,
    fwd_dn_s,
    opp_up_r,
    opp_dn_r,
    dir_up_r,
    dir_dn_r,
    fwd_up_r,
    fwd_dn_r,
    sum_s,
    sum_r,
    kv_all,
    score,
    mixed,
    fin_s,
    fin_r,
    in_sem,
    pair_sem,
    halo_s,
    halo_r,
    w_s,
    w_r,
    y_s,
    y_r,
    sum_ss,
    sum_rs,
    z_s,
    z_r,
    x_s,
    x_r,
    c_s,
    c_r,
    fin_ss,
    fin_rs,
):
    tok = lax.axis_index("tok")
    y = lax.axis_index("head")
    devs = zs * xs * CORES
    z = lax.div(tok, xs * CORES)
    x = lax.rem(lax.div(tok, CORES), xs)
    c = lax.rem(tok, CORES)
    place = lax.rem(tok, BLOCK_DEVS)
    groups, depth, keys = pair_v.shape
    half = keys // 2
    here = token_single.shape[0]
    atoms = single_v.shape[0]
    windows = atoms // WQ

    def tok_of(z_, x_, c_):
        return (z_ * xs + x_) * CORES + c_

    def y_at(k):
        return lax.rem(y + k, Y)

    def mate(k):
        return tok - place + lax.rem(place + k, BLOCK_DEVS)

    nxt = lax.rem(tok + 1, devs)
    prv = lax.rem(tok + devs - 1, devs)
    up, dn = {"head": y_at(1)}, {"head": y_at(3)}

    def remote(src, dst, send, recv, device):
        return pltpu.make_async_remote_copy(
            src_ref=src,
            dst_ref=dst,
            send_sem=send,
            recv_sem=recv,
            device_id=device,
            device_id_type=MESH,
        )

    loads = [
        (atom_single, single_v),
        (atom_qkv, aqkv_v),
        (atom_bias, bias_v),
        (atom_wo, awo_v),
        (atom_agg, agg_v),
        (token_qkvg, qkvg_v),
        (token_single, tok_v),
        (token_wo, two_v),
    ]
    loads = [pltpu.make_async_copy(a, b, in_sem.at[i]) for i, (a, b) in enumerate(loads)]

    def pair_load(g):
        return pltpu.make_async_copy(
            pair.at[pl.ds(pl.multiple_of(g * depth, depth), depth), :],
            pair_v.at[g],
            pair_sem.at[g],
        )

    loads[0].start()
    loads[1].start()
    for g in range(groups):
        pair_load(g).start()
    for load in loads[2:]:
        load.start()

    partners = [{"head": y_at(k)} for k in range(1, Y)]
    partners += [{"tok": nxt}, {"tok": prv}]
    partners += [{"tok": mate(k)} for k in range(1, BLOCK_DEVS)]
    partners += [{"tok": tok_of(lax.rem(z + k, zs), x, c)} for k in range(1, zs)]
    partners += [{"tok": tok_of(z, lax.rem(x + k, xs), c)} for k in range(1, xs)]
    partners += [{"tok": tok_of(z, x, 1 - c)}]
    barrier = pltpu.get_barrier_semaphore()
    for partner in partners:
        pl.semaphore_signal(barrier, inc=1, device_id=partner, device_id_type=MESH)

    loads[0].wait()
    loads[1].wait()
    single = single_v[...].astype(F32)
    normed = normalize(single).astype(BF16)
    query = (dot(normed, aqkv_v[0]) * (1.0 / math.sqrt(ATOM_HEAD_SIZE))).astype(BF16)
    kv_pad[RIM : RIM + atoms, 0:LANES] = dot(normed, aqkv_v[1]).astype(BF16)
    kv_pad[RIM : RIM + atoms, LANES:] = dot(normed, aqkv_v[2]).astype(BF16)

    wt = pair_weight[...]
    heads = wt.shape[0]
    row = iota((Y * CHUNK, heads), 0)
    owner = lax.rem(y + lax.div(row, CHUNK), Y)
    pick = iota((Y * CHUNK, heads), 1) == owner * HL + lax.rem(lax.div(row, ROWS), HL)
    picked = dot(mask(pick).astype(BF16), wt).astype(BF16)
    spread = mask(iota((CH, depth), 0) == lax.rem(iota((CH, depth), 1), CH)).astype(BF16)
    diag = lax.div(iota((Y * CHUNK, depth), 1), CH) == lax.rem(iota((Y * CHUNK, depth), 0), ROWS)
    lhs = (dot(picked, spread) * mask(diag)).astype(BF16)
    picked_f = picked.astype(F32)
    mid = PAIR_MID * jnp.sum(picked_f, axis=1, keepdims=True)
    reach = jnp.maximum(PAIR_HALF * jnp.sum(jnp.abs(picked_f), axis=1, keepdims=True), 1e-20)
    inv = CODE_MAX / reach
    weights[0] = wt

    pl.semaphore_wait(barrier, len(partners))

    halo_up = remote(
        kv_pad.at[pl.ds(atoms, RIM), :],
        kv_pad.at[pl.ds(0, RIM), :],
        halo_s.at[0],
        halo_r.at[0],
        {"tok": nxt},
    )
    halo_dn = remote(
        kv_pad.at[pl.ds(RIM, RIM), :],
        kv_pad.at[pl.ds(atoms + RIM, RIM), :],
        halo_s.at[1],
        halo_r.at[1],
        {"tok": prv},
    )
    w_copies = [
        remote(weights.at[0], weights.at[Y - k], w_s.at[k], w_r.at[Y - k], {"head": y_at(k)})
        for k in range(1, Y)
    ]
    halo_up.start()
    halo_dn.start()
    for copy in w_copies:
        copy.start()

    buffers = {
        OPP_UP: (opp_up_s, opp_up_r, up),
        OPP_DN: (opp_dn_s, opp_dn_r, dn),
        DIR_UP: (dir_up_s, dir_up_r, up),
        DIR_DN: (dir_dn_s, dir_dn_r, dn),
        FWD_UP: (fwd_up_s, fwd_up_r, up),
        FWD_DN: (fwd_dn_s, fwd_dn_r, dn),
    }

    def piece(kind, g):
        src, dst, device = buffers[kind]
        return remote(src.at[g], dst.at[g], y_s.at[kind, g], y_r.at[kind, g], device)

    sub = half // 3 if half % 3 == 0 and (half // 3) % LANES == 0 else half

    def coded(value, scale):
        return jnp.round(value * scale).astype(jnp.int32).astype(I16)

    def produce(g, carry):
        pair_load(g).wait()
        for side in range(2):
            for at in range(0, half, sub):
                cols = slice(side * half + at, side * half + at + sub)
                into = slice(at, at + sub)
                part = dot(lhs, pair_v[g, :, cols])
                own[g, :, cols] = part[0:CHUNK]
                part = part[CHUNK:] - mid[CHUNK:]
                to_up, to_opp, to_dn = (part[i * CHUNK : (i + 1) * CHUNK] for i in range(3))
                i_up, i_opp, i_dn = (inv[i * CHUNK : (i + 1) * CHUNK] for i in range(1, Y))
                if side == 0:
                    opp_up_s[g, :, into] = coded(to_opp, i_opp)
                    hold_up[g, :, into] = to_up
                    dir_dn_s[g, :, into] = coded(to_dn, i_dn)
                else:
                    opp_dn_s[g, :, into] = coded(to_opp, i_opp)
                    hold_dn[g, :, into] = to_dn
                    dir_up_s[g, :, into] = coded(to_up, i_up)
            piece(OPP_UP if side == 0 else OPP_DN, g).start()
        piece(DIR_UP, g).start()
        piece(DIR_DN, g).start()
        return carry

    lax.fori_loop(0, groups, produce, 0)

    halo_up.wait()
    halo_dn.wait()
    loads[2].wait()
    wide = WQ * ATOM_HEADS
    grow = mask(lax.div(iota((wide, WQ), 0), ATOM_HEADS) == iota((wide, WQ), 1)).astype(BF16)
    fold = mask(iota((WQ, wide), 0) == lax.div(iota((WQ, wide), 1), ATOM_HEADS)).astype(BF16)
    in_head = mask(
        lax.div(iota((wide, LANES), 1), ATOM_HEAD_SIZE) == lax.rem(iota((wide, LANES), 0), ATOM_HEADS)
    )
    slot = iota((wide, WK), 1)
    scores = []
    for w in range(windows):
        q_rows = (dot(grow, query[w * WQ : (w + 1) * WQ]) * in_head).astype(BF16)
        s = dot_nt(q_rows, kv_pad[w * WQ : w * WQ + WK, 0:LANES])
        s = s + bias_v[w * wide : (w + 1) * wide, :].astype(F32)
        if w * WQ < RIM or w * WQ + WK > RIM + atoms:
            spot = tok * atoms + w * WQ - RIM + slot
            s = jnp.where((spot >= 0) & (spot < devs * atoms), s, -1e30)
        scores.append(s)
    probs = []
    for s in scores:
        e = jnp.exp(s - jnp.max(s, axis=-1, keepdims=True))
        probs.append((e * (1.0 / jnp.sum(e, axis=-1, keepdims=True))).astype(BF16))
    mixes = []
    for w in range(windows):
        m = dot(probs[w], kv_pad[w * WQ : w * WQ + WK, LANES:])
        mixes.append(dot(fold, (m * in_head).astype(BF16)).astype(BF16))
    mix = jnp.concatenate(mixes, axis=0)
    for load in loads[3:]:
        load.wait()
    a_out = (single + dot(mix, awo_v[...])).astype(BF16)
    atom_out[...] = a_out
    feat = jnp.maximum(dot(a_out, agg_v[...]), 0.0).astype(BF16)

    block = iota((BLOCK_DEVS * here, 1), 0)
    owner_tok = mate(lax.div(block, here)) * here + lax.rem(block, here)
    onehot = mask(owner_tok == atom_token[...]).astype(BF16)
    sums = dot(onehot, feat)
    sum_copies = []
    for k in range(1, BLOCK_DEVS):
        sum_s[k] = sums[k * here : (k + 1) * here].astype(BF16)
        copy = remote(
            sum_s.at[k],
            sum_r.at[BLOCK_DEVS - k],
            sum_ss.at[k],
            sum_rs.at[BLOCK_DEVS - k],
            {"tok": mate(k)},
        )
        copy.start()
        sum_copies.append(copy)

    for copy in w_copies:
        copy.wait()
    r32 = iota((CHUNK, heads), 0)

    def reach_of(sender, k):
        head = y_at(k) * HL + lax.div(r32, ROWS)
        sel = mask(iota((CHUNK, heads), 1) == head).astype(BF16)
        chosen = dot(sel, weights[sender])
        return jnp.maximum(PAIR_HALF * jnp.sum(jnp.abs(chosen), axis=1, keepdims=True), 1e-20)

    def forward(g, carry):
        for kind, out, hold, src, k, to in (
            (OPP_UP, fwd_up_s, hold_up, opp_up_r, 1, FWD_UP),
            (OPP_DN, fwd_dn_s, hold_dn, opp_dn_r, 3, FWD_DN),
        ):
            sender = Y - k
            theirs = reach_of(sender, k)
            both = theirs + reach_of(0, k)
            piece(kind, g).wait_recv()
            got = src[g].astype(F32) * (theirs * (1.0 / CODE_MAX))
            out[g] = coded(got + hold[g], CODE_MAX / both)
            piece(to, g).start()
        return carry

    lax.fori_loop(0, groups // 2, forward, 0)

    for copy in sum_copies:
        copy.wait()
    total = sums[0:here]
    for k in range(1, BLOCK_DEVS):
        total = total + sum_r[k].astype(F32)
    square = iota((here, here), 0) == iota((here, here), 1)
    count = jnp.sum(jnp.where(square, atom_count[...].astype(F32), 0.0), axis=1, keepdims=True)
    token_mid = tok_v[...].astype(F32) + total / count
    normed_t = normalize(token_mid).astype(BF16)
    columns = HL * HEAD_SIZE

    def mine(value):
        return pltpu.roll(value, lax.rem((Y - y) * columns, Y * columns), 1)[:, 0:LANES]

    parts = [mine(dot(normed_t, qkvg_v[:, i, :])) for i in range(4)]
    t_query = (parts[0] * (1.0 / math.sqrt(HEAD_SIZE))).astype(BF16)
    kv_all[z, x, c] = jnp.concatenate([parts[1], parts[2]], axis=1).astype(BF16)
    gate = jax.nn.sigmoid(parts[3])

    z_copies = []
    for k in range(1, zs):
        mineblock = kv_all.at[z, x, c]
        copy = remote(
            mineblock, mineblock, z_s.at[k], z_r.at[k], {"tok": tok_of(lax.rem(z + k, zs), x, c)}
        )
        copy.start()
        z_copies.append(copy)

    lax.fori_loop(groups // 2, groups, forward, 0)

    for k in range(1, zs):
        block_k = kv_all.at[lax.rem(z + zs - k, zs), x, c]
        remote(block_k, block_k, z_s.at[k], z_r.at[k], {"tok": tok}).wait_recv()
    x_copies = []
    for k in range(1, xs):
        column = kv_all.at[:, x, c]
        copy = remote(
            column, column, x_s.at[k], x_r.at[k], {"tok": tok_of(z, lax.rem(x + k, xs), c)}
        )
        copy.start()
        x_copies.append(copy)
    c_copies = []
    for k in range(xs):
        from_x = lax.rem(x + xs - k, xs)
        column = kv_all.at[:, from_x, c]
        if k:
            remote(column, column, x_s.at[k], x_r.at[k], {"tok": tok}).wait_recv()
        copy = remote(column, column, c_s.at[k], c_r.at[k], {"tok": tok_of(z, x, 1 - c)})
        copy.start()
        c_copies.append(copy)
    for k in range(xs):
        column = kv_all.at[:, lax.rem(x + xs - k, xs), 1 - c]
        remote(column, column, c_s.at[k], c_r.at[k], {"tok": tok}).wait_recv()

    rows = groups * CHUNK
    rr = iota((rows, here), 0)
    pick_row = lax.div(rr, CHUNK) * ROWS + lax.rem(rr, ROWS) == iota((rows, here), 1)
    rl = iota((rows, LANES), 0)
    of_head = mask(
        lax.div(iota((rows, LANES), 1), HEAD_SIZE) == lax.rem(lax.div(rl, ROWS), HL)
    )
    q_rows = (dot(mask(pick_row).astype(BF16), t_query) * of_head).astype(BF16)
    key_rows = kv_all[..., 0:LANES].reshape(keys, LANES)
    for at in range(0, keys, 2 * sub):
        s = dot_nt(q_rows, key_rows[at : at + 2 * sub])
        score[:, :, at : at + 2 * sub] = s.reshape(groups, CHUNK, 2 * sub)

    head_mask = of_head[0:CHUNK]

    def attend(g, carry):
        r_up, r_opp, r_dn = (reach_of(k, 0) for k in range(1, Y))
        for kind in (DIR_UP, DIR_DN, FWD_UP, FWD_DN):
            piece(kind, g).wait_recv()
        s_up, s_dn = r_up * (1.0 / CODE_MAX), r_dn * (1.0 / CODE_MAX)
        s_up2, s_dn2 = (r_up + r_opp) * (1.0 / CODE_MAX), (r_dn + r_opp) * (1.0 / CODE_MAX)
        peak = None
        for side, (a_ref, a_scale, b_ref, b_scale) in enumerate(
            ((fwd_up_r, s_dn2, dir_dn_r, s_up), (fwd_dn_r, s_up2, dir_up_r, s_dn))
        ):
            for at in range(0, half, sub):
                cols = slice(side * half + at, side * half + at + sub)
                into = slice(at, at + sub)
                s = score[g, :, cols] + own[g, :, cols]
                s = s + a_ref[g, :, into].astype(F32) * a_scale
                s = s + b_ref[g, :, into].astype(F32) * b_scale
                score[g, :, cols] = s
                high = jnp.max(s, axis=-1, keepdims=True)
                peak = high if peak is None else jnp.maximum(peak, high)
        norm = jnp.zeros((CHUNK, 1), F32)
        acc = jnp.zeros((CHUNK, LANES), F32)
        value_rows = kv_all[..., LANES:].reshape(keys, LANES)
        for at in range(0, keys, sub):
            e = jnp.exp(score[g, :, at : at + sub] - peak)
            norm = norm + jnp.sum(e, axis=-1, keepdims=True)
            acc = acc + dot(e.astype(BF16), value_rows[at : at + sub])
        acc = acc * head_mask / norm
        mixed[g] = jnp.sum(acc.reshape(HL, ROWS, LANES), axis=0)
        return carry

    lax.fori_loop(0, groups, attend, 0)

    out_rows = (mixed[...].reshape(here, LANES) * gate).astype(BF16)
    term = dot(out_rows[:, 0:columns], two_v[...])
    for k in range(1, Y):
        shift = lax.rem((2 * Y - y - k) * columns, Y * columns)
        fin_s[k] = pltpu.roll(term, shift, 1)[:, 0:LANES].astype(BF16)
    fin_copies = [
        remote(fin_s.at[k], fin_r.at[Y - k], fin_ss.at[k], fin_rs.at[Y - k], {"head": y_at(k)})
        for k in range(1, Y)
    ]
    for copy in fin_copies:
        copy.start()
    result = mine(term) + mine(token_mid)
    for copy in fin_copies:
        copy.wait()
    for k in range(1, Y):
        result = result + fin_r[k].astype(F32)
    token_out[...] = result[:, 0:columns].astype(BF16)

    for copy in z_copies + x_copies + c_copies:
        copy.wait_send()

    def drain(g, carry):
        for kind in range(6):
            piece(kind, g).wait_send()
        return carry

    lax.fori_loop(0, groups, drain, 0)


def per_device(
    atom_single,
    atom_bias,
    atom_token,
    atom_count,
    token_single,
    pair,
    atom_qkv,
    atom_wo,
    atom_agg,
    token_qkvg,
    pair_weight,
    token_wo,
):
    devs = lax.axis_size("tok")
    xs = 4 if devs >= 8 else devs // CORES
    zs = devs // (xs * CORES)
    atoms, width = atom_single.shape
    here, width_t = token_single.shape
    keys = pair.shape[2]
    groups = here // ROWS
    half = keys // 2
    columns = width_t // Y
    depth = ROWS * CH
    anywhere = pl.BlockSpec(memory_space=pl.ANY)
    vmem = pl.BlockSpec(memory_space=pltpu.VMEM)
    dma = pltpu.SemaphoreType.DMA
    code = pltpu.VMEM((groups, CHUNK, half), I16)
    operands = (
        atom_single,
        atom_bias.reshape(atoms * ATOM_HEADS, WK),
        atom_token.reshape(1, atoms),
        atom_count.reshape(1, here),
        token_single,
        pair.reshape(here * CH, keys),
        jnp.transpose(atom_qkv, (1, 0, 2)),
        atom_wo,
        atom_agg,
        token_qkvg,
        jnp.transpose(pair_weight),
        token_wo,
    )
    specs = [anywhere] * len(operands)
    for i in (2, 3, 10):
        specs[i] = vmem
    scratch = [
        pltpu.VMEM((atoms, width), BF16),
        pltpu.VMEM((atoms * ATOM_HEADS, WK), BF16),
        pltpu.VMEM((here, width_t), BF16),
        pltpu.VMEM((groups, depth, keys), BF16),
        pltpu.VMEM((3, width, width), BF16),
        pltpu.VMEM(atom_wo.shape, BF16),
        pltpu.VMEM(atom_agg.shape, BF16),
        pltpu.VMEM(token_qkvg.shape, BF16),
        pltpu.VMEM(token_wo.shape, BF16),
        pltpu.VMEM((atoms + 2 * RIM, 2 * width), BF16),
        pltpu.VMEM((Y, Y * HL, CH), BF16),
        pltpu.VMEM((groups, CHUNK, keys), F32),
        pltpu.VMEM((groups, CHUNK, half), F32),
        pltpu.VMEM((groups, CHUNK, half), F32),
        *([code] * 12),
        pltpu.VMEM((BLOCK_DEVS, here, width_t), BF16),
        pltpu.VMEM((BLOCK_DEVS, here, width_t), BF16),
        pltpu.VMEM((zs, xs, CORES, here, 2 * LANES), BF16),
        pltpu.VMEM((groups, CHUNK, keys), F32),
        pltpu.VMEM((groups, ROWS, LANES), F32),
        pltpu.VMEM((Y, here, LANES), BF16),
        pltpu.VMEM((Y, here, LANES), BF16),
        dma((8,)),
        dma((groups,)),
        dma((2,)),
        dma((2,)),
        dma((Y,)),
        dma((Y,)),
        dma((6, groups)),
        dma((6, groups)),
        dma((BLOCK_DEVS,)),
        dma((BLOCK_DEVS,)),
        dma((max(zs, 2),)),
        dma((max(zs, 2),)),
        dma((xs,)),
        dma((xs,)),
        dma((xs,)),
        dma((xs,)),
        dma((Y,)),
        dma((Y,)),
    ]
    return pl.pallas_call(
        functools.partial(fused, zs, xs),
        out_shape=(
            jax.ShapeDtypeStruct((atoms, width), BF16),
            jax.ShapeDtypeStruct((here, columns), BF16),
        ),
        in_specs=specs,
        out_specs=(vmem, vmem),
        scratch_shapes=scratch,
        compiler_params=pltpu.CompilerParams(
            collective_id=0, has_side_effects=True, vmem_limit_bytes=56 * 2**20
        ),
    )(*operands)


def solution(mesh):
    in_specs = (
        P("tok", None),
        P("tok", None, None),
        P("tok"),
        P("tok"),
        P("tok", None),
        P("tok", "head", None),
        P(),
        P(),
        P(),
        P(),
        P("head", None),
        P("head", None),
    )
    out_specs = (P("tok", None), P("tok", "head"))
    return jax.shard_map(
        per_device, mesh=mesh, in_specs=in_specs, out_specs=out_specs, check_vma=False
    )
```

```python
import functools
import math

import jax
import jax.numpy as jnp
from jax import lax
from jax.experimental import pallas as pl
from jax.experimental.pallas import tpu as pltpu
from jax.sharding import PartitionSpec as P

ATOM_HEADS = 4
WQ = 32
WK = 128
RIM = (WK - WQ) // 2
BLOCK_DEVS = 4
HEAD_SIZE = 24
ATOM_HEAD_SIZE = 32
EPS = 1e-05

Y = 4
CORES = 2
ROWS = 8
CH = 32
HL = 4
CHUNK = HL * ROWS
LANES = 128

PAIR_MID = 9.5
PAIR_HALF = 14.5
CODE_MAX = 32700.0

F32 = jnp.float32
BF16 = jnp.bfloat16
I16 = jnp.int16
MESH = pl.DeviceIdType.MESH

OPP_UP, OPP_DN, DIR_UP, DIR_DN, FWD_UP, FWD_DN = range(6)


def iota(shape, dim):
    return lax.broadcasted_iota(jnp.int32, shape, dim)


def dot(a, b):
    return jnp.dot(a, b, preferred_element_type=F32)


def dot_nt(a, b):
    return lax.dot_general(a, b, (((1,), (1,)), ((), ())), preferred_element_type=F32)


def mask(cond):
    return jnp.where(cond, 1.0, 0.0).astype(F32)


def normalize(rows):
    mean = jnp.mean(rows, axis=-1, keepdims=True)
    centered = rows - mean
    spread = jnp.mean(centered * centered, axis=-1, keepdims=True)
    return centered * lax.rsqrt(spread + EPS)


def fused(
    zs,
    xs,
    atom_single,
    atom_bias,
    atom_token,
    atom_count,
    token_single,
    pair,
    atom_qkv,
    atom_wo,
    atom_agg,
    token_qkvg,
    pair_weight,
    token_wo,
    atom_out,
    token_out,
    single_v,
    bias_v,
    name_v,
    count_v,
    tok_v,
    pair_v,
    aqkv_v,
    awo_v,
    agg_v,
    qkvg_v,
    two_v,
    kv_pad,
    weights,
    own,
    hold_up,
    hold_dn,
    opp_up_s,
    opp_dn_s,
    dir_up_s,
    dir_dn_s,
    fwd_up_s,
    fwd_dn_s,
    opp_up_r,
    opp_dn_r,
    dir_up_r,
    dir_dn_r,
    fwd_up_r,
    fwd_dn_r,
    sum_s,
    sum_r,
    kv_all,
    score,
    mixed,
    fin_s,
    fin_r,
    proj_v,
    out_v,
    in_sem,
    pair_sem,
    halo_s,
    halo_r,
    w_s,
    w_r,
    y_s,
    y_r,
    sum_ss,
    sum_rs,
    z_s,
    z_r,
    x_s,
    x_r,
    x2_s,
    x2_r,
    c_s,
    c_r,
    fin_ss,
    fin_rs,
    known,
):
    tok = lax.axis_index("tok")
    y = lax.axis_index("head")
    devs = zs * xs * CORES
    z = lax.div(tok, xs * CORES)
    x = lax.rem(lax.div(tok, CORES), xs)
    c = lax.rem(tok, CORES)
    place = lax.rem(tok, BLOCK_DEVS)
    groups, depth, keys = pair_v.shape
    half = keys // 2
    here = tok_v.shape[0]
    atoms = single_v.shape[0]
    windows = atoms // WQ
    columns = HL * HEAD_SIZE

    def tok_of(z_, x_, c_):
        return (z_ * xs + x_) * CORES + c_

    def y_at(k):
        return lax.rem(y + k, Y)

    def x_at(k):
        return lax.rem(x + k, xs)

    def mate(k):
        return tok - place + lax.rem(place + k, BLOCK_DEVS)

    up, dn = {"head": y_at(1)}, {"head": y_at(3)}

    def remote(src, dst, send, recv, device):
        return pltpu.make_async_remote_copy(
            src_ref=src,
            dst_ref=dst,
            send_sem=send,
            recv_sem=recv,
            device_id=device,
            device_id_type=MESH,
        )

    def signal(sem, device):
        pl.semaphore_signal(sem, inc=1, device_id=device, device_id_type=MESH)

    loads = [
        (pair_weight, weights.at[0]),
        (atom_single, single_v),
        (atom_qkv, aqkv_v),
        (atom_bias, bias_v),
        (atom_wo, awo_v),
        (atom_agg, agg_v),
        (atom_token, name_v),
        (atom_count, count_v),
        (token_qkvg, qkvg_v),
        (token_single, tok_v),
        (token_wo, two_v),
    ]
    loads = [pltpu.make_async_copy(a, b, in_sem.at[i]) for i, (a, b) in enumerate(loads)]

    def pair_load(g):
        return pltpu.make_async_copy(
            pair.at[pl.ds(pl.multiple_of(g * depth, depth), depth), :],
            pair_v.at[g],
            pair_sem.at[g],
        )

    loads[0].start()
    pair_load(0).start()
    loads[1].start()
    loads[2].start()
    for g in range(1, groups):
        pair_load(g).start()
    for load in loads[3:]:
        load.start()

    barrier = pltpu.get_barrier_semaphore()
    partners = [{"head": y_at(k)} for k in range(1, Y)]
    partners += [{"tok": mate(k)} for k in range(1, BLOCK_DEVS)]
    partners += [{"tok": tok_of(z, x_at(k), c)} for k in sorted({1, xs - 1})]
    partners += [{"tok": tok_of(z, x, 1 - c)}]
    for partner in partners:
        signal(barrier, partner)
    edges = [(tok > 0, tok - 1), (tok < devs - 1, tok + 1)]
    edges += [(z > 0, tok - xs * CORES), (z < zs - 1, tok + xs * CORES)]
    expected = len(partners)
    for present, other in edges:
        expected = expected + present.astype(jnp.int32)

        @pl.when(present)
        def _():
            signal(barrier, {"tok": other})

    loads[0].wait()
    wt = weights[0]
    heads = wt.shape[0]
    row = iota((Y * CHUNK, heads), 0)
    owner = lax.rem(y + lax.div(row, CHUNK), Y)
    pick = iota((Y * CHUNK, heads), 1) == owner * HL + lax.rem(lax.div(row, ROWS), HL)
    picked = dot(mask(pick).astype(BF16), wt).astype(BF16)
    spread = mask(iota((CH, depth), 0) == lax.rem(iota((CH, depth), 1), CH)).astype(BF16)
    diag = lax.div(iota((Y * CHUNK, depth), 1), CH) == lax.rem(iota((Y * CHUNK, depth), 0), ROWS)
    lhs = (dot(picked, spread) * mask(diag)).astype(BF16)
    picked_f = picked.astype(F32)
    mid = PAIR_MID * jnp.sum(picked_f, axis=1, keepdims=True)
    reach = jnp.maximum(PAIR_HALF * jnp.sum(jnp.abs(picked_f), axis=1, keepdims=True), 1e-20)
    inv = CODE_MAX / reach

    buffers = {
        OPP_UP: (opp_up_s, opp_up_r, up),
        OPP_DN: (opp_dn_s, opp_dn_r, dn),
        DIR_UP: (dir_up_s, dir_up_r, up),
        DIR_DN: (dir_dn_s, dir_dn_r, dn),
        FWD_UP: (fwd_up_s, fwd_up_r, up),
        FWD_DN: (fwd_dn_s, fwd_dn_r, dn),
    }

    def piece(kind, g):
        src, dst, device = buffers[kind]
        return remote(src.at[g], dst.at[g], y_s.at[kind, g], y_r.at[kind, g], device)

    sub = half // 3 if half % 3 == 0 and (half // 3) % LANES == 0 else half

    def coded(value, scale):
        return jnp.round(value * scale).astype(jnp.int32).astype(I16)

    def produce(g):
        pair_load(g).wait()
        for side in range(2):
            for at in range(0, half, sub):
                cols = slice(side * half + at, side * half + at + sub)
                into = slice(at, at + sub)
                part = dot(lhs, pair_v[g, :, cols])
                own[g, :, cols] = part[0:CHUNK]
                part = part[CHUNK:] - mid[CHUNK:]
                to_up, to_opp, to_dn = (part[i * CHUNK : (i + 1) * CHUNK] for i in range(3))
                i_up, i_opp, i_dn = (inv[i * CHUNK : (i + 1) * CHUNK] for i in range(1, Y))
                if side == 0:
                    opp_up_s[g, :, into] = coded(to_opp, i_opp)
                    hold_up[g, :, into] = to_up
                    dir_dn_s[g, :, into] = coded(to_dn, i_dn)
                else:
                    opp_dn_s[g, :, into] = coded(to_opp, i_opp)
                    hold_dn[g, :, into] = to_dn
                    dir_up_s[g, :, into] = coded(to_up, i_up)

    def send_out(g):
        for kind in (OPP_UP, OPP_DN, DIR_UP, DIR_DN):
            piece(kind, g).start()

    produce(0)

    pl.semaphore_wait(barrier, expected)
    send_out(0)
    w_copies = [
        remote(weights.at[0], weights.at[Y - k], w_s.at[k], w_r.at[Y - k], {"head": y_at(k)})
        for k in range(1, Y)
    ]
    for copy in w_copies:
        copy.start()

    rounds = [d for d in (1, 2, 4) if d < zs]

    def tell(r):
        for present, other in (
            (z >= rounds[r], tok - rounds[r] * xs * CORES),
            (z < zs - rounds[r], tok + rounds[r] * xs * CORES),
        ):

            @pl.when(present)
            def _():
                signal(known.at[r], {"tok": other})

    def learn(r):
        amount = (z >= rounds[r]).astype(jnp.int32) + (z < zs - rounds[r]).astype(jnp.int32)
        pl.semaphore_wait(known.at[r], amount)

    if len(rounds) > 0:
        tell(0)

    loads[1].wait()
    loads[2].wait()
    single = single_v[...].astype(F32)
    normed = normalize(single).astype(BF16)
    query = (dot(normed, aqkv_v[0]) * (1.0 / math.sqrt(ATOM_HEAD_SIZE))).astype(BF16)
    kv_pad[RIM : RIM + atoms, 0:LANES] = dot(normed, aqkv_v[1]).astype(BF16)
    kv_pad[RIM : RIM + atoms, LANES:] = dot(normed, aqkv_v[2]).astype(BF16)
    halo_up = remote(
        kv_pad.at[pl.ds(atoms, RIM), :],
        kv_pad.at[pl.ds(0, RIM), :],
        halo_s.at[0],
        halo_r.at[0],
        {"tok": lax.rem(tok + 1, devs)},
    )
    halo_dn = remote(
        kv_pad.at[pl.ds(RIM, RIM), :],
        kv_pad.at[pl.ds(atoms + RIM, RIM), :],
        halo_s.at[1],
        halo_r.at[1],
        {"tok": lax.rem(tok + devs - 1, devs)},
    )
    first, last = tok == 0, tok == devs - 1

    @pl.when(jnp.logical_not(last))
    def _():
        halo_up.start()

    @pl.when(jnp.logical_not(first))
    def _():
        halo_dn.start()

    def rest(g, carry):
        produce(g)
        send_out(g)
        return carry

    lax.fori_loop(1, groups, rest, 0)
    if len(rounds) > 1:
        learn(0)
        tell(1)

    @pl.when(first)
    def _():
        kv_pad[0:RIM, :] = jnp.zeros((RIM, 2 * LANES), BF16)

    @pl.when(jnp.logical_not(first))
    def _():
        halo_up.wait_recv()
        halo_dn.wait_send()

    @pl.when(last)
    def _():
        kv_pad[atoms + RIM : atoms + 2 * RIM, :] = jnp.zeros((RIM, 2 * LANES), BF16)

    @pl.when(jnp.logical_not(last))
    def _():
        halo_dn.wait_recv()
        halo_up.wait_send()

    loads[3].wait()
    wide = WQ * ATOM_HEADS
    grow = mask(lax.div(iota((wide, WQ), 0), ATOM_HEADS) == iota((wide, WQ), 1)).astype(BF16)
    fold = mask(iota((WQ, wide), 0) == lax.div(iota((WQ, wide), 1), ATOM_HEADS)).astype(BF16)
    in_head = mask(
        lax.div(iota((wide, LANES), 1), ATOM_HEAD_SIZE) == lax.rem(iota((wide, LANES), 0), ATOM_HEADS)
    )
    slot = iota((wide, WK), 1)
    scores = []
    for w in range(windows):
        q_rows = (dot(grow, query[w * WQ : (w + 1) * WQ]) * in_head).astype(BF16)
        s = dot_nt(q_rows, kv_pad[w * WQ : w * WQ + WK, 0:LANES])
        s = s + bias_v[w * wide : (w + 1) * wide, :].astype(F32)
        if w * WQ < RIM or w * WQ + WK > RIM + atoms:
            spot = tok * atoms + w * WQ - RIM + slot
            s = jnp.where((spot >= 0) & (spot < devs * atoms), s, -1e30)
        scores.append(s)
    probs = []
    for s in scores:
        e = jnp.exp(s - jnp.max(s, axis=-1, keepdims=True))
        probs.append((e * (1.0 / jnp.sum(e, axis=-1, keepdims=True))).astype(BF16))
    mixes = []
    for w in range(windows):
        m = dot(probs[w], kv_pad[w * WQ : w * WQ + WK, LANES:])
        mixes.append(dot(fold, (m * in_head).astype(BF16)).astype(BF16))
    mix = jnp.concatenate(mixes, axis=0)
    for load in loads[4:]:
        load.wait()
    a_out = (single + dot(mix, awo_v[...])).astype(BF16)
    atom_out[...] = a_out
    feat = jnp.maximum(dot(a_out, agg_v[...]), 0.0).astype(BF16)

    block = iota((BLOCK_DEVS * here, 1), 0)
    owner_tok = mate(lax.div(block, here)) * here + lax.rem(block, here)
    onehot = mask(owner_tok == name_v[...]).astype(BF16)
    sums = dot(onehot, feat)
    sum_copies = []
    for k in range(1, BLOCK_DEVS):
        sum_s[k] = sums[k * here : (k + 1) * here].astype(BF16)
        copy = remote(
            sum_s.at[k],
            sum_r.at[BLOCK_DEVS - k],
            sum_ss.at[k],
            sum_rs.at[BLOCK_DEVS - k],
            {"tok": mate(k)},
        )
        copy.start()
        sum_copies.append(copy)
    if len(rounds) > 2:
        learn(1)
        tell(2)

    def from_owner(value, k):
        shift = lax.rem((2 * Y - y - k) * columns, Y * columns)
        return pltpu.roll(value, shift, 1)[:, 0:LANES]

    for i in range(4):
        proj_v[:, i * LANES : (i + 1) * LANES] = from_owner(
            qkvg_v[:, i, :].astype(F32), 0
        ).astype(BF16)
    for k in range(Y):
        out_v[:, k * LANES : (k + 1) * LANES] = from_owner(two_v[...].astype(F32), k).astype(BF16)

    for copy in sum_copies:
        copy.wait()
    total = sums[0:here]
    for k in range(1, BLOCK_DEVS):
        total = total + sum_r[k].astype(F32)
    square = iota((here, here), 0) == iota((here, here), 1)
    count = jnp.sum(jnp.where(square, count_v[...].astype(F32), 0.0), axis=1, keepdims=True)
    token_mid = tok_v[...].astype(F32) + total / count
    normed_t = normalize(token_mid).astype(BF16)
    parts = dot(normed_t, proj_v[...])
    t_query = (parts[:, 0:LANES] * (1.0 / math.sqrt(HEAD_SIZE))).astype(BF16)
    kv_all[z, x, c] = parts[:, LANES : 3 * LANES].astype(BF16)
    gate = jax.nn.sigmoid(parts[:, 3 * LANES :])
    residual = from_owner(token_mid, 0)

    if rounds:
        learn(len(rounds) - 1)
    sent = []
    for k in range(1, zs):
        block_k = kv_all.at[z, x, c]
        copy = remote(
            block_k, block_k, z_s.at[k], z_r.at[k], {"tok": tok_of(lax.rem(z + k, zs), x, c)}
        )
        copy.start()
        sent.append(copy)

    for copy in w_copies:
        copy.wait()
    r32 = iota((CHUNK, heads), 0)

    def reach_of(sender, k):
        head = y_at(k) * HL + lax.div(r32, ROWS)
        sel = mask(iota((CHUNK, heads), 1) == head).astype(BF16)
        chosen = dot(sel, weights[sender])
        return jnp.maximum(PAIR_HALF * jnp.sum(jnp.abs(chosen), axis=1, keepdims=True), 1e-20)

    step = 1.0 / CODE_MAX
    legs = []
    for kind, out, hold, src, k, to in (
        (OPP_UP, fwd_up_s, hold_up, opp_up_r, 1, FWD_UP),
        (OPP_DN, fwd_dn_s, hold_dn, opp_dn_r, 3, FWD_DN),
    ):
        theirs = reach_of(Y - k, k)
        legs.append((kind, out, hold, src, to, theirs * step, CODE_MAX / (theirs + reach_of(0, k))))
    r_up, r_opp, r_dn = (reach_of(k, 0) for k in range(1, Y))
    s_up, s_dn = r_up * step, r_dn * step
    s_up2, s_dn2 = (r_up + r_opp) * step, (r_dn + r_opp) * step

    def forward(g, carry):
        for kind, out, hold, src, to, theirs, both in legs:
            piece(kind, g).wait_recv()
            out[g] = coded(src[g].astype(F32) * theirs + hold[g], both)
            piece(to, g).start()
        return carry

    lax.fori_loop(0, groups // 3, forward, 0)

    for k in range(1, zs):
        block_k = kv_all.at[lax.rem(z + zs - k, zs), x, c]
        remote(block_k, block_k, z_s.at[k], z_r.at[k], {"tok": tok}).wait_recv()

    def column(k):
        return kv_all.at[:, x_at(k), c]

    def send(ref, s_sem, r_sem, device):
        copy = remote(ref, ref, s_sem, r_sem, device)
        copy.start()
        sent.append(copy)

    x_up, x_dn = {"tok": tok_of(z, x_at(1), c)}, {"tok": tok_of(z, x_at(xs - 1), c)}
    other = {"tok": tok_of(z, x, 1 - c)}
    send(column(0), x_s.at[0], x_r.at[0], x_up)
    if xs > 2:
        send(column(0), x_s.at[1], x_r.at[1], x_dn)
    send(column(0), c_s.at[0], c_r.at[0], other)

    lax.fori_loop(groups // 3, groups * 2 // 3, forward, 0)

    def arrived(ref, sem):
        remote(ref, ref, x_s.at[0], sem, other).wait_recv()

    arrived(column(xs - 1), x_r.at[0])
    if xs > 2:
        lower, upper = pl.ds(0, zs // 2), pl.ds(zs // 2, zs - zs // 2)
        send(kv_all.at[lower, x_at(xs - 1), c], x2_s.at[0], x2_r.at[0], x_up)
        arrived(column(1), x_r.at[1])
        send(kv_all.at[upper, x_at(1), c], x2_s.at[1], x2_r.at[1], x_dn)
        send(column(1), c_s.at[1], c_r.at[1], other)
    send(column(xs - 1), c_s.at[2], c_r.at[2], other)

    lax.fori_loop(groups * 2 // 3, groups, forward, 0)

    if xs > 2:
        arrived(kv_all.at[lower, x_at(2), c], x2_r.at[0])
        arrived(kv_all.at[upper, x_at(2), c], x2_r.at[1])
        send(column(2), c_s.at[3], c_r.at[3], other)
    for k, sem in ((0, 0), (1, 1), (xs - 1, 2), (2, 3)) if xs > 2 else ((0, 0), (1, 2)):
        arrived(kv_all.at[:, x_at(k), 1 - c], c_r.at[sem])

    rows = groups * CHUNK
    rr = iota((rows, here), 0)
    pick_row = lax.div(rr, CHUNK) * ROWS + lax.rem(rr, ROWS) == iota((rows, here), 1)
    rl = iota((rows, LANES), 0)
    of_head = mask(
        lax.div(iota((rows, LANES), 1), HEAD_SIZE) == lax.rem(lax.div(rl, ROWS), HL)
    )
    q_rows = (dot(mask(pick_row).astype(BF16), t_query) * of_head).astype(BF16)
    key_rows = kv_all[..., 0:LANES].reshape(keys, LANES)
    for at in range(0, keys, 2 * sub):
        s = dot_nt(q_rows, key_rows[at : at + 2 * sub])
        score[:, :, at : at + 2 * sub] = s.reshape(groups, CHUNK, 2 * sub)

    def direct(g, carry):
        piece(DIR_UP, g).wait_recv()
        piece(DIR_DN, g).wait_recv()
        for side, (ref, scale) in enumerate(((dir_dn_r, s_up), (dir_up_r, s_dn))):
            for at in range(0, half, sub):
                cols = slice(side * half + at, side * half + at + sub)
                got = ref[g, :, at : at + sub].astype(F32) * scale
                score[g, :, cols] = score[g, :, cols] + (own[g, :, cols] + got)
        return carry

    lax.fori_loop(0, groups, direct, 0)

    head_mask = of_head[0:CHUNK]

    def attend(g, carry):
        piece(FWD_UP, g).wait_recv()
        piece(FWD_DN, g).wait_recv()
        peak = None
        for side, (ref, scale) in enumerate(((fwd_up_r, s_dn2), (fwd_dn_r, s_up2))):
            for at in range(0, half, sub):
                cols = slice(side * half + at, side * half + at + sub)
                s = score[g, :, cols] + ref[g, :, at : at + sub].astype(F32) * scale
                score[g, :, cols] = s
                high = jnp.max(s, axis=-1, keepdims=True)
                peak = high if peak is None else jnp.maximum(peak, high)
        norm = jnp.zeros((CHUNK, 1), F32)
        acc = jnp.zeros((CHUNK, LANES), F32)
        value_rows = kv_all[..., LANES:].reshape(keys, LANES)
        for at in range(0, keys, sub):
            e = jnp.exp(score[g, :, at : at + sub] - peak)
            norm = norm + jnp.sum(e, axis=-1, keepdims=True)
            acc = acc + dot(e.astype(BF16), value_rows[at : at + sub])
        acc = acc * head_mask / norm
        mixed[g] = jnp.sum(acc.reshape(HL, ROWS, LANES), axis=0)
        return carry

    lax.fori_loop(0, groups, attend, 0)

    out_rows = (mixed[...].reshape(here, LANES) * gate).astype(BF16)
    term = dot(out_rows[:, 0:columns], out_v[...])
    fin_copies = []
    for k in range(1, Y):
        fin_s[k] = term[:, k * LANES : (k + 1) * LANES].astype(BF16)
        copy = remote(
            fin_s.at[k], fin_r.at[Y - k], fin_ss.at[k], fin_rs.at[Y - k], {"head": y_at(k)}
        )
        copy.start()
        fin_copies.append(copy)

    def drain(g, carry):
        for kind in range(6):
            piece(kind, g).wait_send()
        return carry

    lax.fori_loop(0, groups, drain, 0)
    for copy in sent:
        copy.wait_send()
    result = residual + term[:, 0:LANES]
    for copy in fin_copies:
        copy.wait()
    for k in range(1, Y):
        result = result + fin_r[k].astype(F32)
    token_out[...] = result[:, 0:columns].astype(BF16)


def per_device(
    atom_single,
    atom_bias,
    atom_token,
    atom_count,
    token_single,
    pair,
    atom_qkv,
    atom_wo,
    atom_agg,
    token_qkvg,
    pair_weight,
    token_wo,
):
    devs = lax.axis_size("tok")
    xs = 4 if devs % 32 == 0 else 2
    zs = devs // (xs * CORES)
    atoms, width = atom_single.shape
    here, width_t = token_single.shape
    keys = pair.shape[2]
    groups = here // ROWS
    half = keys // 2
    columns = width_t // Y
    depth = ROWS * CH
    anywhere = pl.BlockSpec(memory_space=pl.ANY)
    vmem = pl.BlockSpec(memory_space=pltpu.VMEM)
    dma = pltpu.SemaphoreType.DMA
    code = pltpu.VMEM((groups, CHUNK, half), I16)
    operands = (
        atom_single,
        atom_bias.reshape(atoms * ATOM_HEADS, WK),
        atom_token.reshape(1, atoms),
        atom_count.reshape(1, here),
        token_single,
        pair.reshape(here * CH, keys),
        jnp.transpose(atom_qkv, (1, 0, 2)),
        atom_wo,
        atom_agg,
        token_qkvg,
        jnp.transpose(pair_weight),
        token_wo,
    )
    scratch = [
        pltpu.VMEM((atoms, width), BF16),
        pltpu.VMEM((atoms * ATOM_HEADS, WK), BF16),
        pltpu.VMEM((1, atoms), jnp.int32),
        pltpu.VMEM((1, here), jnp.int32),
        pltpu.VMEM((here, width_t), BF16),
        pltpu.VMEM((groups, depth, keys), BF16),
        pltpu.VMEM((3, width, width), BF16),
        pltpu.VMEM(atom_wo.shape, BF16),
        pltpu.VMEM(atom_agg.shape, BF16),
        pltpu.VMEM(token_qkvg.shape, BF16),
        pltpu.VMEM(token_wo.shape, BF16),
        pltpu.VMEM((atoms + 2 * RIM, 2 * width), BF16),
        pltpu.VMEM((Y, Y * HL, CH), BF16),
        pltpu.VMEM((groups, CHUNK, keys), F32),
        pltpu.VMEM((groups, CHUNK, half), F32),
        pltpu.VMEM((groups, CHUNK, half), F32),
        *([code] * 12),
        pltpu.VMEM((BLOCK_DEVS, here, width_t), BF16),
        pltpu.VMEM((BLOCK_DEVS, here, width_t), BF16),
        pltpu.VMEM((zs, xs, CORES, here, 2 * LANES), BF16),
        pltpu.VMEM((groups, CHUNK, keys), F32),
        pltpu.VMEM((groups, ROWS, LANES), F32),
        pltpu.VMEM((Y, here, LANES), BF16),
        pltpu.VMEM((Y, here, LANES), BF16),
        pltpu.VMEM((width_t, 4 * LANES), BF16),
        pltpu.VMEM((columns, Y * LANES), BF16),
        dma((11,)),
        dma((groups,)),
        dma((2,)),
        dma((2,)),
        dma((Y,)),
        dma((Y,)),
        dma((6, groups)),
        dma((6, groups)),
        dma((BLOCK_DEVS,)),
        dma((BLOCK_DEVS,)),
        dma((max(zs, 2),)),
        dma((max(zs, 2),)),
        *([dma((2,))] * 4),
        dma((4,)),
        dma((4,)),
        dma((Y,)),
        dma((Y,)),
        pltpu.SemaphoreType.REGULAR((3,)),
    ]
    outs = (
        pltpu.VMEM((atoms, width), BF16),
        pltpu.VMEM((here, columns), BF16),
    )
    return pl.pallas_call(
        functools.partial(fused, zs, xs),
        out_shape=outs,
        in_specs=[anywhere] * len(operands),
        out_specs=(vmem, vmem),
        scratch_shapes=scratch,
        compiler_params=pltpu.CompilerParams(
            collective_id=0, has_side_effects=True, vmem_limit_bytes=56 * 2**20
        ),
    )(*operands)


def solution(mesh):
    in_specs = (
        P("tok", None),
        P("tok", None, None),
        P("tok"),
        P("tok"),
        P("tok", None),
        P("tok", "head", None),
        P(),
        P(),
        P(),
        P(),
        P("head", None),
        P("head", None),
    )
    out_specs = (P("tok", None), P("tok", "head"))
    return jax.shard_map(
        per_device, mesh=mesh, in_specs=in_specs, out_specs=out_specs, check_vma=False
    )
```

```python
import functools
import math

import jax
import jax.numpy as jnp
from jax import lax
from jax.experimental import pallas as pl
from jax.experimental.pallas import tpu as pltpu
from jax.sharding import PartitionSpec as P

ATOM_HEADS = 4
WQ = 32
WK = 128
RIM = (WK - WQ) // 2
BLOCK_DEVS = 4
HEAD_SIZE = 24
ATOM_HEAD_SIZE = 32
EPS = 1e-05

Y = 4
CORES = 2
ROWS = 8
CH = 32
HL = 4
CHUNK = HL * ROWS
LANES = 128

PAIR_MID = 9.5
PAIR_HALF = 14.5
CODE_MAX = 32700.0

F32 = jnp.float32
BF16 = jnp.bfloat16
I16 = jnp.int16
MESH = pl.DeviceIdType.MESH

OPP_UP, OPP_DN, DIR_UP, DIR_DN, FWD_UP, FWD_DN = range(6)


def iota(shape, dim):
    return lax.broadcasted_iota(jnp.int32, shape, dim)


def dot(a, b):
    return jnp.dot(a, b, preferred_element_type=F32)


def dot_nt(a, b):
    return lax.dot_general(a, b, (((1,), (1,)), ((), ())), preferred_element_type=F32)


def mask(cond):
    return jnp.where(cond, 1.0, 0.0).astype(F32)


def normalize(rows):
    mean = jnp.mean(rows, axis=-1, keepdims=True)
    centered = rows - mean
    spread = jnp.mean(centered * centered, axis=-1, keepdims=True)
    return centered * lax.rsqrt(spread + EPS)


def fused(
    zs,
    xs,
    atom_single,
    atom_bias,
    atom_token,
    atom_count,
    token_single,
    pair,
    atom_qkv,
    atom_wo,
    atom_agg,
    token_qkvg,
    pair_weight,
    token_wo,
    atom_out,
    token_out,
    single_v,
    bias_v,
    name_v,
    count_v,
    tok_v,
    pair_v,
    aqkv_v,
    awo_v,
    agg_v,
    qkvg_v,
    two_v,
    kv_pad,
    weights,
    own,
    hold_up,
    hold_dn,
    opp_up_s,
    opp_dn_s,
    dir_up_s,
    dir_dn_s,
    fwd_up_s,
    fwd_dn_s,
    opp_up_r,
    opp_dn_r,
    dir_up_r,
    dir_dn_r,
    fwd_up_r,
    fwd_dn_r,
    sum_s,
    sum_r,
    kv_all,
    score,
    mixed,
    fin_s,
    fin_r,
    proj_v,
    out_v,
    in_sem,
    pair_sem,
    halo_s,
    halo_r,
    w_s,
    w_r,
    y_s,
    opp_r,
    dir_r,
    fwd_r,
    sum_ss,
    sum_rs,
    z_s,
    z_r,
    x_s,
    x_r,
    c_s,
    c_r,
    fin_ss,
    fin_rs,
    known,
    near,
):
    tok = lax.axis_index("tok")
    y = lax.axis_index("head")
    devs = zs * xs * CORES
    z = lax.div(tok, xs * CORES)
    x = lax.rem(lax.div(tok, CORES), xs)
    c = lax.rem(tok, CORES)
    place = lax.rem(tok, BLOCK_DEVS)
    groups, depth, keys = pair_v.shape
    half = keys // 2
    here = tok_v.shape[0]
    atoms = single_v.shape[0]
    windows = atoms // WQ
    columns = HL * HEAD_SIZE
    paired = groups // 2

    def tok_of(z_, x_, c_):
        return (z_ * xs + x_) * CORES + c_

    def y_at(k):
        return lax.rem(y + k, Y)

    def x_at(k):
        return lax.rem(x + k, xs)

    def mate(k):
        return tok - place + lax.rem(place + k, BLOCK_DEVS)

    up, dn = {"head": y_at(1)}, {"head": y_at(3)}

    def remote(src, dst, send, recv, device):
        return pltpu.make_async_remote_copy(
            src_ref=src,
            dst_ref=dst,
            send_sem=send,
            recv_sem=recv,
            device_id=device,
            device_id_type=MESH,
        )

    def signal(sem, device):
        pl.semaphore_signal(sem, inc=1, device_id=device, device_id_type=MESH)

    barrier = pltpu.get_barrier_semaphore()
    for k in range(1, Y):
        signal(barrier, {"head": y_at(k)})

    loads = [
        (pair_weight, weights.at[0]),
        (atom_single, single_v),
        (atom_qkv, aqkv_v),
        (atom_bias, bias_v),
        (atom_wo, awo_v),
        (atom_agg, agg_v),
        (atom_token, name_v),
        (atom_count, count_v),
        (token_qkvg, qkvg_v),
        (token_single, tok_v),
        (token_wo, two_v),
    ]
    loads = [pltpu.make_async_copy(a, b, in_sem.at[i]) for i, (a, b) in enumerate(loads)]

    def pair_load(g):
        return pltpu.make_async_copy(
            pair.at[pl.ds(pl.multiple_of(g * depth, depth), depth), :],
            pair_v.at[g],
            pair_sem.at[g],
        )

    head_loads = [
        pltpu.make_async_copy(
            pair.at[pl.ds(0, depth), pl.ds(side * half, half)],
            pair_v.at[0, :, pl.ds(side * half, half)],
            pair_sem.at[side * groups],
        )
        for side in range(2)
    ]
    loads[0].start()
    for load in head_loads:
        load.start()
    loads[1].start()
    loads[2].start()
    for g in range(1, groups):
        pair_load(g).start()
    for load in loads[3:]:
        load.start()

    first_core = c == 0
    edges = []
    for k in range(1, BLOCK_DEVS):
        same = lax.div(place, CORES) == lax.div(lax.rem(place + k, BLOCK_DEVS), CORES)
        edges.append((None, jnp.where(same, first_core, place + k >= BLOCK_DEVS), mate(k)))
    for k in sorted({1, xs - 1}):
        edges.append((None, x + k >= xs, tok_of(z, x_at(k), c)))
    edges.append((None, first_core, tok_of(z, x, 1 - c)))
    edges.append((tok > 0, first_core, tok - 1))
    edges.append((tok < devs - 1, first_core, tok + 1))
    edges.append((z > 0, True, tok - xs * CORES))
    edges.append((z < zs - 1, False, tok + xs * CORES))

    def both(a, b):
        return b if a is None else a if b is True else jnp.logical_and(a, b)

    waited, waiting, expected, back = [], [], Y - 1, 0
    for there, waits, other in edges:
        if waits is not False:
            waited.append((both(there, waits), other))
            expected = expected + waited[-1][0].astype(jnp.int32)
        if waits is not True:
            waiting.append((both(there, True if waits is False else jnp.logical_not(waits)), other))
            back = back + waiting[-1][0].astype(jnp.int32)

    def signal_all(sem, group):
        for there, other in group:

            @pl.when(there)
            def _():
                signal(sem, {"tok": other})

    signal_all(barrier, waiting)

    loads[0].wait()
    wt = weights[0]
    heads = wt.shape[0]
    row = iota((Y * CHUNK, heads), 0)
    owner = lax.rem(y + lax.div(row, CHUNK), Y)
    pick = iota((Y * CHUNK, heads), 1) == owner * HL + lax.rem(lax.div(row, ROWS), HL)
    picked = dot(mask(pick).astype(BF16), wt).astype(BF16)
    spread = mask(iota((CH, depth), 0) == lax.rem(iota((CH, depth), 1), CH)).astype(BF16)
    diag = lax.div(iota((Y * CHUNK, depth), 1), CH) == lax.rem(iota((Y * CHUNK, depth), 0), ROWS)
    lhs = (dot(picked, spread) * mask(diag)).astype(BF16)
    picked_f = picked.astype(F32)
    mid = PAIR_MID * jnp.sum(picked_f, axis=1, keepdims=True)
    reach = jnp.maximum(PAIR_HALF * jnp.sum(jnp.abs(picked_f), axis=1, keepdims=True), 1e-20)
    inv = CODE_MAX / reach

    buffers = {
        OPP_UP: (opp_up_s, opp_up_r, up),
        OPP_DN: (opp_dn_s, opp_dn_r, dn),
        DIR_UP: (dir_up_s, dir_up_r, up),
        DIR_DN: (dir_dn_s, dir_dn_r, dn),
        FWD_UP: (fwd_up_s, fwd_up_r, up),
        FWD_DN: (fwd_dn_s, fwd_dn_r, dn),
    }

    def landed(kind, g):
        if kind in (OPP_UP, OPP_DN):
            return opp_r.at[kind - OPP_UP, lax.div(g, 2)]
        if kind in (DIR_UP, DIR_DN):
            return dir_r.at[kind - DIR_UP]
        return fwd_r.at[kind - FWD_UP, jnp.maximum(lax.div(g, 2), g - (groups - 1) + paired)]

    def piece(kind, g):
        src, dst, device = buffers[kind]
        return remote(src.at[g], dst.at[g], y_s.at[kind], landed(kind, g), device)

    def pieces(kind, g, n):
        src, dst, device = buffers[kind]
        some = pl.ds(g, n)
        return remote(src.at[some], dst.at[some], y_s.at[kind], landed(kind, g), device)

    sub = half // 3 if half % 3 == 0 and (half // 3) % LANES == 0 else half

    def coded(value, scale):
        return jnp.round(value * scale).astype(jnp.int32).astype(I16)

    def produce(g, sides):
        for side in sides:
            for at in range(0, half, sub):
                cols = slice(side * half + at, side * half + at + sub)
                into = slice(at, at + sub)
                part = dot(lhs, pair_v[g, :, cols])
                own[g, :, cols] = part[0:CHUNK]
                part = part[CHUNK:] - mid[CHUNK:]
                to_up, to_opp, to_dn = (part[i * CHUNK : (i + 1) * CHUNK] for i in range(3))
                i_up, i_opp, i_dn = (inv[i * CHUNK : (i + 1) * CHUNK] for i in range(1, Y))
                if side == 0:
                    opp_up_s[g, :, into] = coded(to_opp, i_opp)
                    hold_up[g, :, into] = to_up
                    dir_dn_s[g, :, into] = coded(to_dn, i_dn)
                else:
                    opp_dn_s[g, :, into] = coded(to_opp, i_opp)
                    hold_dn[g, :, into] = to_dn
                    dir_up_s[g, :, into] = coded(to_up, i_up)

    head_loads[0].wait()
    produce(0, (0,))

    pl.semaphore_wait(barrier, expected)
    piece(OPP_UP, 0).start()
    piece(DIR_DN, 0).start()
    head_loads[1].wait()
    produce(0, (1,))
    piece(OPP_DN, 0).start()
    piece(DIR_UP, 0).start()
    for k in range(1, Y):
        remote(weights.at[0], weights.at[Y - k], w_s, w_r, {"head": y_at(k)}).start()
    signal_all(near, waited)

    rounds = [d for d in (1, 2, 4) if d < zs]

    def tell(r):
        for present, other in (
            (z >= rounds[r], tok - rounds[r] * xs * CORES),
            (z < zs - rounds[r], tok + rounds[r] * xs * CORES),
        ):

            @pl.when(present)
            def _():
                signal(known.at[r], {"tok": other})

    def learn(r):
        amount = (z >= rounds[r]).astype(jnp.int32) + (z < zs - rounds[r]).astype(jnp.int32)
        pl.semaphore_wait(known.at[r], amount)

    loads[1].wait()
    loads[2].wait()
    single = single_v[...].astype(F32)
    normed = normalize(single).astype(BF16)
    query = (dot(normed, aqkv_v[0]) * (1.0 / math.sqrt(ATOM_HEAD_SIZE))).astype(BF16)
    kv_pad[RIM : RIM + atoms, 0:LANES] = dot(normed, aqkv_v[1]).astype(BF16)
    kv_pad[RIM : RIM + atoms, LANES:] = dot(normed, aqkv_v[2]).astype(BF16)
    halo_up = remote(
        kv_pad.at[pl.ds(atoms, RIM), :],
        kv_pad.at[pl.ds(0, RIM), :],
        halo_s.at[0],
        halo_r.at[0],
        {"tok": lax.rem(tok + 1, devs)},
    )
    halo_dn = remote(
        kv_pad.at[pl.ds(RIM, RIM), :],
        kv_pad.at[pl.ds(atoms + RIM, RIM), :],
        halo_s.at[1],
        halo_r.at[1],
        {"tok": lax.rem(tok + devs - 1, devs)},
    )

    def rest(g, carry):
        pair_load(g).wait()
        produce(g, (0, 1))
        for kind in (OPP_UP, OPP_DN, DIR_UP, DIR_DN):
            piece(kind, g).start()
        return carry

    lax.fori_loop(1, groups, rest, 0)

    @pl.when(back > 0)
    def _():
        pl.semaphore_wait(near, back)

    if len(rounds) > 0:
        tell(0)
    first, last = tok == 0, tok == devs - 1

    @pl.when(jnp.logical_not(last))
    def _():
        halo_up.start()

    @pl.when(jnp.logical_not(first))
    def _():
        halo_dn.start()

    def from_owner(value, k):
        shift = lax.rem((2 * Y - y - k) * columns, Y * columns)
        return pltpu.roll(value, shift, 1)[:, 0:LANES]

    for load in loads[4:]:
        load.wait()
    for i in range(4):
        proj_v[:, i * LANES : (i + 1) * LANES] = from_owner(
            qkvg_v[:, i, :].astype(F32), 0
        ).astype(BF16)
    for k in range(Y):
        out_v[:, k * LANES : (k + 1) * LANES] = from_owner(two_v[...].astype(F32), k).astype(BF16)
    if len(rounds) > 1:
        learn(0)
        tell(1)

    @pl.when(first)
    def _():
        kv_pad[0:RIM, :] = jnp.zeros((RIM, 2 * LANES), BF16)

    @pl.when(jnp.logical_not(first))
    def _():
        halo_up.wait_recv()
        halo_dn.wait_send()

    @pl.when(last)
    def _():
        kv_pad[atoms + RIM : atoms + 2 * RIM, :] = jnp.zeros((RIM, 2 * LANES), BF16)

    @pl.when(jnp.logical_not(last))
    def _():
        halo_dn.wait_recv()
        halo_up.wait_send()

    loads[3].wait()
    wide = WQ * ATOM_HEADS
    grow = mask(lax.div(iota((wide, WQ), 0), ATOM_HEADS) == iota((wide, WQ), 1)).astype(BF16)
    fold = mask(iota((WQ, wide), 0) == lax.div(iota((WQ, wide), 1), ATOM_HEADS)).astype(BF16)
    in_head = mask(
        lax.div(iota((wide, LANES), 1), ATOM_HEAD_SIZE) == lax.rem(iota((wide, LANES), 0), ATOM_HEADS)
    )
    slot = iota((wide, WK), 1)
    scores = []
    for w in range(windows):
        q_rows = (dot(grow, query[w * WQ : (w + 1) * WQ]) * in_head).astype(BF16)
        s = dot_nt(q_rows, kv_pad[w * WQ : w * WQ + WK, 0:LANES])
        s = s + bias_v[w * wide : (w + 1) * wide, :].astype(F32)
        if w * WQ < RIM or w * WQ + WK > RIM + atoms:
            spot = tok * atoms + w * WQ - RIM + slot
            s = jnp.where((spot >= 0) & (spot < devs * atoms), s, -1e30)
        scores.append(s)
    probs = []
    for s in scores:
        e = jnp.exp(s - jnp.max(s, axis=-1, keepdims=True))
        probs.append((e * (1.0 / jnp.sum(e, axis=-1, keepdims=True))).astype(BF16))
    mixes = []
    for w in range(windows):
        m = dot(probs[w], kv_pad[w * WQ : w * WQ + WK, LANES:])
        mixes.append(dot(fold, (m * in_head).astype(BF16)).astype(BF16))
    mix = jnp.concatenate(mixes, axis=0)
    a_out = (single + dot(mix, awo_v[...])).astype(BF16)
    atom_out[...] = a_out
    feat = jnp.maximum(dot(a_out, agg_v[...]), 0.0).astype(BF16)

    block = iota((BLOCK_DEVS * here, 1), 0)
    owner_tok = mate(lax.div(block, here)) * here + lax.rem(block, here)
    onehot = mask(owner_tok == name_v[...]).astype(BF16)
    sums = dot(onehot, feat)
    for k in range(1, BLOCK_DEVS):
        sum_s[k] = sums[k * here : (k + 1) * here].astype(BF16)
        remote(
            sum_s.at[k], sum_r.at[BLOCK_DEVS - k], sum_ss, sum_rs, {"tok": mate(k)}
        ).start()
    if len(rounds) > 2:
        learn(1)
        tell(2)

    others = pl.ds(1, BLOCK_DEVS - 1)
    remote(sum_s.at[others], sum_r.at[others], sum_ss, sum_rs, up).wait()
    total = sums[0:here]
    for k in range(1, BLOCK_DEVS):
        total = total + sum_r[k].astype(F32)
    square = iota((here, here), 0) == iota((here, here), 1)
    count = jnp.sum(jnp.where(square, count_v[...].astype(F32), 0.0), axis=1, keepdims=True)
    token_mid = tok_v[...].astype(F32) + total / count
    normed_t = normalize(token_mid).astype(BF16)
    parts = dot(normed_t, proj_v[...])
    t_query = (parts[:, 0:LANES] * (1.0 / math.sqrt(HEAD_SIZE))).astype(BF16)
    kv_all[z, x, c] = parts[:, LANES : 3 * LANES].astype(BF16)
    gate = jax.nn.sigmoid(parts[:, 3 * LANES :])
    residual = from_owner(token_mid, 0)

    if rounds:
        learn(len(rounds) - 1)
    sent = []
    for k in range(1, zs):
        block_k = kv_all.at[z, x, c]
        copy = remote(
            block_k, block_k, z_s.at[k], z_r.at[k], {"tok": tok_of(lax.rem(z + k, zs), x, c)}
        )
        copy.start()
        sent.append(copy)

    peers = pl.ds(1, Y - 1)
    remote(weights.at[peers], weights.at[peers], w_s, w_r, up).wait()
    r32 = iota((CHUNK, heads), 0)

    def reach_of(sender, k):
        head = y_at(k) * HL + lax.div(r32, ROWS)
        sel = mask(iota((CHUNK, heads), 1) == head).astype(BF16)
        chosen = dot(sel, weights[sender])
        return jnp.maximum(PAIR_HALF * jnp.sum(jnp.abs(chosen), axis=1, keepdims=True), 1e-20)

    step = 1.0 / CODE_MAX
    legs = []
    for kind, out, hold, src, k, to in (
        (OPP_UP, fwd_up_s, hold_up, opp_up_r, 1, FWD_UP),
        (OPP_DN, fwd_dn_s, hold_dn, opp_dn_r, 3, FWD_DN),
    ):
        theirs = reach_of(Y - k, k)
        legs.append((kind, out, hold, src, to, theirs * step, CODE_MAX / (theirs + reach_of(0, k))))
    r_up, r_opp, r_dn = (reach_of(k, 0) for k in range(1, Y))
    s_up, s_dn = r_up * step, r_dn * step
    s_up2, s_dn2 = (r_up + r_opp) * step, (r_dn + r_opp) * step

    def forward(pair_of, carry):
        for kind, out, hold, src, to, theirs, scale in legs:
            pieces(kind, 2 * pair_of, 2).wait_recv()
            for i in range(2):
                g = 2 * pair_of + i
                out[g] = coded(src[g].astype(F32) * theirs + hold[g], scale)
                piece(to, g).start()
        return carry

    lax.fori_loop(0, groups // 6, forward, 0)

    for k in range(1, zs):
        block_k = kv_all.at[lax.rem(z + zs - k, zs), x, c]
        remote(block_k, block_k, z_s.at[k], z_r.at[k], {"tok": tok}).wait_recv()

    def column(k):
        return kv_all.at[:, x_at(k), c]

    def send(ref, s_sem, r_sem, device):
        copy = remote(ref, ref, s_sem, r_sem, device)
        copy.start()
        return copy

    x_up, x_dn = {"tok": tok_of(z, x_at(1), c)}, {"tok": tok_of(z, x_at(xs - 1), c)}
    other = {"tok": tok_of(z, x, 1 - c)}
    sent.append(send(column(0), x_s.at[0], x_r.at[0], x_up))
    if xs > 2:
        sent.append(send(column(0), x_s.at[1], x_r.at[1], x_dn))
    send(column(0), c_s, c_r, other)

    lax.fori_loop(groups // 6, groups // 3, forward, 0)

    def arrived(ref, sem):
        remote(ref, ref, x_s.at[0], sem, other).wait_recv()

    arrived(column(xs - 1), x_r.at[0])
    if xs > 2:
        lower, upper = pl.ds(0, zs // 2), pl.ds(zs // 2, zs - zs // 2)
        sent.append(send(kv_all.at[lower, x_at(xs - 1), c], x_s.at[2], x_r.at[2], x_up))
        arrived(column(1), x_r.at[1])
        sent.append(send(kv_all.at[upper, x_at(1), c], x_s.at[3], x_r.at[2], x_dn))
        send(column(1), c_s, c_r, other)
    send(column(xs - 1), c_s, c_r, other)

    lax.fori_loop(groups // 3, groups // 2, forward, 0)

    if xs > 2:
        arrived(column(2), x_r.at[2])
        send(column(2), c_s, c_r, other)
    arrived(kv_all.at[:, :, 1 - c], c_r)

    rows = groups * CHUNK
    rr = iota((rows, here), 0)
    pick_row = lax.div(rr, CHUNK) * ROWS + lax.rem(rr, ROWS) == iota((rows, here), 1)
    rl = iota((rows, LANES), 0)
    of_head = mask(
        lax.div(iota((rows, LANES), 1), HEAD_SIZE) == lax.rem(lax.div(rl, ROWS), HL)
    )
    q_rows = (dot(mask(pick_row).astype(BF16), t_query) * of_head).astype(BF16)
    key_rows = kv_all[..., 0:LANES].reshape(keys, LANES)
    for at in range(0, keys, 2 * sub):
        s = dot_nt(q_rows, key_rows[at : at + 2 * sub])
        score[:, :, at : at + 2 * sub] = s.reshape(groups, CHUNK, 2 * sub)

    for kind in (DIR_UP, DIR_DN):
        pieces(kind, 0, groups).wait_recv()

    def direct(g, carry):
        for side, (ref, scale) in enumerate(((dir_dn_r, s_up), (dir_up_r, s_dn))):
            for at in range(0, half, sub):
                cols = slice(side * half + at, side * half + at + sub)
                got = ref[g, :, at : at + sub].astype(F32) * scale
                score[g, :, cols] = score[g, :, cols] + (own[g, :, cols] + got)
        return carry

    lax.fori_loop(0, groups, direct, 0)

    head_mask = of_head[0:CHUNK]

    def attend(g, carry):
        peak = None
        for side, (ref, scale) in enumerate(((fwd_up_r, s_dn2), (fwd_dn_r, s_up2))):
            for at in range(0, half, sub):
                cols = slice(side * half + at, side * half + at + sub)
                s = score[g, :, cols] + ref[g, :, at : at + sub].astype(F32) * scale
                score[g, :, cols] = s
                high = jnp.max(s, axis=-1, keepdims=True)
                peak = high if peak is None else jnp.maximum(peak, high)
        norm = jnp.zeros((CHUNK, 1), F32)
        acc = jnp.zeros((CHUNK, LANES), F32)
        value_rows = kv_all[..., LANES:].reshape(keys, LANES)
        for at in range(0, keys, sub):
            e = jnp.exp(score[g, :, at : at + sub] - peak)
            norm = norm + jnp.sum(e, axis=-1, keepdims=True)
            acc = acc + dot(e.astype(BF16), value_rows[at : at + sub])
        acc = acc * head_mask / norm
        mixed[g] = jnp.sum(acc.reshape(HL, ROWS, LANES), axis=0)
        return carry

    for g in range(0, groups - 2, 2):
        for kind in (FWD_UP, FWD_DN):
            pieces(kind, g, 2).wait_recv()
        lax.fori_loop(g, g + 2, attend, 0)
    for g in (groups - 2, groups - 1):
        for kind in (FWD_UP, FWD_DN):
            piece(kind, g).wait_recv()
        lax.fori_loop(g, g + 1, attend, 0)

    out_rows = (mixed[...].reshape(here, LANES) * gate).astype(BF16)
    term = dot(out_rows[:, 0:columns], out_v[...])
    for k in range(1, Y):
        fin_s[k] = term[:, k * LANES : (k + 1) * LANES].astype(BF16)
        remote(fin_s.at[k], fin_r.at[Y - k], fin_ss, fin_rs, {"head": y_at(k)}).start()
    for kind in range(6):
        pieces(kind, 0, groups).wait_send()
    for copy in sent:
        copy.wait_send()
    remote(kv_all.at[:, :, c], kv_all.at[:, :, c], c_s, c_r, other).wait_send()
    result = residual + term[:, 0:LANES]
    remote(fin_s.at[peers], fin_r.at[peers], fin_ss, fin_rs, up).wait()
    for k in range(1, Y):
        result = result + fin_r[k].astype(F32)
    token_out[...] = result[:, 0:columns].astype(BF16)


def per_device(
    atom_single,
    atom_bias,
    atom_token,
    atom_count,
    token_single,
    pair,
    atom_qkv,
    atom_wo,
    atom_agg,
    token_qkvg,
    pair_weight,
    token_wo,
):
    devs = lax.axis_size("tok")
    xs = 4 if devs % 32 == 0 else 2
    zs = devs // (xs * CORES)
    atoms, width = atom_single.shape
    here, width_t = token_single.shape
    keys = pair.shape[2]
    groups = here // ROWS
    half = keys // 2
    columns = width_t // Y
    depth = ROWS * CH
    anywhere = pl.BlockSpec(memory_space=pl.ANY)
    vmem = pl.BlockSpec(memory_space=pltpu.VMEM)
    dma = pltpu.SemaphoreType.DMA
    code = pltpu.VMEM((groups, CHUNK, half), I16)
    operands = (
        atom_single,
        atom_bias.reshape(atoms * ATOM_HEADS, WK),
        atom_token.reshape(1, atoms),
        atom_count.reshape(1, here),
        token_single,
        pair.reshape(here * CH, keys),
        jnp.transpose(atom_qkv, (1, 0, 2)),
        atom_wo,
        atom_agg,
        token_qkvg,
        jnp.transpose(pair_weight),
        token_wo,
    )
    scratch = [
        pltpu.VMEM((atoms, width), BF16),
        pltpu.VMEM((atoms * ATOM_HEADS, WK), BF16),
        pltpu.VMEM((1, atoms), jnp.int32),
        pltpu.VMEM((1, here), jnp.int32),
        pltpu.VMEM((here, width_t), BF16),
        pltpu.VMEM((groups, depth, keys), BF16),
        pltpu.VMEM((3, width, width), BF16),
        pltpu.VMEM(atom_wo.shape, BF16),
        pltpu.VMEM(atom_agg.shape, BF16),
        pltpu.VMEM(token_qkvg.shape, BF16),
        pltpu.VMEM(token_wo.shape, BF16),
        pltpu.VMEM((atoms + 2 * RIM, 2 * width), BF16),
        pltpu.VMEM((Y, Y * HL, CH), BF16),
        pltpu.VMEM((groups, CHUNK, keys), F32),
        pltpu.VMEM((groups, CHUNK, half), F32),
        pltpu.VMEM((groups, CHUNK, half), F32),
        *([code] * 12),
        pltpu.VMEM((BLOCK_DEVS, here, width_t), BF16),
        pltpu.VMEM((BLOCK_DEVS, here, width_t), BF16),
        pltpu.VMEM((zs, xs, CORES, here, 2 * LANES), BF16),
        pltpu.VMEM((groups, CHUNK, keys), F32),
        pltpu.VMEM((groups, ROWS, LANES), F32),
        pltpu.VMEM((Y, here, LANES), BF16),
        pltpu.VMEM((Y, here, LANES), BF16),
        pltpu.VMEM((width_t, 4 * LANES), BF16),
        pltpu.VMEM((columns, Y * LANES), BF16),
        dma((11,)),
        dma((groups + 1,)),
        dma((2,)),
        dma((2,)),
        dma,
        dma,
        dma((6,)),
        dma((2, groups // 2)),
        dma((2,)),
        dma((2, groups // 2 + 1)),
        dma,
        dma,
        dma((max(zs, 2),)),
        dma((max(zs, 2),)),
        dma((4,)),
        dma((3,)),
        dma,
        dma,
        dma,
        dma,
        pltpu.SemaphoreType.REGULAR((3,)),
        pltpu.SemaphoreType.REGULAR,
    ]
    outs = (
        pltpu.VMEM((atoms, width), BF16),
        pltpu.VMEM((here, columns), BF16),
    )
    return pl.pallas_call(
        functools.partial(fused, zs, xs),
        out_shape=outs,
        in_specs=[anywhere] * len(operands),
        out_specs=(vmem, vmem),
        scratch_shapes=scratch,
        compiler_params=pltpu.CompilerParams(
            collective_id=0, has_side_effects=True, vmem_limit_bytes=56 * 2**20
        ),
    )(*operands)


def solution(mesh):
    in_specs = (
        P("tok", None),
        P("tok", None, None),
        P("tok"),
        P("tok"),
        P("tok", None),
        P("tok", "head", None),
        P(),
        P(),
        P(),
        P(),
        P("head", None),
        P("head", None),
    )
    out_specs = (P("tok", None), P("tok", "head"))
    return jax.shard_map(
        per_device, mesh=mesh, in_specs=in_specs, out_specs=out_specs, check_vma=False
    )
```

```python
import functools
import math

import jax
import jax.numpy as jnp
from jax import lax
from jax.experimental import pallas as pl
from jax.experimental.pallas import tpu as pltpu
from jax.sharding import PartitionSpec as P

ATOM_HEADS = 4
WQ = 32
WK = 128
RIM = (WK - WQ) // 2
BLOCK_DEVS = 4
HEAD_SIZE = 24
ATOM_HEAD_SIZE = 32
EPS = 1e-05

Y = 4
CORES = 2
ROWS = 8
CH = 32
HL = 4
CHUNK = HL * ROWS
LANES = 128

PAIR_MID = 9.5
PAIR_HALF = 14.5
CODE_MAX = 32700.0

F32 = jnp.float32
BF16 = jnp.bfloat16
I16 = jnp.int16
MESH = pl.DeviceIdType.MESH

OPP_UP, OPP_DN, DIR_UP, DIR_DN, FWD_UP, FWD_DN = range(6)


def iota(shape, dim):
    return lax.broadcasted_iota(jnp.int32, shape, dim)


def dot(a, b):
    return jnp.dot(a, b, preferred_element_type=F32)


def dot_nt(a, b):
    return lax.dot_general(a, b, (((1,), (1,)), ((), ())), preferred_element_type=F32)


def mask(cond):
    return jnp.where(cond, 1.0, 0.0).astype(F32)


def normalize(rows):
    mean = jnp.mean(rows, axis=-1, keepdims=True)
    centered = rows - mean
    spread = jnp.mean(centered * centered, axis=-1, keepdims=True)
    return centered * lax.rsqrt(spread + EPS)


def fused(
    zs,
    xs,
    atom_single,
    atom_bias,
    atom_token,
    atom_count,
    token_single,
    pair,
    atom_qkv,
    atom_wo,
    atom_agg,
    token_qkvg,
    pair_weight,
    token_wo,
    atom_out,
    token_out,
    single_v,
    bias_v,
    name_v,
    count_v,
    tok_v,
    pair_v,
    aqkv_v,
    awo_v,
    agg_v,
    qkvg_v,
    two_v,
    kv_pad,
    weights,
    own,
    hold_up,
    hold_dn,
    opp_up_s,
    opp_dn_s,
    dir_up_s,
    dir_dn_s,
    fwd_up_s,
    fwd_dn_s,
    opp_up_r,
    opp_dn_r,
    dir_up_r,
    dir_dn_r,
    fwd_up_r,
    fwd_dn_r,
    sum_s,
    sum_r,
    kv_all,
    score,
    mixed,
    fin_s,
    fin_r,
    proj_v,
    out_v,
    in_sem,
    pair_sem,
    halo_s,
    halo_r,
    w_s,
    w_r,
    y_s,
    opp_r,
    dir_r,
    fwd_r,
    sum_ss,
    sum_rs,
    z_s,
    z_r,
    x_s,
    x_r,
    c_s,
    c_r,
    fin_ss,
    fin_rs,
    known,
    near,
    opposite,
):
    tok = lax.axis_index("tok")
    y = lax.axis_index("head")
    devs = zs * xs * CORES
    z = lax.div(tok, xs * CORES)
    x = lax.rem(lax.div(tok, CORES), xs)
    c = lax.rem(tok, CORES)
    place = lax.rem(tok, BLOCK_DEVS)
    groups, depth, keys = pair_v.shape
    half = keys // 2
    here = tok_v.shape[0]
    atoms = single_v.shape[0]
    windows = atoms // WQ
    sub = half // 3 if half % 3 == 0 else half
    columns = HL * HEAD_SIZE
    paired = groups // 2

    def tok_of(z_, x_, c_):
        return (z_ * xs + x_) * CORES + c_

    def y_at(k):
        return lax.rem(y + k, Y)

    def x_at(k):
        return lax.rem(x + k, xs)

    def mate(k):
        return tok - place + lax.rem(place + k, BLOCK_DEVS)

    up, dn = {"head": y_at(1)}, {"head": y_at(3)}

    def remote(src, dst, send, recv, device):
        return pltpu.make_async_remote_copy(
            src_ref=src,
            dst_ref=dst,
            send_sem=send,
            recv_sem=recv,
            device_id=device,
            device_id_type=MESH,
        )

    def signal(sem, device):
        pl.semaphore_signal(sem, inc=1, device_id=device, device_id_type=MESH)

    barrier = pltpu.get_barrier_semaphore()
    for device in (up, dn):
        signal(barrier, device)

    loads = [
        (pair_weight, weights.at[0]),
        (atom_single, single_v),
        (atom_qkv, aqkv_v),
        (atom_bias, bias_v),
        (atom_wo, awo_v),
        (atom_agg, agg_v),
        (atom_token, name_v),
        (atom_count, count_v),
        (token_qkvg, qkvg_v),
        (token_single, tok_v),
        (token_wo, two_v),
    ]
    loads = [pltpu.make_async_copy(a, b, in_sem.at[i]) for i, (a, b) in enumerate(loads)]

    def pair_load(g):
        return pltpu.make_async_copy(
            pair.at[pl.ds(pl.multiple_of(g * depth, depth), depth), :],
            pair_v.at[g],
            pair_sem.at[g],
        )

    head_loads = [
        pltpu.make_async_copy(
            pair.at[pl.ds(0, depth), pl.ds(at, width)],
            pair_v.at[0, :, pl.ds(at, width)],
            pair_sem.at[sem],
        )
        for at, width, sem in ((0, sub, 0), (sub, half - sub, groups), (half, half, groups + 1))
        if width
    ]
    loads[0].start()
    for load in head_loads:
        load.start()
    loads[1].start()
    loads[2].start()
    for g in range(1, groups):
        pair_load(g).start()
    for load in loads[3:]:
        load.start()

    first_core = c == 0
    edges = []
    for k in range(1, BLOCK_DEVS):
        same = lax.div(place, CORES) == lax.div(lax.rem(place + k, BLOCK_DEVS), CORES)
        edges.append((None, jnp.where(same, first_core, place + k >= BLOCK_DEVS), mate(k)))
    for k in sorted({1, xs - 1}):
        edges.append((None, x + k >= xs, tok_of(z, x_at(k), c)))
    edges.append((None, first_core, tok_of(z, x, 1 - c)))
    edges.append((tok > 0, first_core, tok - 1))
    edges.append((tok < devs - 1, first_core, tok + 1))
    edges.append((z > 0, True, tok - xs * CORES))
    edges.append((z < zs - 1, False, tok + xs * CORES))

    def both(a, b):
        return b if a is None else a if b is True else jnp.logical_and(a, b)

    waited, waiting, expected, back = [], [], 2, 0
    for there, waits, other in edges:
        if waits is not False:
            waited.append((both(there, waits), other))
            expected = expected + waited[-1][0].astype(jnp.int32)
        if waits is not True:
            waiting.append((both(there, True if waits is False else jnp.logical_not(waits)), other))
            back = back + waiting[-1][0].astype(jnp.int32)

    def signal_all(sem, group):
        for there, other in group:

            @pl.when(there)
            def _():
                signal(sem, {"tok": other})

    signal_all(barrier, waiting)

    loads[0].wait()
    wt = weights[0]
    heads = wt.shape[0]
    row = iota((Y * CHUNK, heads), 0)
    owner = lax.rem(y + lax.div(row, CHUNK), Y)
    pick = iota((Y * CHUNK, heads), 1) == owner * HL + lax.rem(lax.div(row, ROWS), HL)
    picked = dot(mask(pick).astype(BF16), wt).astype(BF16)
    spread = mask(iota((CH, depth), 0) == lax.rem(iota((CH, depth), 1), CH)).astype(BF16)
    diag = lax.div(iota((Y * CHUNK, depth), 1), CH) == lax.rem(iota((Y * CHUNK, depth), 0), ROWS)
    lhs = (dot(picked, spread) * mask(diag)).astype(BF16)
    picked_f = picked.astype(F32)
    mid = PAIR_MID * jnp.sum(picked_f, axis=1, keepdims=True)
    reach = jnp.maximum(PAIR_HALF * jnp.sum(jnp.abs(picked_f), axis=1, keepdims=True), 1e-20)
    inv = CODE_MAX / reach

    buffers = {
        OPP_UP: (opp_up_s, opp_up_r, up),
        OPP_DN: (opp_dn_s, opp_dn_r, dn),
        DIR_UP: (dir_up_s, dir_up_r, up),
        DIR_DN: (dir_dn_s, dir_dn_r, dn),
        FWD_UP: (fwd_up_s, fwd_up_r, up),
        FWD_DN: (fwd_dn_s, fwd_dn_r, dn),
    }

    def landed(kind, g):
        if kind in (OPP_UP, OPP_DN):
            return opp_r.at[kind - OPP_UP, lax.div(g, 2)]
        if kind in (DIR_UP, DIR_DN):
            return dir_r.at[kind - DIR_UP]
        return fwd_r.at[kind - FWD_UP, jnp.maximum(lax.div(g, 2), g - (groups - 1) + paired)]

    def landed_last(kind, at):
        return fwd_r.at[kind - FWD_UP, paired + (1 if at else 0)]

    def piece(kind, g):
        src, dst, device = buffers[kind]
        return remote(src.at[g], dst.at[g], y_s.at[kind], landed(kind, g), device)

    def part_of(kind, g, at, width, sem):
        src, dst, device = buffers[kind]
        cols = pl.ds(at, width)
        return remote(src.at[g, :, cols], dst.at[g, :, cols], y_s.at[kind], sem, device)

    def pieces(kind, g, n):
        src, dst, device = buffers[kind]
        some = pl.ds(g, n)
        return remote(src.at[some], dst.at[some], y_s.at[kind], landed(kind, g), device)

    def coded(value, scale):
        return jnp.round(value * scale).astype(jnp.int32).astype(I16)

    def produce(g, sides, ats):
        for side in sides:
            for at in ats:
                cols = slice(side * half + at, side * half + at + sub)
                into = slice(at, at + sub)
                part = dot(lhs, pair_v[g, :, cols])
                own[g, :, cols] = part[0:CHUNK]
                part = part[CHUNK:] - mid[CHUNK:]
                to_up, to_opp, to_dn = (part[i * CHUNK : (i + 1) * CHUNK] for i in range(3))
                i_up, i_opp, i_dn = (inv[i * CHUNK : (i + 1) * CHUNK] for i in range(1, Y))
                if side == 0:
                    opp_up_s[g, :, into] = coded(to_opp, i_opp)
                    hold_up[g, :, into] = to_up
                    dir_dn_s[g, :, into] = coded(to_dn, i_dn)
                else:
                    opp_dn_s[g, :, into] = coded(to_opp, i_opp)
                    hold_dn[g, :, into] = to_dn
                    dir_up_s[g, :, into] = coded(to_up, i_up)

    ats = tuple(range(0, half, sub))
    head_loads[0].wait()
    produce(0, (0,), ats[:1])

    pl.semaphore_wait(barrier, expected)

    def weights_copy(k):
        to = {"head": y_at(k)}
        return remote(weights.at[0], weights.at[Y - k], w_s, w_r.at[1 if k == 2 else 0], to)

    weights_copy(1).start()
    weights_copy(3).start()
    for side in range(2):
        for at in ats:
            if side or at:
                if at == ats[1 - side]:
                    head_loads[1 + side].wait()
                produce(0, (side,), (at,))
            for kind in (OPP_DN, DIR_UP) if side else (OPP_UP, DIR_DN):
                part_of(kind, 0, at, sub, landed(kind, 0)).start()
    signal(opposite, up)
    signal_all(near, waited)

    rounds = [d for d in (1, 2, 4) if d < zs]

    def tell(r):
        for present, other in (
            (z >= rounds[r], tok - rounds[r] * xs * CORES),
            (z < zs - rounds[r], tok + rounds[r] * xs * CORES),
        ):

            @pl.when(present)
            def _():
                signal(known.at[r], {"tok": other})

    def learn(r):
        amount = (z >= rounds[r]).astype(jnp.int32) + (z < zs - rounds[r]).astype(jnp.int32)
        pl.semaphore_wait(known.at[r], amount)

    loads[1].wait()
    loads[2].wait()
    single = single_v[...].astype(F32)
    normed = normalize(single).astype(BF16)
    query = (dot(normed, aqkv_v[0]) * (1.0 / math.sqrt(ATOM_HEAD_SIZE))).astype(BF16)
    kv_pad[RIM : RIM + atoms, 0:LANES] = dot(normed, aqkv_v[1]).astype(BF16)
    kv_pad[RIM : RIM + atoms, LANES:] = dot(normed, aqkv_v[2]).astype(BF16)
    halo_up = remote(
        kv_pad.at[pl.ds(atoms, RIM), :],
        kv_pad.at[pl.ds(0, RIM), :],
        halo_s.at[0],
        halo_r.at[0],
        {"tok": lax.rem(tok + 1, devs)},
    )
    halo_dn = remote(
        kv_pad.at[pl.ds(RIM, RIM), :],
        kv_pad.at[pl.ds(atoms + RIM, RIM), :],
        halo_s.at[1],
        halo_r.at[1],
        {"tok": lax.rem(tok + devs - 1, devs)},
    )

    def rest(g, carry):
        pair_load(g).wait()
        produce(g, (0, 1), ats)
        for kind in (OPP_UP, OPP_DN, DIR_UP, DIR_DN):
            piece(kind, g).start()
        return carry

    lax.fori_loop(1, groups, rest, 0)

    @pl.when(back > 0)
    def _():
        pl.semaphore_wait(near, back)

    pl.semaphore_wait(opposite, 1)
    weights_copy(2).start()
    if len(rounds) > 0:
        tell(0)
    first, last = tok == 0, tok == devs - 1

    @pl.when(jnp.logical_not(last))
    def _():
        halo_up.start()

    @pl.when(jnp.logical_not(first))
    def _():
        halo_dn.start()

    def from_owner(value, k):
        shift = lax.rem((2 * Y - y - k) * columns, Y * columns)
        return pltpu.roll(value, shift, 1)[:, 0:LANES]

    for load in loads[4:]:
        load.wait()
    for i in range(4):
        proj_v[:, i * LANES : (i + 1) * LANES] = from_owner(
            qkvg_v[:, i, :].astype(F32), 0
        ).astype(BF16)
    for k in range(Y):
        out_v[:, k * LANES : (k + 1) * LANES] = from_owner(two_v[...].astype(F32), k).astype(BF16)
    if len(rounds) > 1:
        learn(0)
        tell(1)

    @pl.when(first)
    def _():
        kv_pad[0:RIM, :] = jnp.zeros((RIM, 2 * LANES), BF16)

    @pl.when(jnp.logical_not(first))
    def _():
        halo_up.wait_recv()
        halo_dn.wait_send()

    @pl.when(last)
    def _():
        kv_pad[atoms + RIM : atoms + 2 * RIM, :] = jnp.zeros((RIM, 2 * LANES), BF16)

    @pl.when(jnp.logical_not(last))
    def _():
        halo_dn.wait_recv()
        halo_up.wait_send()

    loads[3].wait()
    wide = WQ * ATOM_HEADS
    grow = mask(lax.div(iota((wide, WQ), 0), ATOM_HEADS) == iota((wide, WQ), 1)).astype(BF16)
    fold = mask(iota((WQ, wide), 0) == lax.div(iota((WQ, wide), 1), ATOM_HEADS)).astype(BF16)
    in_head = mask(
        lax.div(iota((wide, LANES), 1), ATOM_HEAD_SIZE) == lax.rem(iota((wide, LANES), 0), ATOM_HEADS)
    )
    slot = iota((wide, WK), 1)
    scores = []
    for w in range(windows):
        q_rows = (dot(grow, query[w * WQ : (w + 1) * WQ]) * in_head).astype(BF16)
        s = dot_nt(q_rows, kv_pad[w * WQ : w * WQ + WK, 0:LANES])
        s = s + bias_v[w * wide : (w + 1) * wide, :].astype(F32)
        if w * WQ < RIM or w * WQ + WK > RIM + atoms:
            spot = tok * atoms + w * WQ - RIM + slot
            s = jnp.where((spot >= 0) & (spot < devs * atoms), s, -1e30)
        scores.append(s)
    probs = []
    for s in scores:
        e = jnp.exp(s - jnp.max(s, axis=-1, keepdims=True))
        probs.append((e * (1.0 / jnp.sum(e, axis=-1, keepdims=True))).astype(BF16))
    mixes = []
    for w in range(windows):
        m = dot(probs[w], kv_pad[w * WQ : w * WQ + WK, LANES:])
        mixes.append(dot(fold, (m * in_head).astype(BF16)).astype(BF16))
    mix = jnp.concatenate(mixes, axis=0)
    a_out = (single + dot(mix, awo_v[...])).astype(BF16)
    atom_out[...] = a_out
    feat = jnp.maximum(dot(a_out, agg_v[...]), 0.0).astype(BF16)

    block = iota((BLOCK_DEVS * here, 1), 0)
    owner_tok = mate(lax.div(block, here)) * here + lax.rem(block, here)
    onehot = mask(owner_tok == name_v[...]).astype(BF16)
    sums = dot(onehot, feat)
    for k in range(1, BLOCK_DEVS):
        sum_s[k] = sums[k * here : (k + 1) * here].astype(BF16)
        remote(
            sum_s.at[k], sum_r.at[BLOCK_DEVS - k], sum_ss, sum_rs, {"tok": mate(k)}
        ).start()
    if len(rounds) > 2:
        learn(1)
        tell(2)

    others = pl.ds(1, BLOCK_DEVS - 1)
    remote(sum_s.at[others], sum_r.at[others], sum_ss, sum_rs, up).wait()
    total = sums[0:here]
    for k in range(1, BLOCK_DEVS):
        total = total + sum_r[k].astype(F32)
    square = iota((here, here), 0) == iota((here, here), 1)
    count = jnp.sum(jnp.where(square, count_v[...].astype(F32), 0.0), axis=1, keepdims=True)
    token_mid = tok_v[...].astype(F32) + total / count
    normed_t = normalize(token_mid).astype(BF16)
    parts = dot(normed_t, proj_v[...])
    t_query = (parts[:, 0:LANES] * (1.0 / math.sqrt(HEAD_SIZE))).astype(BF16)
    kv_all[z, x, c] = parts[:, LANES : 3 * LANES].astype(BF16)
    gate = jax.nn.sigmoid(parts[:, 3 * LANES :])
    residual = from_owner(token_mid, 0)

    if rounds:
        learn(len(rounds) - 1)
    sent = []
    for k in range(1, zs):
        block_k = kv_all.at[z, x, c]
        copy = remote(
            block_k, block_k, z_s.at[k], z_r.at[k], {"tok": tok_of(lax.rem(z + k, zs), x, c)}
        )
        copy.start()
        sent.append(copy)

    two = pl.ds(1, 2)
    remote(weights.at[two], weights.at[two], w_s, w_r.at[0], up).wait_recv()
    r32 = iota((CHUNK, heads), 0)

    def reach_of(sender, k):
        head = y_at(k) * HL + lax.div(r32, ROWS)
        sel = mask(iota((CHUNK, heads), 1) == head).astype(BF16)
        chosen = dot(sel, weights[sender])
        return jnp.maximum(PAIR_HALF * jnp.sum(jnp.abs(chosen), axis=1, keepdims=True), 1e-20)

    step = 1.0 / CODE_MAX
    legs = []
    for kind, out, hold, src, k, to in (
        (OPP_UP, fwd_up_s, hold_up, opp_up_r, 1, FWD_UP),
        (OPP_DN, fwd_dn_s, hold_dn, opp_dn_r, 3, FWD_DN),
    ):
        theirs = reach_of(Y - k, k)
        legs.append((kind, out, hold, src, to, theirs * step, CODE_MAX / (theirs + reach_of(0, k))))
    r_up, r_dn = reach_of(1, 0), reach_of(3, 0)
    s_up, s_dn = r_up * step, r_dn * step

    early = half - sub if half > sub else half
    last_parts = [(0, early), (early, half - early)] if early < half else [(0, half)]

    def forward(g, last):
        for kind, out, hold, src, to, theirs, scale in legs:
            out[g] = coded(src[g].astype(F32) * theirs + hold[g], scale)
            if not last:
                piece(to, g).start()
        if last:
            for at, width in last_parts:
                for to in (FWD_UP, FWD_DN):
                    part_of(to, g, at, width, landed_last(to, at)).start()

    def forward_two(i, last=False):
        for kind in (OPP_UP, OPP_DN):
            pieces(kind, 2 * i, 2).wait_recv()
        forward(2 * i, False)
        forward(2 * i + 1, last)

    forward_two(0)

    for k in range(1, zs):
        block_k = kv_all.at[lax.rem(z + zs - k, zs), x, c]
        remote(block_k, block_k, z_s.at[k], z_r.at[k], {"tok": tok}).wait_recv()

    def column(k):
        return kv_all.at[:, x_at(k), c]

    def send(ref, s_sem, r_sem, device):
        copy = remote(ref, ref, s_sem, r_sem, device)
        copy.start()
        return copy

    x_up, x_dn = {"tok": tok_of(z, x_at(1), c)}, {"tok": tok_of(z, x_at(xs - 1), c)}
    other = {"tok": tok_of(z, x, 1 - c)}
    sent.append(send(column(0), x_s.at[0], x_r.at[0], x_up))
    if xs > 2:
        sent.append(send(column(0), x_s.at[1], x_r.at[1], x_dn))
    send(column(0), c_s, c_r, other)

    forward_two(1)

    def arrived(ref, sem):
        remote(ref, ref, x_s.at[0], sem, other).wait_recv()

    arrived(column(xs - 1), x_r.at[0])
    if xs > 2:
        lower, upper = pl.ds(0, zs // 2), pl.ds(zs // 2, zs - zs // 2)
        sent.append(send(kv_all.at[lower, x_at(xs - 1), c], x_s.at[2], x_r.at[2], x_up))
        arrived(column(1), x_r.at[1])
        sent.append(send(kv_all.at[upper, x_at(1), c], x_s.at[3], x_r.at[2], x_dn))
        send(column(1), c_s, c_r, other)
    send(column(xs - 1), c_s, c_r, other)

    forward_two(2, True)

    if xs > 2:
        arrived(column(2), x_r.at[2])
        send(column(2), c_s, c_r, other)
    arrived(kv_all.at[:, :, 1 - c], c_r)

    rows = groups * CHUNK
    rr = iota((rows, here), 0)
    pick_row = lax.div(rr, CHUNK) * ROWS + lax.rem(rr, ROWS) == iota((rows, here), 1)
    rl = iota((rows, LANES), 0)
    of_head = mask(
        lax.div(iota((rows, LANES), 1), HEAD_SIZE) == lax.rem(lax.div(rl, ROWS), HL)
    )
    q_rows = (dot(mask(pick_row).astype(BF16), t_query) * of_head).astype(BF16)
    key_rows = kv_all[..., 0:LANES].reshape(keys, LANES)
    for at in range(0, keys, 2 * sub):
        s = dot_nt(q_rows, key_rows[at : at + 2 * sub])
        score[:, :, at : at + 2 * sub] = s.reshape(groups, CHUNK, 2 * sub)

    for kind in (DIR_UP, DIR_DN):
        pieces(kind, 0, groups).wait_recv()

    def direct(g, carry):
        for side, (ref, scale) in enumerate(((dir_dn_r, s_up), (dir_up_r, s_dn))):
            for at in range(0, half, sub):
                cols = slice(side * half + at, side * half + at + sub)
                got = ref[g, :, at : at + sub].astype(F32) * scale
                score[g, :, cols] = score[g, :, cols] + (own[g, :, cols] + got)
        return carry

    lax.fori_loop(0, groups, direct, 0)

    head_mask = of_head[0:CHUNK]

    weights_copy(2).wait_recv()
    r_opp = reach_of(2, 0)
    s_up2, s_dn2 = (r_up + r_opp) * step, (r_dn + r_opp) * step

    def attend_part(g, at_first, width, state):
        spans = []
        peak = state[0] if state else None
        for side, (ref, scale) in enumerate(((fwd_up_r, s_dn2), (fwd_dn_r, s_up2))):
            for at in range(at_first, at_first + width, sub):
                cols = slice(side * half + at, side * half + at + sub)
                s = score[g, :, cols] + ref[g, :, at : at + sub].astype(F32) * scale
                score[g, :, cols] = s
                spans.append(cols)
                high = jnp.max(s, axis=-1, keepdims=True)
                peak = high if peak is None else jnp.maximum(peak, high)
        if state:
            shrink = jnp.exp(state[0] - peak)
            norm, acc = state[1] * shrink, state[2] * shrink
        else:
            norm, acc = jnp.zeros((CHUNK, 1), F32), jnp.zeros((CHUNK, LANES), F32)
        value_rows = kv_all[..., LANES:].reshape(keys, LANES)
        for cols in spans:
            e = jnp.exp(score[g, :, cols] - peak)
            norm = norm + jnp.sum(e, axis=-1, keepdims=True)
            acc = acc + dot(e.astype(BF16), value_rows[cols])
        return peak, norm, acc

    def finish(g, state):
        acc = state[2] * head_mask / state[1]
        mixed[g] = jnp.sum(acc.reshape(HL, ROWS, LANES), axis=0)

    def attend(g, carry):
        finish(g, attend_part(g, 0, half, None))
        return carry

    for g in range(0, groups - 2, 2):
        for kind in (FWD_UP, FWD_DN):
            pieces(kind, g, 2).wait_recv()
        lax.fori_loop(g, g + 2, attend, 0)
    for kind in (FWD_UP, FWD_DN):
        piece(kind, groups - 2).wait_recv()
    attend(groups - 2, 0)
    state = None
    for at, width in last_parts:
        for kind in (FWD_UP, FWD_DN):
            part_of(kind, groups - 1, at, width, landed_last(kind, at)).wait_recv()
        state = attend_part(groups - 1, at, width, state)
    finish(groups - 1, state)

    out_rows = (mixed[...].reshape(here, LANES) * gate).astype(BF16)
    term = dot(out_rows[:, 0:columns], out_v[...])
    for k in range(1, Y):
        fin_s[k] = term[:, k * LANES : (k + 1) * LANES].astype(BF16)
        remote(fin_s.at[k], fin_r.at[Y - k], fin_ss, fin_rs, {"head": y_at(k)}).start()
    peers = pl.ds(1, Y - 1)
    for kind in range(6):
        pieces(kind, 0, groups).wait_send()
    remote(weights.at[peers], weights.at[peers], w_s, w_r.at[0], up).wait_send()
    for copy in sent:
        copy.wait_send()
    remote(kv_all.at[:, :, c], kv_all.at[:, :, c], c_s, c_r, other).wait_send()
    result = residual + term[:, 0:LANES]
    remote(fin_s.at[peers], fin_r.at[peers], fin_ss, fin_rs, up).wait()
    for k in range(1, Y):
        result = result + fin_r[k].astype(F32)
    token_out[...] = result[:, 0:columns].astype(BF16)


def hand_over(a, b, a_out, b_out, sems):
    copies = [
        pltpu.make_async_copy(a, a_out, sems.at[0]),
        pltpu.make_async_copy(b, b_out, sems.at[1]),
    ]
    for copy in copies:
        copy.start()
    for copy in copies:
        copy.wait()


def per_device(
    atom_single,
    atom_bias,
    atom_token,
    atom_count,
    token_single,
    pair,
    atom_qkv,
    atom_wo,
    atom_agg,
    token_qkvg,
    pair_weight,
    token_wo,
):
    devs = lax.axis_size("tok")
    xs = 4 if devs % 32 == 0 else 2
    zs = devs // (xs * CORES)
    atoms, width = atom_single.shape
    here, width_t = token_single.shape
    keys = pair.shape[2]
    groups = here // ROWS
    half = keys // 2
    columns = width_t // Y
    depth = ROWS * CH
    anywhere = pl.BlockSpec(memory_space=pl.ANY)
    vmem = pl.BlockSpec(memory_space=pltpu.VMEM)
    dma = pltpu.SemaphoreType.DMA
    code = pltpu.VMEM((groups, CHUNK, half), I16)
    operands = (
        atom_single,
        atom_bias.reshape(atoms * ATOM_HEADS, WK),
        atom_token.reshape(1, atoms),
        atom_count.reshape(1, here),
        token_single,
        pair.reshape(here * CH, keys),
        jnp.transpose(atom_qkv, (1, 0, 2)),
        atom_wo,
        atom_agg,
        token_qkvg,
        jnp.transpose(pair_weight),
        token_wo,
    )
    scratch = [
        pltpu.VMEM((atoms, width), BF16),
        pltpu.VMEM((atoms * ATOM_HEADS, WK), BF16),
        pltpu.VMEM((1, atoms), jnp.int32),
        pltpu.VMEM((1, here), jnp.int32),
        pltpu.VMEM((here, width_t), BF16),
        pltpu.VMEM((groups, depth, keys), BF16),
        pltpu.VMEM((3, width, width), BF16),
        pltpu.VMEM(atom_wo.shape, BF16),
        pltpu.VMEM(atom_agg.shape, BF16),
        pltpu.VMEM(token_qkvg.shape, BF16),
        pltpu.VMEM(token_wo.shape, BF16),
        pltpu.VMEM((atoms + 2 * RIM, 2 * width), BF16),
        pltpu.VMEM((Y, Y * HL, CH), BF16),
        pltpu.VMEM((groups, CHUNK, keys), F32),
        pltpu.VMEM((groups, CHUNK, half), F32),
        pltpu.VMEM((groups, CHUNK, half), F32),
        *([code] * 12),
        pltpu.VMEM((BLOCK_DEVS, here, width_t), BF16),
        pltpu.VMEM((BLOCK_DEVS, here, width_t), BF16),
        pltpu.VMEM((zs, xs, CORES, here, 2 * LANES), BF16),
        pltpu.VMEM((groups, CHUNK, keys), F32),
        pltpu.VMEM((groups, ROWS, LANES), F32),
        pltpu.VMEM((Y, here, LANES), BF16),
        pltpu.VMEM((Y, here, LANES), BF16),
        pltpu.VMEM((width_t, 4 * LANES), BF16),
        pltpu.VMEM((columns, Y * LANES), BF16),
        dma((11,)),
        dma((groups + 2,)),
        dma((2,)),
        dma((2,)),
        dma,
        dma((2,)),
        dma((6,)),
        dma((2, groups // 2)),
        dma((2,)),
        dma((2, groups // 2 + 2)),
        dma,
        dma,
        dma((max(zs, 2),)),
        dma((max(zs, 2),)),
        dma((4,)),
        dma((3,)),
        dma,
        dma,
        dma,
        dma,
        pltpu.SemaphoreType.REGULAR((3,)),
        pltpu.SemaphoreType.REGULAR,
        pltpu.SemaphoreType.REGULAR,
    ]
    outs = (
        pltpu.VMEM((atoms, width), BF16),
        pltpu.VMEM((here, columns), BF16),
    )
    results = pl.pallas_call(
        functools.partial(fused, zs, xs),
        out_shape=outs,
        in_specs=[anywhere] * len(operands),
        out_specs=(vmem, vmem),
        scratch_shapes=scratch,
        compiler_params=pltpu.CompilerParams(
            collective_id=0, has_side_effects=True, vmem_limit_bytes=56 * 2**20
        ),
    )(*operands)
    results = [pltpu.with_memory_space_constraint(r, pltpu.VMEM) for r in results]
    return pl.pallas_call(
        hand_over,
        out_shape=tuple(pltpu.HBM(r.shape, r.dtype) for r in results),
        in_specs=[anywhere, anywhere],
        out_specs=(anywhere, anywhere),
        scratch_shapes=[dma((2,))],
    )(*results)


def solution(mesh):
    in_specs = (
        P("tok", None),
        P("tok", None, None),
        P("tok"),
        P("tok"),
        P("tok", None),
        P("tok", "head", None),
        P(),
        P(),
        P(),
        P(),
        P("head", None),
        P("head", None),
    )
    out_specs = (P("tok", None), P("tok", "head"))
    return jax.shard_map(
        per_device, mesh=mesh, in_specs=in_specs, out_specs=out_specs, check_vma=False
    )
```

```python
import functools
import math

import jax
import jax.numpy as jnp
from jax import lax
from jax.experimental import pallas as pl
from jax.experimental.pallas import tpu as pltpu
from jax.sharding import PartitionSpec as P

ATOM_HEADS = 4
WQ = 32
WK = 128
RIM = (WK - WQ) // 2
BLOCK_DEVS = 4
HEAD_SIZE = 24
ATOM_HEAD_SIZE = 32
EPS = 1e-05

Y = 4
CORES = 2
ROWS = 8
CH = 32
HL = 4
CHUNK = HL * ROWS
LANES = 128

PAIR_MID = 9.5
PAIR_HALF = 14.5
CODE_MAX = 32700.0

F32 = jnp.float32
BF16 = jnp.bfloat16
I16 = jnp.int16
MESH = pl.DeviceIdType.MESH

OPP_UP, OPP_DN, DIR_UP, DIR_DN, FWD_UP, FWD_DN = range(6)


def iota(shape, dim):
    return lax.broadcasted_iota(jnp.int32, shape, dim)


def dot(a, b):
    return jnp.dot(a, b, preferred_element_type=F32)


def dot_nt(a, b):
    return lax.dot_general(a, b, (((1,), (1,)), ((), ())), preferred_element_type=F32)


def mask(cond):
    return jnp.where(cond, 1.0, 0.0).astype(F32)


def normalize(rows):
    mean = jnp.mean(rows, axis=-1, keepdims=True)
    centered = rows - mean
    spread = jnp.mean(centered * centered, axis=-1, keepdims=True)
    return centered * lax.rsqrt(spread + EPS)


def fused(
    zs,
    xs,
    atom_single,
    atom_bias,
    atom_token,
    atom_count,
    token_single,
    pair,
    atom_qkv,
    atom_wo,
    atom_agg,
    token_qkvg,
    pair_weight,
    token_wo,
    atom_out,
    token_out,
    single_v,
    bias_v,
    name_v,
    count_v,
    tok_v,
    pair_v,
    aqkv_v,
    awo_v,
    agg_v,
    qkvg_v,
    two_v,
    kv_pad,
    weights,
    own,
    hold_up,
    hold_dn,
    codes_s,
    opp_up_r,
    opp_dn_r,
    dir_up_r,
    dir_dn_r,
    fwd_up_r,
    fwd_dn_r,
    sum_s,
    sum_r,
    kv_all,
    score,
    mixed,
    fin_s,
    fin_r,
    proj_v,
    out_v,
    in_sem,
    pair_sem,
    halo_s,
    halo_r,
    w_s,
    w_r,
    y_s,
    opp_r,
    dir_r,
    fwd_r,
    sum_ss,
    sum_rs,
    z_s,
    z_r,
    x_s,
    x_r,
    c_s,
    c_r,
    fin_ss,
    fin_rs,
    known,
    near,
    opposite,
):
    tok = lax.axis_index("tok")
    y = lax.axis_index("head")
    devs = zs * xs * CORES
    z = lax.div(tok, xs * CORES)
    x = lax.rem(lax.div(tok, CORES), xs)
    c = lax.rem(tok, CORES)
    place = lax.rem(tok, BLOCK_DEVS)
    groups, depth, keys = pair_v.shape
    half = keys // 2
    here = tok_v.shape[0]
    atoms = single_v.shape[0]
    windows = atoms // WQ
    sub = half // 3 if half % 3 == 0 else half
    columns = HL * HEAD_SIZE
    paired = groups // 2

    def tok_of(z_, x_, c_):
        return (z_ * xs + x_) * CORES + c_

    def y_at(k):
        return lax.rem(y + k, Y)

    def x_at(k):
        return lax.rem(x + k, xs)

    def mate(k):
        return tok - place + lax.rem(place + k, BLOCK_DEVS)

    up, dn = {"head": y_at(1)}, {"head": y_at(3)}

    def remote(src, dst, send, recv, device):
        return pltpu.make_async_remote_copy(
            src_ref=src,
            dst_ref=dst,
            send_sem=send,
            recv_sem=recv,
            device_id=device,
            device_id_type=MESH,
        )

    def signal(sem, device):
        pl.semaphore_signal(sem, inc=1, device_id=device, device_id_type=MESH)

    barrier = pltpu.get_barrier_semaphore()
    for device in (up, dn):
        signal(barrier, device)

    opp_up_s, opp_dn_s, dir_up_s, dir_dn_s, fwd_up_s, fwd_dn_s = (codes_s.at[i] for i in range(6))

    loads = [
        (pair_weight, weights.at[0]),
        (atom_single, single_v),
        (atom_qkv, aqkv_v),
        (atom_bias, bias_v),
        (atom_wo, awo_v),
        (atom_agg, agg_v),
        (atom_token, name_v),
        (atom_count, count_v),
        (token_qkvg, qkvg_v),
        (token_single, tok_v),
        (token_wo, two_v),
    ]
    loads = [pltpu.make_async_copy(a, b, in_sem.at[i]) for i, (a, b) in enumerate(loads)]

    def pair_load(g):
        return pltpu.make_async_copy(
            pair.at[pl.ds(pl.multiple_of(g * depth, depth), depth), :],
            pair_v.at[g],
            pair_sem.at[5 if g == 1 else g // 2],
        )

    head_loads = [
        pltpu.make_async_copy(
            pair.at[pl.ds(0, depth), pl.ds(at, width)],
            pair_v.at[0, :, pl.ds(at, width)],
            pair_sem.at[sem],
        )
        for at, width, sem in ((0, sub, 0), (sub, half - sub, 3), (half, half, 4))
        if width
    ]
    loads[0].start()
    for load in head_loads:
        load.start()
    loads[1].start()
    loads[2].start()
    for g in range(1, groups):
        pair_load(g).start()
    for load in loads[3:]:
        load.start()

    first_core = c == 0
    edges = []
    for k in range(1, BLOCK_DEVS):
        same = lax.div(place, CORES) == lax.div(lax.rem(place + k, BLOCK_DEVS), CORES)
        edges.append((None, jnp.where(same, first_core, place + k >= BLOCK_DEVS), mate(k)))
    for k in sorted({1, xs - 1}):
        edges.append((None, x + k >= xs, tok_of(z, x_at(k), c)))
    edges.append((None, first_core, tok_of(z, x, 1 - c)))
    edges.append((tok > 0, first_core, tok - 1))
    edges.append((tok < devs - 1, first_core, tok + 1))
    edges.append((z > 0, True, tok - xs * CORES))
    edges.append((z < zs - 1, False, tok + xs * CORES))

    def both(a, b):
        return b if a is None else a if b is True else jnp.logical_and(a, b)

    waited, waiting, expected, back = [], [], 2, 0
    for there, waits, other in edges:
        if waits is not False:
            waited.append((both(there, waits), other))
            expected = expected + waited[-1][0].astype(jnp.int32)
        if waits is not True:
            waiting.append((both(there, True if waits is False else jnp.logical_not(waits)), other))
            back = back + waiting[-1][0].astype(jnp.int32)

    def signal_all(sem, group):
        for there, other in group:

            @pl.when(there)
            def _():
                signal(sem, {"tok": other})

    signal_all(barrier, waiting)

    loads[0].wait()
    wt = weights[0]
    heads = wt.shape[0]
    row = iota((Y * CHUNK, heads), 0)
    owner = lax.rem(y + lax.div(row, CHUNK), Y)
    pick = iota((Y * CHUNK, heads), 1) == owner * HL + lax.rem(lax.div(row, ROWS), HL)
    picked = dot(mask(pick).astype(BF16), wt).astype(BF16)
    spread = mask(iota((CH, depth), 0) == lax.rem(iota((CH, depth), 1), CH)).astype(BF16)
    diag = lax.div(iota((Y * CHUNK, depth), 1), CH) == lax.rem(iota((Y * CHUNK, depth), 0), ROWS)
    lhs = (dot(picked, spread) * mask(diag)).astype(BF16)
    picked_f = picked.astype(F32)
    mid = PAIR_MID * jnp.sum(picked_f, axis=1, keepdims=True)
    reach = jnp.maximum(PAIR_HALF * jnp.sum(jnp.abs(picked_f), axis=1, keepdims=True), 1e-20)
    inv = CODE_MAX / reach

    buffers = {
        OPP_UP: (opp_up_s, opp_up_r, up),
        OPP_DN: (opp_dn_s, opp_dn_r, dn),
        DIR_UP: (dir_up_s, dir_up_r, up),
        DIR_DN: (dir_dn_s, dir_dn_r, dn),
        FWD_UP: (fwd_up_s, fwd_up_r, up),
        FWD_DN: (fwd_dn_s, fwd_dn_r, dn),
    }

    def landed(kind, g):
        if kind in (OPP_UP, OPP_DN):
            return opp_r.at[kind - OPP_UP, lax.div(g, 2)]
        if kind in (DIR_UP, DIR_DN):
            return dir_r.at[kind - DIR_UP]
        return fwd_r.at[kind - FWD_UP, jnp.maximum(lax.div(g, 2), g - (groups - 1) + paired)]

    def landed_last(kind, at):
        return fwd_r.at[kind - FWD_UP, paired + (1 if at else 0)]

    def piece(kind, g):
        src, dst, device = buffers[kind]
        return remote(src.at[g], dst.at[g], y_s, landed(kind, g), device)

    def part_of(kind, g, at, width, sem):
        src, dst, device = buffers[kind]
        cols = pl.ds(at, width)
        return remote(src.at[g, :, cols], dst.at[g, :, cols], y_s, sem, device)

    def pieces(kind, g, n):
        src, dst, device = buffers[kind]
        some = pl.ds(g, n)
        return remote(src.at[some], dst.at[some], y_s, landed(kind, g), device)

    def coded(value, scale):
        return jnp.round(value * scale).astype(jnp.int32).astype(I16)

    def produce(g, sides, ats):
        for side in sides:
            for at in ats:
                cols = slice(side * half + at, side * half + at + sub)
                into = slice(at, at + sub)
                part = dot(lhs, pair_v[g, :, cols])
                own[g, :, cols] = part[0:CHUNK]
                part = part[CHUNK:] - mid[CHUNK:]
                to_up, to_opp, to_dn = (part[i * CHUNK : (i + 1) * CHUNK] for i in range(3))
                i_up, i_opp, i_dn = (inv[i * CHUNK : (i + 1) * CHUNK] for i in range(1, Y))
                if side == 0:
                    opp_up_s[g, :, into] = coded(to_opp, i_opp)
                    hold_up[g, :, into] = to_up
                    dir_dn_s[g, :, into] = coded(to_dn, i_dn)
                else:
                    opp_dn_s[g, :, into] = coded(to_opp, i_opp)
                    hold_dn[g, :, into] = to_dn
                    dir_up_s[g, :, into] = coded(to_up, i_up)

    ats = tuple(range(0, half, sub))
    head_loads[0].wait()
    produce(0, (0,), ats[:1])

    pl.semaphore_wait(barrier, expected)

    def weights_copy(k):
        to = {"head": y_at(k)}
        return remote(weights.at[0], weights.at[Y - k], w_s, w_r.at[1 if k == 2 else 0], to)

    for side in range(2):
        for at in ats:
            if side or at:
                if at == ats[1 - side]:
                    head_loads[1 + side].wait()
                produce(0, (side,), (at,))
            for kind in (OPP_DN, DIR_UP) if side else (OPP_UP, DIR_DN):
                part_of(kind, 0, at, sub, landed(kind, 0)).start()
    weights_copy(1).start()
    weights_copy(3).start()
    signal(opposite, up)
    signal_all(near, waited)

    rounds = [d for d in (1, 2, 4) if d < zs]

    def tell(r):
        for present, other in (
            (z >= rounds[r], tok - rounds[r] * xs * CORES),
            (z < zs - rounds[r], tok + rounds[r] * xs * CORES),
        ):

            @pl.when(present)
            def _():
                signal(known.at[r], {"tok": other})

    def learn(r):
        amount = (z >= rounds[r]).astype(jnp.int32) + (z < zs - rounds[r]).astype(jnp.int32)
        pl.semaphore_wait(known.at[r], amount)

    loads[1].wait()
    loads[2].wait()
    single = single_v[...].astype(F32)
    normed = normalize(single).astype(BF16)
    query = (dot(normed, aqkv_v[0]) * (1.0 / math.sqrt(ATOM_HEAD_SIZE))).astype(BF16)
    kv_pad[RIM : RIM + atoms, 0:LANES] = dot(normed, aqkv_v[1]).astype(BF16)
    kv_pad[RIM : RIM + atoms, LANES:] = dot(normed, aqkv_v[2]).astype(BF16)
    halo_up = remote(
        kv_pad.at[pl.ds(atoms, RIM), :],
        kv_pad.at[pl.ds(0, RIM), :],
        halo_s.at[0],
        halo_r.at[0],
        {"tok": lax.rem(tok + 1, devs)},
    )
    halo_dn = remote(
        kv_pad.at[pl.ds(RIM, RIM), :],
        kv_pad.at[pl.ds(atoms + RIM, RIM), :],
        halo_s.at[1],
        halo_r.at[1],
        {"tok": lax.rem(tok + devs - 1, devs)},
    )

    def rest(g, carry):
        produce(g, (0, 1), ats)
        for kind in (OPP_UP, OPP_DN, DIR_UP, DIR_DN):
            piece(kind, g).start()
        return carry

    pair_load(1).wait()
    rest(1, 0)
    for g in range(2, groups, 2):
        two_groups = pair_v.at[pl.ds(g, 2)]
        pltpu.make_async_copy(two_groups, two_groups, pair_sem.at[g // 2]).wait()
        lax.fori_loop(g, g + 2, rest, 0)

    @pl.when(back > 0)
    def _():
        pl.semaphore_wait(near, back)

    pl.semaphore_wait(opposite, 1)
    weights_copy(2).start()
    if len(rounds) > 0:
        tell(0)
    first, last = tok == 0, tok == devs - 1

    @pl.when(jnp.logical_not(last))
    def _():
        halo_up.start()

    @pl.when(jnp.logical_not(first))
    def _():
        halo_dn.start()

    def from_owner(value, k):
        shift = lax.rem((2 * Y - y - k) * columns, Y * columns)
        return pltpu.roll(value, shift, 1)[:, 0:LANES]

    for load in loads[4:]:
        load.wait()
    for i in range(4):
        proj_v[:, i * LANES : (i + 1) * LANES] = from_owner(
            qkvg_v[:, i, :].astype(F32), 0
        ).astype(BF16)
    for k in range(Y):
        out_v[:, k * LANES : (k + 1) * LANES] = from_owner(two_v[...].astype(F32), k).astype(BF16)
    if len(rounds) > 1:
        learn(0)
        tell(1)

    @pl.when(first)
    def _():
        kv_pad[0:RIM, :] = jnp.zeros((RIM, 2 * LANES), BF16)

    @pl.when(jnp.logical_not(first))
    def _():
        halo_up.wait_recv()
        halo_dn.wait_send()

    @pl.when(last)
    def _():
        kv_pad[atoms + RIM : atoms + 2 * RIM, :] = jnp.zeros((RIM, 2 * LANES), BF16)

    @pl.when(jnp.logical_not(last))
    def _():
        halo_dn.wait_recv()
        halo_up.wait_send()

    loads[3].wait()
    wide = WQ * ATOM_HEADS
    grow = mask(lax.div(iota((wide, WQ), 0), ATOM_HEADS) == iota((wide, WQ), 1)).astype(BF16)
    fold = mask(iota((WQ, wide), 0) == lax.div(iota((WQ, wide), 1), ATOM_HEADS)).astype(BF16)
    in_head = mask(
        lax.div(iota((wide, LANES), 1), ATOM_HEAD_SIZE) == lax.rem(iota((wide, LANES), 0), ATOM_HEADS)
    )
    slot = iota((wide, WK), 1)
    scores = []
    for w in range(windows):
        q_rows = (dot(grow, query[w * WQ : (w + 1) * WQ]) * in_head).astype(BF16)
        s = dot_nt(q_rows, kv_pad[w * WQ : w * WQ + WK, 0:LANES])
        s = s + bias_v[w * wide : (w + 1) * wide, :].astype(F32)
        if w * WQ < RIM or w * WQ + WK > RIM + atoms:
            spot = tok * atoms + w * WQ - RIM + slot
            s = jnp.where((spot >= 0) & (spot < devs * atoms), s, -1e30)
        scores.append(s)
    probs = []
    for s in scores:
        e = jnp.exp(s - jnp.max(s, axis=-1, keepdims=True))
        probs.append((e * (1.0 / jnp.sum(e, axis=-1, keepdims=True))).astype(BF16))
    mixes = []
    for w in range(windows):
        m = dot(probs[w], kv_pad[w * WQ : w * WQ + WK, LANES:])
        mixes.append(dot(fold, (m * in_head).astype(BF16)).astype(BF16))
    mix = jnp.concatenate(mixes, axis=0)
    a_out = (single + dot(mix, awo_v[...])).astype(BF16)
    atom_out[...] = a_out
    feat = jnp.maximum(dot(a_out, agg_v[...]), 0.0).astype(BF16)

    block = iota((BLOCK_DEVS * here, 1), 0)
    owner_tok = mate(lax.div(block, here)) * here + lax.rem(block, here)
    onehot = mask(owner_tok == name_v[...]).astype(BF16)
    sums = dot(onehot, feat)
    for k in range(1, BLOCK_DEVS):
        sum_s[k] = sums[k * here : (k + 1) * here].astype(BF16)
        remote(
            sum_s.at[k], sum_r.at[BLOCK_DEVS - k], sum_ss, sum_rs, {"tok": mate(k)}
        ).start()
    if len(rounds) > 2:
        learn(1)
        tell(2)

    others = pl.ds(1, BLOCK_DEVS - 1)
    remote(sum_s.at[others], sum_r.at[others], sum_ss, sum_rs, up).wait()
    total = sums[0:here]
    for k in range(1, BLOCK_DEVS):
        total = total + sum_r[k].astype(F32)
    square = iota((here, here), 0) == iota((here, here), 1)
    count = jnp.sum(jnp.where(square, count_v[...].astype(F32), 0.0), axis=1, keepdims=True)
    token_mid = tok_v[...].astype(F32) + total / count
    normed_t = normalize(token_mid).astype(BF16)
    parts = dot(normed_t, proj_v[...])
    t_query = (parts[:, 0:LANES] * (1.0 / math.sqrt(HEAD_SIZE))).astype(BF16)
    kv_all[z, x, c] = parts[:, LANES : 3 * LANES].astype(BF16)
    gate = jax.nn.sigmoid(parts[:, 3 * LANES :])
    residual = from_owner(token_mid, 0)

    if rounds:
        learn(len(rounds) - 1)
    for k in range(1, zs):
        block_k = kv_all.at[z, x, c]
        remote(block_k, block_k, z_s, z_r, {"tok": tok_of(lax.rem(z + k, zs), x, c)}).start()

    two = pl.ds(1, 2)
    remote(weights.at[two], weights.at[two], w_s, w_r.at[0], up).wait_recv()
    r32 = iota((CHUNK, heads), 0)

    def reach_of(sender, k):
        head = y_at(k) * HL + lax.div(r32, ROWS)
        sel = mask(iota((CHUNK, heads), 1) == head).astype(BF16)
        chosen = dot(sel, weights[sender])
        return jnp.maximum(PAIR_HALF * jnp.sum(jnp.abs(chosen), axis=1, keepdims=True), 1e-20)

    step = 1.0 / CODE_MAX
    legs = []
    for kind, out, hold, src, k, to in (
        (OPP_UP, fwd_up_s, hold_up, opp_up_r, 1, FWD_UP),
        (OPP_DN, fwd_dn_s, hold_dn, opp_dn_r, 3, FWD_DN),
    ):
        theirs = reach_of(Y - k, k)
        legs.append((kind, out, hold, src, to, theirs * step, CODE_MAX / (theirs + reach_of(0, k))))
    r_up, r_dn = reach_of(1, 0), reach_of(3, 0)
    s_up, s_dn = r_up * step, r_dn * step

    early = half - sub if half > sub else half
    last_parts = [(0, early), (early, half - early)] if early < half else [(0, half)]

    def forward(g, last):
        for kind, out, hold, src, to, theirs, scale in legs:
            out[g] = coded(src[g].astype(F32) * theirs + hold[g], scale)
            if not last:
                piece(to, g).start()
        if last:
            for at, width in last_parts:
                for to in (FWD_UP, FWD_DN):
                    part_of(to, g, at, width, landed_last(to, at)).start()

    def forward_two(i, last=False):
        for kind in (OPP_UP, OPP_DN):
            pieces(kind, 2 * i, 2).wait_recv()
        forward(2 * i, False)
        forward(2 * i + 1, last)

    forward_two(0)

    if zs > 1:
        others_z = kv_all.at[pl.ds(0, zs - 1), x, c]
        remote(others_z, others_z, z_s, z_r, {"tok": tok}).wait_recv()

    def column(k):
        return kv_all.at[:, x_at(k), c]

    def send(ref, s_sem, r_sem, device):
        copy = remote(ref, ref, s_sem, r_sem, device)
        copy.start()
        return copy

    x_up, x_dn = {"tok": tok_of(z, x_at(1), c)}, {"tok": tok_of(z, x_at(xs - 1), c)}
    other = {"tok": tok_of(z, x, 1 - c)}
    send(column(0), x_s, x_r.at[0], x_up)
    if xs > 2:
        send(column(0), x_s, x_r.at[1], x_dn)
    send(column(0), c_s, c_r, other)

    forward_two(1)

    def arrived(ref, sem):
        remote(ref, ref, x_s, sem, other).wait_recv()

    arrived(column(xs - 1), x_r.at[0])
    if xs > 2:
        lower, upper = pl.ds(0, zs // 2), pl.ds(zs // 2, zs - zs // 2)
        send(kv_all.at[lower, x_at(xs - 1), c], x_s, x_r.at[2], x_up)
        arrived(column(1), x_r.at[1])
        send(kv_all.at[upper, x_at(1), c], x_s, x_r.at[2], x_dn)
        send(column(1), c_s, c_r, other)
    send(column(xs - 1), c_s, c_r, other)

    forward_two(2, True)

    if xs > 2:
        arrived(column(2), x_r.at[2])
        send(column(2), c_s, c_r, other)
    arrived(kv_all.at[:, :, 1 - c], c_r)

    rows = groups * CHUNK
    rr = iota((rows, here), 0)
    pick_row = lax.div(rr, CHUNK) * ROWS + lax.rem(rr, ROWS) == iota((rows, here), 1)
    rl = iota((rows, LANES), 0)
    of_head = mask(
        lax.div(iota((rows, LANES), 1), HEAD_SIZE) == lax.rem(lax.div(rl, ROWS), HL)
    )
    q_rows = (dot(mask(pick_row).astype(BF16), t_query) * of_head).astype(BF16)
    key_rows = kv_all[..., 0:LANES].reshape(keys, LANES)
    for at in range(0, keys, 2 * sub):
        s = dot_nt(q_rows, key_rows[at : at + 2 * sub])
        score[:, :, at : at + 2 * sub] = s.reshape(groups, CHUNK, 2 * sub)

    for kind in (DIR_UP, DIR_DN):
        pieces(kind, 0, groups).wait_recv()

    def direct(g, carry):
        for side, (ref, scale) in enumerate(((dir_dn_r, s_up), (dir_up_r, s_dn))):
            for at in range(0, half, sub):
                cols = slice(side * half + at, side * half + at + sub)
                got = ref[g, :, at : at + sub].astype(F32) * scale
                score[g, :, cols] = score[g, :, cols] + (own[g, :, cols] + got)
        return carry

    lax.fori_loop(0, groups, direct, 0)

    head_mask = of_head[0:CHUNK]

    weights_copy(2).wait_recv()
    r_opp = reach_of(2, 0)
    s_up2, s_dn2 = (r_up + r_opp) * step, (r_dn + r_opp) * step

    def attend_part(g, at_first, width, state):
        spans = []
        peak = state[0] if state else None
        for side, (ref, scale) in enumerate(((fwd_up_r, s_dn2), (fwd_dn_r, s_up2))):
            for at in range(at_first, at_first + width, sub):
                cols = slice(side * half + at, side * half + at + sub)
                s = score[g, :, cols] + ref[g, :, at : at + sub].astype(F32) * scale
                score[g, :, cols] = s
                spans.append(cols)
                high = jnp.max(s, axis=-1, keepdims=True)
                peak = high if peak is None else jnp.maximum(peak, high)
        if state:
            shrink = jnp.exp(state[0] - peak)
            norm, acc = state[1] * shrink, state[2] * shrink
        else:
            norm, acc = jnp.zeros((CHUNK, 1), F32), jnp.zeros((CHUNK, LANES), F32)
        value_rows = kv_all[..., LANES:].reshape(keys, LANES)
        for cols in spans:
            e = jnp.exp(score[g, :, cols] - peak)
            norm = norm + jnp.sum(e, axis=-1, keepdims=True)
            acc = acc + dot(e.astype(BF16), value_rows[cols])
        return peak, norm, acc

    def finish(g, state):
        acc = state[2] * head_mask / state[1]
        mixed[g] = jnp.sum(acc.reshape(HL, ROWS, LANES), axis=0)

    def attend(g, carry):
        finish(g, attend_part(g, 0, half, None))
        return carry

    for g in range(0, groups - 2, 2):
        for kind in (FWD_UP, FWD_DN):
            pieces(kind, g, 2).wait_recv()
        lax.fori_loop(g, g + 2, attend, 0)
    for kind in (FWD_UP, FWD_DN):
        piece(kind, groups - 2).wait_recv()
    attend(groups - 2, 0)
    state = None
    for at, width in last_parts:
        for kind in (FWD_UP, FWD_DN):
            part_of(kind, groups - 1, at, width, landed_last(kind, at)).wait_recv()
        state = attend_part(groups - 1, at, width, state)
    finish(groups - 1, state)

    out_rows = (mixed[...].reshape(here, LANES) * gate).astype(BF16)
    term = dot(out_rows[:, 0:columns], out_v[...])
    for k in range(1, Y):
        fin_s[k] = term[:, k * LANES : (k + 1) * LANES].astype(BF16)
    for i in range(Y - 1):
        target = i + (y <= i).astype(jnp.int32)
        k = lax.rem(target - y + Y, Y)
        remote(fin_s.at[k], fin_r.at[Y - k], fin_ss, fin_rs, {"head": target}).start()
    peers = pl.ds(1, Y - 1)
    remote(codes_s, codes_s, y_s, w_r.at[0], up).wait_send()
    remote(weights.at[peers], weights.at[peers], w_s, w_r.at[0], up).wait_send()
    if zs > 1:
        remote(others_z, others_z, z_s, z_r, other).wait_send()
    x_sent = kv_all.at[:, pl.ds(0, 3 if xs > 2 else 1), c]
    remote(x_sent, x_sent, x_s, x_r.at[0], other).wait_send()
    remote(kv_all.at[:, :, c], kv_all.at[:, :, c], c_s, c_r, other).wait_send()
    result = residual + term[:, 0:LANES]
    remote(fin_s.at[peers], fin_r.at[peers], fin_ss, fin_rs, up).wait()
    for k in range(1, Y):
        result = result + fin_r[k].astype(F32)
    token_out[...] = result[:, 0:columns].astype(BF16)


def hand_over(a, b, a_out, b_out, sems):
    copies = [
        pltpu.make_async_copy(a, a_out, sems.at[0]),
        pltpu.make_async_copy(b, b_out, sems.at[1]),
    ]
    for copy in copies:
        copy.start()
    for copy in copies:
        copy.wait()


def per_device(
    atom_single,
    atom_bias,
    atom_token,
    atom_count,
    token_single,
    pair,
    atom_qkv,
    atom_wo,
    atom_agg,
    token_qkvg,
    pair_weight,
    token_wo,
):
    devs = lax.axis_size("tok")
    xs = 4 if devs % 32 == 0 else 2
    zs = devs // (xs * CORES)
    atoms, width = atom_single.shape
    here, width_t = token_single.shape
    keys = pair.shape[2]
    groups = here // ROWS
    half = keys // 2
    columns = width_t // Y
    depth = ROWS * CH
    anywhere = pl.BlockSpec(memory_space=pl.ANY)
    vmem = pl.BlockSpec(memory_space=pltpu.VMEM)
    dma = pltpu.SemaphoreType.DMA
    code = pltpu.VMEM((groups, CHUNK, half), I16)
    operands = (
        atom_single,
        atom_bias.reshape(atoms * ATOM_HEADS, WK),
        atom_token.reshape(1, atoms),
        atom_count.reshape(1, here),
        token_single,
        pair.reshape(here * CH, keys),
        jnp.transpose(atom_qkv, (1, 0, 2)),
        atom_wo,
        atom_agg,
        token_qkvg,
        jnp.transpose(pair_weight),
        token_wo,
    )
    scratch = [
        pltpu.VMEM((atoms, width), BF16),
        pltpu.VMEM((atoms * ATOM_HEADS, WK), BF16),
        pltpu.VMEM((1, atoms), jnp.int32),
        pltpu.VMEM((1, here), jnp.int32),
        pltpu.VMEM((here, width_t), BF16),
        pltpu.VMEM((groups, depth, keys), BF16),
        pltpu.VMEM((3, width, width), BF16),
        pltpu.VMEM(atom_wo.shape, BF16),
        pltpu.VMEM(atom_agg.shape, BF16),
        pltpu.VMEM(token_qkvg.shape, BF16),
        pltpu.VMEM(token_wo.shape, BF16),
        pltpu.VMEM((atoms + 2 * RIM, 2 * width), BF16),
        pltpu.VMEM((Y, Y * HL, CH), BF16),
        pltpu.VMEM((groups, CHUNK, keys), F32),
        pltpu.VMEM((groups, CHUNK, half), F32),
        pltpu.VMEM((groups, CHUNK, half), F32),
        pltpu.VMEM((6, groups, CHUNK, half), I16),
        *([code] * 6),
        pltpu.VMEM((BLOCK_DEVS, here, width_t), BF16),
        pltpu.VMEM((BLOCK_DEVS, here, width_t), BF16),
        pltpu.VMEM((zs, xs, CORES, here, 2 * LANES), BF16),
        pltpu.VMEM((groups, CHUNK, keys), F32),
        pltpu.VMEM((groups, ROWS, LANES), F32),
        pltpu.VMEM((Y, here, LANES), BF16),
        pltpu.VMEM((Y, here, LANES), BF16),
        pltpu.VMEM((width_t, 4 * LANES), BF16),
        pltpu.VMEM((columns, Y * LANES), BF16),
        dma((11,)),
        dma((6,)),
        dma((2,)),
        dma((2,)),
        dma,
        dma((2,)),
        dma,
        dma((2, groups // 2)),
        dma((2,)),
        dma((2, groups // 2 + 2)),
        dma,
        dma,
        dma,
        dma,
        dma,
        dma((3,)),
        dma,
        dma,
        dma,
        dma,
        pltpu.SemaphoreType.REGULAR((3,)),
        pltpu.SemaphoreType.REGULAR,
        pltpu.SemaphoreType.REGULAR,
    ]
    outs = (
        pltpu.VMEM((atoms, width), BF16),
        pltpu.VMEM((here, columns), BF16),
    )
    results = pl.pallas_call(
        functools.partial(fused, zs, xs),
        out_shape=outs,
        in_specs=[anywhere] * len(operands),
        out_specs=(vmem, vmem),
        scratch_shapes=scratch,
        compiler_params=pltpu.CompilerParams(
            collective_id=0, has_side_effects=True, vmem_limit_bytes=56 * 2**20
        ),
    )(*operands)
    results = [pltpu.with_memory_space_constraint(r, pltpu.VMEM) for r in results]
    return pl.pallas_call(
        hand_over,
        out_shape=tuple(pltpu.HBM(r.shape, r.dtype) for r in results),
        in_specs=[anywhere, anywhere],
        out_specs=(anywhere, anywhere),
        scratch_shapes=[dma((2,))],
    )(*results)


def solution(mesh):
    in_specs = (
        P("tok", None),
        P("tok", None, None),
        P("tok"),
        P("tok"),
        P("tok", None),
        P("tok", "head", None),
        P(),
        P(),
        P(),
        P(),
        P("head", None),
        P("head", None),
    )
    out_specs = (P("tok", None), P("tok", "head"))
    return jax.shard_map(
        per_device, mesh=mesh, in_specs=in_specs, out_specs=out_specs, check_vma=False
    )
```

```python
import functools
import math

import jax
import jax.numpy as jnp
from jax import lax
from jax.experimental import pallas as pl
from jax.experimental.pallas import tpu as pltpu
from jax.sharding import PartitionSpec as P

ATOM_HEADS = 4
WQ = 32
WK = 128
RIM = (WK - WQ) // 2
BLOCK_DEVS = 4
HEAD_SIZE = 24
ATOM_HEAD_SIZE = 32
EPS = 1e-05

Y = 4
CORES = 2
ROWS = 8
CH = 32
HL = 4
CHUNK = HL * ROWS
LANES = 128

PAIR_MID = 9.5
PAIR_HALF = 14.5
CODE_MAX = 32700.0

F32 = jnp.float32
BF16 = jnp.bfloat16
I16 = jnp.int16
MESH = pl.DeviceIdType.MESH

OPP_UP, OPP_DN, DIR_UP, DIR_DN, FWD_UP, FWD_DN = range(6)


def iota(shape, dim):
    return lax.broadcasted_iota(jnp.int32, shape, dim)


def dot(a, b):
    return jnp.dot(a, b, preferred_element_type=F32)


def dot_nt(a, b):
    return lax.dot_general(a, b, (((1,), (1,)), ((), ())), preferred_element_type=F32)


def mask(cond):
    return jnp.where(cond, 1.0, 0.0).astype(F32)


def normalize(rows):
    mean = jnp.mean(rows, axis=-1, keepdims=True)
    centered = rows - mean
    spread = jnp.mean(centered * centered, axis=-1, keepdims=True)
    return centered * lax.rsqrt(spread + EPS)


def fused(
    zs,
    xs,
    atom_single,
    atom_bias,
    atom_token,
    atom_count,
    token_single,
    pair,
    atom_qkv,
    atom_wo,
    atom_agg,
    token_qkvg,
    pair_weight,
    token_wo,
    atom_out,
    token_out,
    single_v,
    bias_v,
    name_v,
    count_v,
    tok_v,
    pair_v,
    aqkv_v,
    awo_v,
    agg_v,
    qkvg_v,
    two_v,
    kv_pad,
    weights,
    own,
    hold_up,
    hold_dn,
    codes_s,
    opp_up_r,
    opp_dn_r,
    dir_up_r,
    dir_dn_r,
    fwd_up_r,
    fwd_dn_r,
    sum_s,
    sum_r,
    kv_all,
    score,
    mixed,
    fin_s,
    fin_r,
    proj_v,
    out_v,
    in_sem,
    pair_sem,
    halo_s,
    halo_r,
    w_s,
    w_r,
    y_s,
    opp_r,
    dir_r,
    fwd_r,
    sum_ss,
    sum_rs,
    z_s,
    z_r,
    x_s,
    x_r,
    c_s,
    c_r,
    fin_ss,
    fin_rs,
    known,
    near,
    opposite,
):
    tok = lax.axis_index("tok")
    y = lax.axis_index("head")
    devs = zs * xs * CORES
    z = lax.div(tok, xs * CORES)
    x = lax.rem(lax.div(tok, CORES), xs)
    c = lax.rem(tok, CORES)
    place = lax.rem(tok, BLOCK_DEVS)
    groups, depth, keys = pair_v.shape
    half = keys // 2
    here = tok_v.shape[0]
    atoms = single_v.shape[0]
    windows = atoms // WQ
    sub = half // 3 if half % 3 == 0 else half
    columns = HL * HEAD_SIZE
    paired = groups // 2

    def tok_of(z_, x_, c_):
        return (z_ * xs + x_) * CORES + c_

    def y_at(k):
        return lax.rem(y + k, Y)

    def x_at(k):
        return lax.rem(x + k, xs)

    def mate(k):
        return tok - place + lax.rem(place + k, BLOCK_DEVS)

    up, dn = {"head": y_at(1)}, {"head": y_at(3)}

    def remote(src, dst, send, recv, device):
        return pltpu.make_async_remote_copy(
            src_ref=src,
            dst_ref=dst,
            send_sem=send,
            recv_sem=recv,
            device_id=device,
            device_id_type=MESH,
        )

    def signal(sem, device):
        pl.semaphore_signal(sem, inc=1, device_id=device, device_id_type=MESH)

    barrier = pltpu.get_barrier_semaphore()
    for device in (up, dn):
        signal(barrier, device)

    opp_up_s, opp_dn_s, dir_up_s, dir_dn_s, fwd_up_s, fwd_dn_s = (codes_s.at[i] for i in range(6))

    loads = [
        (pair_weight, weights.at[0]),
        (atom_single, single_v),
        (atom_qkv, aqkv_v),
        (atom_bias, bias_v),
        (atom_wo, awo_v),
        (atom_agg, agg_v),
        (atom_token, name_v),
        (atom_count, count_v),
        (token_qkvg, qkvg_v),
        (token_single, tok_v),
        (token_wo, two_v),
    ]
    loads = [pltpu.make_async_copy(a, b, in_sem.at[i]) for i, (a, b) in enumerate(loads)]

    def pair_load(g):
        return pltpu.make_async_copy(
            pair.at[pl.ds(pl.multiple_of(g * depth, depth), depth), :],
            pair_v.at[g],
            pair_sem.at[5 if g == 1 else g // 2],
        )

    head_loads = [
        pltpu.make_async_copy(
            pair.at[pl.ds(0, depth), pl.ds(at, width)],
            pair_v.at[0, :, pl.ds(at, width)],
            pair_sem.at[sem],
        )
        for at, width, sem in ((0, sub, 0), (sub, half - sub, 3), (half, half, 4))
        if width
    ]
    loads[0].start()
    for load in head_loads:
        load.start()
    loads[1].start()
    loads[2].start()

    first_core = c == 0
    edges = []
    for k in range(1, BLOCK_DEVS):
        same = lax.div(place, CORES) == lax.div(lax.rem(place + k, BLOCK_DEVS), CORES)
        edges.append((None, jnp.where(same, first_core, place + k >= BLOCK_DEVS), mate(k)))
    for k in sorted({1, xs - 1}):
        edges.append((None, x + k >= xs, tok_of(z, x_at(k), c)))
    edges.append((None, first_core, tok_of(z, x, 1 - c)))
    edges.append((tok > 0, first_core, tok - 1))
    edges.append((tok < devs - 1, first_core, tok + 1))
    edges.append((z > 0, True, tok - xs * CORES))
    edges.append((z < zs - 1, False, tok + xs * CORES))

    def both(a, b):
        return b if a is None else a if b is True else jnp.logical_and(a, b)

    waited, waiting, expected, back = [], [], 2, 0
    for there, waits, other in edges:
        if waits is not False:
            waited.append((both(there, waits), other))
            expected = expected + waited[-1][0].astype(jnp.int32)
        if waits is not True:
            waiting.append((both(there, True if waits is False else jnp.logical_not(waits)), other))
            back = back + waiting[-1][0].astype(jnp.int32)

    def signal_all(sem, group):
        for there, other in group:

            @pl.when(there)
            def _():
                signal(sem, {"tok": other})

    signal_all(barrier, waiting)

    heads = weights.shape[1]
    row = iota((Y * CHUNK, heads), 0)
    owner = lax.rem(y + lax.div(row, CHUNK), Y)
    pick = iota((Y * CHUNK, heads), 1) == owner * HL + lax.rem(lax.div(row, ROWS), HL)
    pick = mask(pick).astype(BF16)
    diag = lax.div(iota((Y * CHUNK, depth), 1), CH) == lax.rem(iota((Y * CHUNK, depth), 0), ROWS)
    diag = mask(diag)
    loads[0].wait()
    tiled = jnp.concatenate([weights[0]] * ROWS, axis=1)
    picked_f = dot(pick, tiled)
    lhs = (picked_f * diag).astype(BF16)
    picked_f = picked_f[:, 0:CH]
    mid = PAIR_MID * jnp.sum(picked_f, axis=1, keepdims=True)
    reach = jnp.maximum(PAIR_HALF * jnp.sum(jnp.abs(picked_f), axis=1, keepdims=True), 1e-20)
    inv = CODE_MAX / reach

    buffers = {
        OPP_UP: (opp_up_s, opp_up_r, up),
        OPP_DN: (opp_dn_s, opp_dn_r, dn),
        DIR_UP: (dir_up_s, dir_up_r, up),
        DIR_DN: (dir_dn_s, dir_dn_r, dn),
        FWD_UP: (fwd_up_s, fwd_up_r, up),
        FWD_DN: (fwd_dn_s, fwd_dn_r, dn),
    }

    def landed(kind, g):
        if kind in (OPP_UP, OPP_DN):
            return opp_r.at[kind - OPP_UP, lax.div(g, 2)]
        if kind in (DIR_UP, DIR_DN):
            return dir_r.at[kind - DIR_UP]
        return fwd_r.at[kind - FWD_UP, jnp.maximum(lax.div(g, 2), g - (groups - 1) + paired)]

    def landed_last(kind, at):
        return fwd_r.at[kind - FWD_UP, paired + (1 if at else 0)]

    def piece(kind, g):
        src, dst, device = buffers[kind]
        return remote(src.at[g], dst.at[g], y_s, landed(kind, g), device)

    def part_of(kind, g, at, width, sem):
        src, dst, device = buffers[kind]
        cols = pl.ds(at, width)
        return remote(src.at[g, :, cols], dst.at[g, :, cols], y_s, sem, device)

    def pieces(kind, g, n):
        src, dst, device = buffers[kind]
        some = pl.ds(g, n)
        return remote(src.at[some], dst.at[some], y_s, landed(kind, g), device)

    def coded(value, scale):
        return jnp.round(value * scale).astype(jnp.int32).astype(I16)

    def produce(g, sides, ats):
        for side in sides:
            for at in ats:
                cols = slice(side * half + at, side * half + at + sub)
                into = slice(at, at + sub)
                part = dot(lhs, pair_v[g, :, cols])
                own[g, :, cols] = part[0:CHUNK]
                part = part[CHUNK:] - mid[CHUNK:]
                to_up, to_opp, to_dn = (part[i * CHUNK : (i + 1) * CHUNK] for i in range(3))
                i_up, i_opp, i_dn = (inv[i * CHUNK : (i + 1) * CHUNK] for i in range(1, Y))
                if side == 0:
                    opp_up_s[g, :, into] = coded(to_opp, i_opp)
                    hold_up[g, :, into] = to_up
                    dir_dn_s[g, :, into] = coded(to_dn, i_dn)
                else:
                    opp_dn_s[g, :, into] = coded(to_opp, i_opp)
                    hold_dn[g, :, into] = to_dn
                    dir_up_s[g, :, into] = coded(to_up, i_up)

    ats = tuple(range(0, half, sub))
    head_loads[0].wait()
    for g in range(1, groups):
        pair_load(g).start()
    for load in loads[3:]:
        load.start()
    produce(0, (0,), ats[:1])

    pl.semaphore_wait(barrier, expected)

    def weights_copy(k):
        to = {"head": y_at(k)}
        return remote(weights.at[0], weights.at[Y - k], w_s, w_r.at[1 if k == 2 else 0], to)

    for side in range(2):
        for at in ats:
            if side or at:
                if at == ats[1 - side]:
                    head_loads[1 + side].wait()
                produce(0, (side,), (at,))
            for kind in (OPP_DN, DIR_UP) if side else (OPP_UP, DIR_DN):
                part_of(kind, 0, at, sub, landed(kind, 0)).start()
    weights_copy(1).start()
    weights_copy(3).start()
    signal(opposite, up)
    signal_all(near, waited)

    rounds = [d for d in (1, 2, 4) if d < zs]

    def tell(r):
        for present, other in (
            (z >= rounds[r], tok - rounds[r] * xs * CORES),
            (z < zs - rounds[r], tok + rounds[r] * xs * CORES),
        ):

            @pl.when(present)
            def _():
                signal(known.at[r], {"tok": other})

    def learn(r):
        amount = (z >= rounds[r]).astype(jnp.int32) + (z < zs - rounds[r]).astype(jnp.int32)
        pl.semaphore_wait(known.at[r], amount)

    loads[1].wait()
    loads[2].wait()
    single = single_v[...].astype(F32)
    normed = normalize(single).astype(BF16)
    query = (dot(normed, aqkv_v[0]) * (1.0 / math.sqrt(ATOM_HEAD_SIZE))).astype(BF16)
    kv_pad[RIM : RIM + atoms, 0:LANES] = dot(normed, aqkv_v[1]).astype(BF16)
    kv_pad[RIM : RIM + atoms, LANES:] = dot(normed, aqkv_v[2]).astype(BF16)
    halo_up = remote(
        kv_pad.at[pl.ds(atoms, RIM), :],
        kv_pad.at[pl.ds(0, RIM), :],
        halo_s.at[0],
        halo_r.at[0],
        {"tok": lax.rem(tok + 1, devs)},
    )
    halo_dn = remote(
        kv_pad.at[pl.ds(RIM, RIM), :],
        kv_pad.at[pl.ds(atoms + RIM, RIM), :],
        halo_s.at[1],
        halo_r.at[1],
        {"tok": lax.rem(tok + devs - 1, devs)},
    )

    def rest(g, carry):
        produce(g, (0, 1), ats)
        for kind in (OPP_UP, OPP_DN, DIR_UP, DIR_DN):
            piece(kind, g).start()
        return carry

    pair_load(1).wait()
    rest(1, 0)
    for g in range(2, groups, 2):
        two_groups = pair_v.at[pl.ds(g, 2)]
        pltpu.make_async_copy(two_groups, two_groups, pair_sem.at[g // 2]).wait()
        lax.fori_loop(g, g + 2, rest, 0)

    @pl.when(back > 0)
    def _():
        pl.semaphore_wait(near, back)

    pl.semaphore_wait(opposite, 1)
    weights_copy(2).start()
    if len(rounds) > 0:
        tell(0)
    first, last = tok == 0, tok == devs - 1

    @pl.when(jnp.logical_not(last))
    def _():
        halo_up.start()

    @pl.when(jnp.logical_not(first))
    def _():
        halo_dn.start()

    def from_owner(value, k):
        shift = lax.rem((2 * Y - y - k) * columns, Y * columns)
        return pltpu.roll(value, shift, 1)[:, 0:LANES]

    for load in loads[4:]:
        load.wait()
    for i in range(4):
        proj_v[:, i * LANES : (i + 1) * LANES] = from_owner(
            qkvg_v[:, i, :].astype(F32), 0
        ).astype(BF16)
    for k in range(Y):
        out_v[:, k * LANES : (k + 1) * LANES] = from_owner(two_v[...].astype(F32), k).astype(BF16)
    if len(rounds) > 1:
        learn(0)
        tell(1)

    @pl.when(first)
    def _():
        kv_pad[0:RIM, :] = jnp.zeros((RIM, 2 * LANES), BF16)

    @pl.when(jnp.logical_not(first))
    def _():
        halo_up.wait_recv()
        halo_dn.wait_send()

    @pl.when(last)
    def _():
        kv_pad[atoms + RIM : atoms + 2 * RIM, :] = jnp.zeros((RIM, 2 * LANES), BF16)

    @pl.when(jnp.logical_not(last))
    def _():
        halo_dn.wait_recv()
        halo_up.wait_send()

    loads[3].wait()
    wide = WQ * ATOM_HEADS
    grow = mask(lax.div(iota((wide, WQ), 0), ATOM_HEADS) == iota((wide, WQ), 1)).astype(BF16)
    fold = mask(iota((WQ, wide), 0) == lax.div(iota((WQ, wide), 1), ATOM_HEADS)).astype(BF16)
    in_head = mask(
        lax.div(iota((wide, LANES), 1), ATOM_HEAD_SIZE) == lax.rem(iota((wide, LANES), 0), ATOM_HEADS)
    )
    slot = iota((wide, WK), 1)
    scores = []
    for w in range(windows):
        q_rows = (dot(grow, query[w * WQ : (w + 1) * WQ]) * in_head).astype(BF16)
        s = dot_nt(q_rows, kv_pad[w * WQ : w * WQ + WK, 0:LANES])
        s = s + bias_v[w * wide : (w + 1) * wide, :].astype(F32)
        if w * WQ < RIM or w * WQ + WK > RIM + atoms:
            spot = tok * atoms + w * WQ - RIM + slot
            s = jnp.where((spot >= 0) & (spot < devs * atoms), s, -1e30)
        scores.append(s)
    probs = []
    for s in scores:
        e = jnp.exp(s - jnp.max(s, axis=-1, keepdims=True))
        probs.append((e * (1.0 / jnp.sum(e, axis=-1, keepdims=True))).astype(BF16))
    mixes = []
    for w in range(windows):
        m = dot(probs[w], kv_pad[w * WQ : w * WQ + WK, LANES:])
        mixes.append(dot(fold, (m * in_head).astype(BF16)).astype(BF16))
    mix = jnp.concatenate(mixes, axis=0)
    a_out = (single + dot(mix, awo_v[...])).astype(BF16)
    atom_out[...] = a_out
    feat = jnp.maximum(dot(a_out, agg_v[...]), 0.0).astype(BF16)

    block = iota((BLOCK_DEVS * here, 1), 0)
    owner_tok = mate(lax.div(block, here)) * here + lax.rem(block, here)
    onehot = mask(owner_tok == name_v[...]).astype(BF16)
    sums = dot(onehot, feat)
    for k in range(1, BLOCK_DEVS):
        sum_s[k] = sums[k * here : (k + 1) * here].astype(BF16)
        remote(
            sum_s.at[k], sum_r.at[BLOCK_DEVS - k], sum_ss, sum_rs, {"tok": mate(k)}
        ).start()
    if len(rounds) > 2:
        learn(1)
        tell(2)

    others = pl.ds(1, BLOCK_DEVS - 1)
    remote(sum_s.at[others], sum_r.at[others], sum_ss, sum_rs, up).wait()
    total = sums[0:here]
    for k in range(1, BLOCK_DEVS):
        total = total + sum_r[k].astype(F32)
    square = iota((here, here), 0) == iota((here, here), 1)
    count = jnp.sum(jnp.where(square, count_v[...].astype(F32), 0.0), axis=1, keepdims=True)
    token_mid = tok_v[...].astype(F32) + total / count
    normed_t = normalize(token_mid).astype(BF16)
    parts = dot(normed_t, proj_v[...])
    t_query = (parts[:, 0:LANES] * (1.0 / math.sqrt(HEAD_SIZE))).astype(BF16)
    kv_all[z, x, c] = parts[:, LANES : 3 * LANES].astype(BF16)
    gate = jax.nn.sigmoid(parts[:, 3 * LANES :])
    residual = from_owner(token_mid, 0)

    if rounds:
        learn(len(rounds) - 1)
    for k in range(1, zs):
        block_k = kv_all.at[z, x, c]
        remote(block_k, block_k, z_s, z_r, {"tok": tok_of(lax.rem(z + k, zs), x, c)}).start()

    two = pl.ds(1, 2)
    remote(weights.at[two], weights.at[two], w_s, w_r.at[0], up).wait_recv()
    r32 = iota((CHUNK, heads), 0)

    def reach_of(sender, k):
        head = y_at(k) * HL + lax.div(r32, ROWS)
        sel = mask(iota((CHUNK, heads), 1) == head).astype(BF16)
        chosen = dot(sel, weights[sender])
        return jnp.maximum(PAIR_HALF * jnp.sum(jnp.abs(chosen), axis=1, keepdims=True), 1e-20)

    step = 1.0 / CODE_MAX
    legs = []
    for kind, out, hold, src, k, to in (
        (OPP_UP, fwd_up_s, hold_up, opp_up_r, 1, FWD_UP),
        (OPP_DN, fwd_dn_s, hold_dn, opp_dn_r, 3, FWD_DN),
    ):
        theirs = reach_of(Y - k, k)
        legs.append((kind, out, hold, src, to, theirs * step, CODE_MAX / (theirs + reach_of(0, k))))
    r_up, r_dn = reach_of(1, 0), reach_of(3, 0)
    s_up, s_dn = r_up * step, r_dn * step

    early = half - sub if half > sub else half
    last_parts = [(0, early), (early, half - early)] if early < half else [(0, half)]

    def forward(g, last):
        for kind, out, hold, src, to, theirs, scale in legs:
            out[g] = coded(src[g].astype(F32) * theirs + hold[g], scale)
            if not last:
                piece(to, g).start()
        if last:
            for at, width in last_parts:
                for to in (FWD_UP, FWD_DN):
                    part_of(to, g, at, width, landed_last(to, at)).start()

    def forward_two(i, last=False):
        for kind in (OPP_UP, OPP_DN):
            pieces(kind, 2 * i, 2).wait_recv()
        forward(2 * i, False)
        forward(2 * i + 1, last)

    forward_two(0)

    if zs > 1:
        others_z = kv_all.at[pl.ds(0, zs - 1), x, c]
        remote(others_z, others_z, z_s, z_r, {"tok": tok}).wait_recv()

    def column(k):
        return kv_all.at[:, x_at(k), c]

    def send(ref, s_sem, r_sem, device):
        copy = remote(ref, ref, s_sem, r_sem, device)
        copy.start()
        return copy

    x_up, x_dn = {"tok": tok_of(z, x_at(1), c)}, {"tok": tok_of(z, x_at(xs - 1), c)}
    other = {"tok": tok_of(z, x, 1 - c)}
    send(column(0), x_s, x_r.at[0], x_up)
    if xs > 2:
        send(column(0), x_s, x_r.at[1], x_dn)
    send(column(0), c_s, c_r, other)

    forward_two(1)

    def arrived(ref, sem):
        remote(ref, ref, x_s, sem, other).wait_recv()

    arrived(column(xs - 1), x_r.at[0])
    if xs > 2:
        lower, upper = pl.ds(0, zs // 2), pl.ds(zs // 2, zs - zs // 2)
        send(kv_all.at[lower, x_at(xs - 1), c], x_s, x_r.at[2], x_up)
        arrived(column(1), x_r.at[1])
        send(kv_all.at[upper, x_at(1), c], x_s, x_r.at[2], x_dn)
        send(column(1), c_s, c_r, other)
    send(column(xs - 1), c_s, c_r, other)

    forward_two(2, True)

    if xs > 2:
        arrived(column(2), x_r.at[2])
        send(column(2), c_s, c_r, other)
    arrived(kv_all.at[:, :, 1 - c], c_r)

    rows = groups * CHUNK
    rr = iota((rows, here), 0)
    pick_row = lax.div(rr, CHUNK) * ROWS + lax.rem(rr, ROWS) == iota((rows, here), 1)
    rl = iota((rows, LANES), 0)
    of_head = mask(
        lax.div(iota((rows, LANES), 1), HEAD_SIZE) == lax.rem(lax.div(rl, ROWS), HL)
    )
    q_rows = (dot(mask(pick_row).astype(BF16), t_query) * of_head).astype(BF16)
    key_rows = kv_all[..., 0:LANES].reshape(keys, LANES)
    for at in range(0, keys, 2 * sub):
        s = dot_nt(q_rows, key_rows[at : at + 2 * sub])
        score[:, :, at : at + 2 * sub] = s.reshape(groups, CHUNK, 2 * sub)

    for kind in (DIR_UP, DIR_DN):
        pieces(kind, 0, groups).wait_recv()

    def direct(g, carry):
        for side, (ref, scale) in enumerate(((dir_dn_r, s_up), (dir_up_r, s_dn))):
            for at in range(0, half, sub):
                cols = slice(side * half + at, side * half + at + sub)
                got = ref[g, :, at : at + sub].astype(F32) * scale
                score[g, :, cols] = score[g, :, cols] + (own[g, :, cols] + got)
        return carry

    lax.fori_loop(0, groups, direct, 0)

    head_mask = of_head[0:CHUNK]

    weights_copy(2).wait_recv()
    r_opp = reach_of(2, 0)
    s_up2, s_dn2 = (r_up + r_opp) * step, (r_dn + r_opp) * step

    def attend_part(g, at_first, width, state):
        spans = []
        peak = state[0] if state else None
        for side, (ref, scale) in enumerate(((fwd_up_r, s_dn2), (fwd_dn_r, s_up2))):
            for at in range(at_first, at_first + width, sub):
                cols = slice(side * half + at, side * half + at + sub)
                s = score[g, :, cols] + ref[g, :, at : at + sub].astype(F32) * scale
                score[g, :, cols] = s
                spans.append(cols)
                high = jnp.max(s, axis=-1, keepdims=True)
                peak = high if peak is None else jnp.maximum(peak, high)
        if state:
            shrink = jnp.exp(state[0] - peak)
            norm, acc = state[1] * shrink, state[2] * shrink
        else:
            norm, acc = jnp.zeros((CHUNK, 1), F32), jnp.zeros((CHUNK, LANES), F32)
        value_rows = kv_all[..., LANES:].reshape(keys, LANES)
        for cols in spans:
            e = jnp.exp(score[g, :, cols] - peak)
            norm = norm + jnp.sum(e, axis=-1, keepdims=True)
            acc = acc + dot(e.astype(BF16), value_rows[cols])
        return peak, norm, acc

    def finish(g, state):
        acc = state[2] * head_mask / state[1]
        mixed[g] = jnp.sum(acc.reshape(HL, ROWS, LANES), axis=0)

    def attend(g, carry):
        finish(g, attend_part(g, 0, half, None))
        return carry

    cut = (groups - 2) * ROWS
    out_parts = [(0, cut), (cut, here - cut)]

    def hand_out(i):
        at, n = out_parts[i]
        mix_rows = mixed[at // ROWS : (at + n) // ROWS].reshape(n, LANES)
        out_rows = (mix_rows * gate[at : at + n]).astype(BF16)
        term = dot(out_rows[:, 0:columns], out_v[...])
        for k in range(1, Y):
            fin_s[k, at : at + n] = term[:, k * LANES : (k + 1) * LANES].astype(BF16)
        for j in range(Y - 1):
            target = j + (y <= j).astype(jnp.int32)
            k = lax.rem(target - y + Y, Y)
            some = pl.ds(at, n)
            remote(
                fin_s.at[k, some],
                fin_r.at[Y - k, some],
                fin_ss.at[i],
                fin_rs.at[i],
                {"head": target},
            ).start()
        return residual[at : at + n] + term[:, 0:LANES]

    def take_in(i, result):
        at, n = out_parts[i]
        part = fin_r.at[pl.ds(1, Y - 1), pl.ds(at, n)]
        sent = fin_s.at[pl.ds(1, Y - 1), pl.ds(at, n)]
        remote(sent, part, fin_ss.at[i], fin_rs.at[i], up).wait()
        for k in range(1, Y):
            result = result + fin_r[k, at : at + n].astype(F32)
        token_out[at : at + n] = result[:, 0:columns].astype(BF16)

    for g in range(0, groups - 2, 2):
        for kind in (FWD_UP, FWD_DN):
            pieces(kind, g, 2).wait_recv()
        lax.fori_loop(g, g + 2, attend, 0)
    early_rows = hand_out(0)
    for kind in (FWD_UP, FWD_DN):
        piece(kind, groups - 2).wait_recv()
    attend(groups - 2, 0)
    state = None
    for at, width in last_parts:
        for kind in (FWD_UP, FWD_DN):
            part_of(kind, groups - 1, at, width, landed_last(kind, at)).wait_recv()
        state = attend_part(groups - 1, at, width, state)
    finish(groups - 1, state)

    late_rows = hand_out(1)
    peers = pl.ds(1, Y - 1)
    remote(codes_s, codes_s, y_s, w_r.at[0], up).wait_send()
    remote(weights.at[peers], weights.at[peers], w_s, w_r.at[0], up).wait_send()
    if zs > 1:
        remote(others_z, others_z, z_s, z_r, other).wait_send()
    x_sent = kv_all.at[:, pl.ds(0, 3 if xs > 2 else 1), c]
    remote(x_sent, x_sent, x_s, x_r.at[0], other).wait_send()
    remote(kv_all.at[:, :, c], kv_all.at[:, :, c], c_s, c_r, other).wait_send()
    take_in(0, early_rows)
    take_in(1, late_rows)


def hand_over(a, b, a_out, b_out, sems):
    copies = [
        pltpu.make_async_copy(a, a_out, sems.at[0]),
        pltpu.make_async_copy(b, b_out, sems.at[1]),
    ]
    for copy in copies:
        copy.start()
    for copy in copies:
        copy.wait()


def per_device(
    atom_single,
    atom_bias,
    atom_token,
    atom_count,
    token_single,
    pair,
    atom_qkv,
    atom_wo,
    atom_agg,
    token_qkvg,
    pair_weight,
    token_wo,
):
    devs = lax.axis_size("tok")
    xs = 4 if devs % 32 == 0 else 2
    zs = devs // (xs * CORES)
    atoms, width = atom_single.shape
    here, width_t = token_single.shape
    keys = pair.shape[2]
    groups = here // ROWS
    half = keys // 2
    columns = width_t // Y
    depth = ROWS * CH
    anywhere = pl.BlockSpec(memory_space=pl.ANY)
    vmem = pl.BlockSpec(memory_space=pltpu.VMEM)
    dma = pltpu.SemaphoreType.DMA
    code = pltpu.VMEM((groups, CHUNK, half), I16)
    operands = (
        atom_single,
        atom_bias.reshape(atoms * ATOM_HEADS, WK),
        atom_token.reshape(1, atoms),
        atom_count.reshape(1, here),
        token_single,
        pair.reshape(here * CH, keys),
        jnp.transpose(atom_qkv, (1, 0, 2)),
        atom_wo,
        atom_agg,
        token_qkvg,
        jnp.transpose(pair_weight),
        token_wo,
    )
    scratch = [
        pltpu.VMEM((atoms, width), BF16),
        pltpu.VMEM((atoms * ATOM_HEADS, WK), BF16),
        pltpu.VMEM((1, atoms), jnp.int32),
        pltpu.VMEM((1, here), jnp.int32),
        pltpu.VMEM((here, width_t), BF16),
        pltpu.VMEM((groups, depth, keys), BF16),
        pltpu.VMEM((3, width, width), BF16),
        pltpu.VMEM(atom_wo.shape, BF16),
        pltpu.VMEM(atom_agg.shape, BF16),
        pltpu.VMEM(token_qkvg.shape, BF16),
        pltpu.VMEM(token_wo.shape, BF16),
        pltpu.VMEM((atoms + 2 * RIM, 2 * width), BF16),
        pltpu.VMEM((Y, Y * HL, CH), BF16),
        pltpu.VMEM((groups, CHUNK, keys), F32),
        pltpu.VMEM((groups, CHUNK, half), F32),
        pltpu.VMEM((groups, CHUNK, half), F32),
        pltpu.VMEM((6, groups, CHUNK, half), I16),
        *([code] * 6),
        pltpu.VMEM((BLOCK_DEVS, here, width_t), BF16),
        pltpu.VMEM((BLOCK_DEVS, here, width_t), BF16),
        pltpu.VMEM((zs, xs, CORES, here, 2 * LANES), BF16),
        pltpu.VMEM((groups, CHUNK, keys), F32),
        pltpu.VMEM((groups, ROWS, LANES), F32),
        pltpu.VMEM((Y, here, LANES), BF16),
        pltpu.VMEM((Y, here, LANES), BF16),
        pltpu.VMEM((width_t, 4 * LANES), BF16),
        pltpu.VMEM((columns, Y * LANES), BF16),
        dma((11,)),
        dma((6,)),
        dma((2,)),
        dma((2,)),
        dma,
        dma((2,)),
        dma,
        dma((2, groups // 2)),
        dma((2,)),
        dma((2, groups // 2 + 2)),
        dma,
        dma,
        dma,
        dma,
        dma,
        dma((3,)),
        dma,
        dma,
        dma((2,)),
        dma((2,)),
        pltpu.SemaphoreType.REGULAR((3,)),
        pltpu.SemaphoreType.REGULAR,
        pltpu.SemaphoreType.REGULAR,
    ]
    outs = (
        pltpu.VMEM((atoms, width), BF16),
        pltpu.VMEM((here, columns), BF16),
    )
    results = pl.pallas_call(
        functools.partial(fused, zs, xs),
        out_shape=outs,
        in_specs=[anywhere] * len(operands),
        out_specs=(vmem, vmem),
        scratch_shapes=scratch,
        compiler_params=pltpu.CompilerParams(
            collective_id=0, has_side_effects=True, vmem_limit_bytes=56 * 2**20
        ),
    )(*operands)
    results = [pltpu.with_memory_space_constraint(r, pltpu.VMEM) for r in results]
    return pl.pallas_call(
        hand_over,
        out_shape=tuple(pltpu.HBM(r.shape, r.dtype) for r in results),
        in_specs=[anywhere, anywhere],
        out_specs=(anywhere, anywhere),
        scratch_shapes=[dma((2,))],
    )(*results)


def solution(mesh):
    in_specs = (
        P("tok", None),
        P("tok", None, None),
        P("tok"),
        P("tok"),
        P("tok", None),
        P("tok", "head", None),
        P(),
        P(),
        P(),
        P(),
        P("head", None),
        P("head", None),
    )
    out_specs = (P("tok", None), P("tok", "head"))
    return jax.shard_map(
        per_device, mesh=mesh, in_specs=in_specs, out_specs=out_specs, check_vma=False
    )
```

```python
import functools
import math

import jax
import jax.numpy as jnp
from jax import lax
from jax.experimental import pallas as pl
from jax.experimental.pallas import tpu as pltpu
from jax.sharding import PartitionSpec as P

ATOM_HEADS = 4
WQ = 32
WK = 128
RIM = (WK - WQ) // 2
BLOCK_DEVS = 4
HEAD_SIZE = 24
ATOM_HEAD_SIZE = 32
EPS = 1e-05

Y = 4
CORES = 2
ROWS = 8
CH = 32
HL = 4
CHUNK = HL * ROWS
LANES = 128

PAIR_MID = 9.5
PAIR_HALF = 14.5
CODE_MAX = 32700.0

F32 = jnp.float32
BF16 = jnp.bfloat16
I16 = jnp.int16
MESH = pl.DeviceIdType.MESH

OPP_UP, OPP_DN, DIR_UP, DIR_DN, FWD_UP, FWD_DN = range(6)


def iota(shape, dim):
    return lax.broadcasted_iota(jnp.int32, shape, dim)


def dot(a, b):
    return jnp.dot(a, b, preferred_element_type=F32)


def dot_nt(a, b):
    return lax.dot_general(a, b, (((1,), (1,)), ((), ())), preferred_element_type=F32)


def mask(cond):
    return jnp.where(cond, 1.0, 0.0).astype(F32)


def normalize(rows):
    mean = jnp.mean(rows, axis=-1, keepdims=True)
    centered = rows - mean
    spread = jnp.mean(centered * centered, axis=-1, keepdims=True)
    return centered * lax.rsqrt(spread + EPS)


def fused(
    zs,
    xs,
    atom_single,
    atom_bias,
    atom_token,
    atom_count,
    token_single,
    pair,
    atom_qkv,
    atom_wo,
    atom_agg,
    token_qkvg,
    pair_weight,
    token_wo,
    atom_out,
    token_out,
    single_v,
    bias_v,
    name_v,
    count_v,
    tok_v,
    pair_v,
    aqkv_v,
    awo_v,
    agg_v,
    qkvg_v,
    two_v,
    kv_pad,
    weights,
    own,
    hold_up,
    hold_dn,
    codes_s,
    opp_up_r,
    opp_dn_r,
    dir_up_r,
    dir_dn_r,
    fwd_up_r,
    fwd_dn_r,
    sum_s,
    sum_r,
    kv_all,
    score,
    mixed,
    fin_s,
    fin_r,
    proj_v,
    out_v,
    in_sem,
    pair_sem,
    halo_s,
    halo_r,
    w_s,
    w_r,
    y_s,
    opp_r,
    dir_r,
    fwd_r,
    sum_ss,
    sum_rs,
    z_s,
    z_r,
    x_s,
    x_r,
    c_s,
    c_r,
    fin_ss,
    fin_rs,
    known,
    near,
    opposite,
):
    tok = lax.axis_index("tok")
    y = lax.axis_index("head")
    devs = zs * xs * CORES
    z = lax.div(tok, xs * CORES)
    x = lax.rem(lax.div(tok, CORES), xs)
    c = lax.rem(tok, CORES)
    place = lax.rem(tok, BLOCK_DEVS)
    groups, depth, keys = pair_v.shape
    half = keys // 2
    here = tok_v.shape[0]
    atoms = single_v.shape[0]
    windows = atoms // WQ
    sub = half // 3 if half % 3 == 0 else half
    columns = HL * HEAD_SIZE
    paired = groups // 2

    def tok_of(z_, x_, c_):
        return (z_ * xs + x_) * CORES + c_

    def y_at(k):
        return lax.rem(y + k, Y)

    def x_at(k):
        return lax.rem(x + k, xs)

    def mate(k):
        return tok - place + lax.rem(place + k, BLOCK_DEVS)

    up, dn = {"head": y_at(1)}, {"head": y_at(3)}

    def remote(src, dst, send, recv, device):
        return pltpu.make_async_remote_copy(
            src_ref=src,
            dst_ref=dst,
            send_sem=send,
            recv_sem=recv,
            device_id=device,
            device_id_type=MESH,
        )

    def signal(sem, device):
        pl.semaphore_signal(sem, inc=1, device_id=device, device_id_type=MESH)

    barrier = pltpu.get_barrier_semaphore()
    for device in (up, dn):
        signal(barrier, device)

    opp_up_s, opp_dn_s, dir_up_s, dir_dn_s, fwd_up_s, fwd_dn_s = (codes_s.at[i] for i in range(6))

    loads = [
        (pair_weight, weights.at[0]),
        (atom_single, single_v),
        (atom_qkv, aqkv_v),
        (atom_bias, bias_v),
        (atom_wo, awo_v),
        (atom_agg, agg_v),
        (atom_token, name_v),
        (atom_count, count_v),
        (token_qkvg, qkvg_v),
        (token_single, tok_v),
        (token_wo, two_v),
    ]
    loads = [pltpu.make_async_copy(a, b, in_sem.at[i]) for i, (a, b) in enumerate(loads)]

    def pair_load(g):
        return pltpu.make_async_copy(
            pair.at[pl.ds(pl.multiple_of(g * depth, depth), depth), :],
            pair_v.at[g],
            pair_sem.at[5 if g == 1 else g // 2],
        )

    head_loads = [
        pltpu.make_async_copy(
            pair.at[pl.ds(0, depth), pl.ds(at, width)],
            pair_v.at[0, :, pl.ds(at, width)],
            pair_sem.at[sem],
        )
        for at, width, sem in ((0, sub, 0), (sub, half - sub, 3), (half, half, 4))
        if width
    ]
    loads[0].start()
    for load in head_loads:
        load.start()
    loads[1].start()
    loads[2].start()

    def other_loads():
        for g in range(1, groups):
            pair_load(g).start()
        for load in loads[3:]:
            load.start()

    pl.when(y < Y // 2)(other_loads)

    first_core = c == 0
    edges = []
    for k in range(1, BLOCK_DEVS):
        same = lax.div(place, CORES) == lax.div(lax.rem(place + k, BLOCK_DEVS), CORES)
        edges.append((None, jnp.where(same, first_core, place + k >= BLOCK_DEVS), mate(k)))
    for k in sorted({1, xs - 1}):
        edges.append((None, x + k >= xs, tok_of(z, x_at(k), c)))
    edges.append((None, first_core, tok_of(z, x, 1 - c)))
    edges.append((tok > 0, first_core, tok - 1))
    edges.append((tok < devs - 1, first_core, tok + 1))
    edges.append((z > 0, True, tok - xs * CORES))
    edges.append((z < zs - 1, False, tok + xs * CORES))

    def both(a, b):
        return b if a is None else a if b is True else jnp.logical_and(a, b)

    waited, waiting, expected, back = [], [], 2, 0
    for there, waits, other in edges:
        if waits is not False:
            waited.append((both(there, waits), other))
            expected = expected + waited[-1][0].astype(jnp.int32)
        if waits is not True:
            waiting.append((both(there, True if waits is False else jnp.logical_not(waits)), other))
            back = back + waiting[-1][0].astype(jnp.int32)

    def signal_all(sem, group):
        for there, other in group:

            @pl.when(there)
            def _():
                signal(sem, {"tok": other})

    signal_all(barrier, waiting)

    loads[0].wait()
    wt = weights[0]
    heads = wt.shape[0]
    row = iota((Y * CHUNK, heads), 0)
    owner = lax.rem(y + lax.div(row, CHUNK), Y)
    pick = iota((Y * CHUNK, heads), 1) == owner * HL + lax.rem(lax.div(row, ROWS), HL)
    picked = dot(mask(pick).astype(BF16), wt).astype(BF16)
    spread = mask(iota((CH, depth), 0) == lax.rem(iota((CH, depth), 1), CH)).astype(BF16)
    diag = lax.div(iota((Y * CHUNK, depth), 1), CH) == lax.rem(iota((Y * CHUNK, depth), 0), ROWS)
    lhs = (dot(picked, spread) * mask(diag)).astype(BF16)
    picked_f = picked.astype(F32)
    mid = PAIR_MID * jnp.sum(picked_f, axis=1, keepdims=True)
    reach = jnp.maximum(PAIR_HALF * jnp.sum(jnp.abs(picked_f), axis=1, keepdims=True), 1e-20)
    inv = CODE_MAX / reach

    buffers = {
        OPP_UP: (opp_up_s, opp_up_r, up),
        OPP_DN: (opp_dn_s, opp_dn_r, dn),
        DIR_UP: (dir_up_s, dir_up_r, up),
        DIR_DN: (dir_dn_s, dir_dn_r, dn),
        FWD_UP: (fwd_up_s, fwd_up_r, up),
        FWD_DN: (fwd_dn_s, fwd_dn_r, dn),
    }

    def landed(kind, g):
        if kind in (OPP_UP, OPP_DN):
            return opp_r.at[kind - OPP_UP, lax.div(g, 2)]
        if kind in (DIR_UP, DIR_DN):
            return dir_r.at[kind - DIR_UP]
        return fwd_r.at[kind - FWD_UP, jnp.maximum(lax.div(g, 2), g - (groups - 1) + paired)]

    def landed_last(kind, at):
        return fwd_r.at[kind - FWD_UP, paired + (1 if at else 0)]

    def piece(kind, g):
        src, dst, device = buffers[kind]
        return remote(src.at[g], dst.at[g], y_s, landed(kind, g), device)

    def part_of(kind, g, at, width, sem):
        src, dst, device = buffers[kind]
        cols = pl.ds(at, width)
        return remote(src.at[g, :, cols], dst.at[g, :, cols], y_s, sem, device)

    def pieces(kind, g, n):
        src, dst, device = buffers[kind]
        some = pl.ds(g, n)
        return remote(src.at[some], dst.at[some], y_s, landed(kind, g), device)

    def coded(value, scale):
        return jnp.round(value * scale).astype(jnp.int32).astype(I16)

    def produce(g, sides, ats):
        for side in sides:
            for at in ats:
                cols = slice(side * half + at, side * half + at + sub)
                into = slice(at, at + sub)
                part = dot(lhs, pair_v[g, :, cols])
                own[g, :, cols] = part[0:CHUNK]
                part = part[CHUNK:] - mid[CHUNK:]
                to_up, to_opp, to_dn = (part[i * CHUNK : (i + 1) * CHUNK] for i in range(3))
                i_up, i_opp, i_dn = (inv[i * CHUNK : (i + 1) * CHUNK] for i in range(1, Y))
                if side == 0:
                    opp_up_s[g, :, into] = coded(to_opp, i_opp)
                    hold_up[g, :, into] = to_up
                    dir_dn_s[g, :, into] = coded(to_dn, i_dn)
                else:
                    opp_dn_s[g, :, into] = coded(to_opp, i_opp)
                    hold_dn[g, :, into] = to_dn
                    dir_up_s[g, :, into] = coded(to_up, i_up)

    ats = tuple(range(0, half, sub))
    head_loads[0].wait()
    produce(0, (0,), ats[:1])

    pl.semaphore_wait(barrier, expected)

    def weights_copy(k):
        to = {"head": y_at(k)}
        return remote(weights.at[0], weights.at[Y - k], w_s, w_r.at[1 if k == 2 else 0], to)

    for side in range(2):
        for at in ats:
            if side or at:
                if at == ats[1 - side]:
                    head_loads[1 + side].wait()
                produce(0, (side,), (at,))
            for kind in (OPP_DN, DIR_UP) if side else (OPP_UP, DIR_DN):
                part_of(kind, 0, at, sub, landed(kind, 0)).start()
            if side + at == 0:
                pl.when(y >= Y // 2)(other_loads)
    weights_copy(1).start()
    weights_copy(3).start()
    signal(opposite, up)
    signal_all(near, waited)

    rounds = [d for d in (1, 2, 4) if d < zs]

    def tell(r):
        for present, other in (
            (z >= rounds[r], tok - rounds[r] * xs * CORES),
            (z < zs - rounds[r], tok + rounds[r] * xs * CORES),
        ):

            @pl.when(present)
            def _():
                signal(known.at[r], {"tok": other})

    def learn(r):
        amount = (z >= rounds[r]).astype(jnp.int32) + (z < zs - rounds[r]).astype(jnp.int32)
        pl.semaphore_wait(known.at[r], amount)

    loads[1].wait()
    loads[2].wait()
    single = single_v[...].astype(F32)
    normed = normalize(single).astype(BF16)
    query = (dot(normed, aqkv_v[0]) * (1.0 / math.sqrt(ATOM_HEAD_SIZE))).astype(BF16)
    kv_pad[RIM : RIM + atoms, 0:LANES] = dot(normed, aqkv_v[1]).astype(BF16)
    kv_pad[RIM : RIM + atoms, LANES:] = dot(normed, aqkv_v[2]).astype(BF16)
    halo_up = remote(
        kv_pad.at[pl.ds(atoms, RIM), :],
        kv_pad.at[pl.ds(0, RIM), :],
        halo_s.at[0],
        halo_r.at[0],
        {"tok": lax.rem(tok + 1, devs)},
    )
    halo_dn = remote(
        kv_pad.at[pl.ds(RIM, RIM), :],
        kv_pad.at[pl.ds(atoms + RIM, RIM), :],
        halo_s.at[1],
        halo_r.at[1],
        {"tok": lax.rem(tok + devs - 1, devs)},
    )

    def rest(g, carry):
        produce(g, (0, 1), ats)
        for kind in (OPP_UP, OPP_DN, DIR_UP, DIR_DN):
            piece(kind, g).start()
        return carry

    pair_load(1).wait()
    rest(1, 0)
    for g in range(2, groups, 2):
        two_groups = pair_v.at[pl.ds(g, 2)]
        pltpu.make_async_copy(two_groups, two_groups, pair_sem.at[g // 2]).wait()
        lax.fori_loop(g, g + 2, rest, 0)

    @pl.when(back > 0)
    def _():
        pl.semaphore_wait(near, back)

    pl.semaphore_wait(opposite, 1)
    weights_copy(2).start()
    if len(rounds) > 0:
        tell(0)
    first, last = tok == 0, tok == devs - 1

    @pl.when(jnp.logical_not(last))
    def _():
        halo_up.start()

    @pl.when(jnp.logical_not(first))
    def _():
        halo_dn.start()

    def from_owner(value, k):
        shift = lax.rem((2 * Y - y - k) * columns, Y * columns)
        return pltpu.roll(value, shift, 1)[:, 0:LANES]

    for load in loads[4:]:
        load.wait()
    for i in range(4):
        proj_v[:, i * LANES : (i + 1) * LANES] = from_owner(
            qkvg_v[:, i, :].astype(F32), 0
        ).astype(BF16)
    for k in range(Y):
        out_v[:, k * LANES : (k + 1) * LANES] = from_owner(two_v[...].astype(F32), k).astype(BF16)
    if len(rounds) > 1:
        learn(0)
        tell(1)

    @pl.when(first)
    def _():
        kv_pad[0:RIM, :] = jnp.zeros((RIM, 2 * LANES), BF16)

    @pl.when(jnp.logical_not(first))
    def _():
        halo_up.wait_recv()
        halo_dn.wait_send()

    @pl.when(last)
    def _():
        kv_pad[atoms + RIM : atoms + 2 * RIM, :] = jnp.zeros((RIM, 2 * LANES), BF16)

    @pl.when(jnp.logical_not(last))
    def _():
        halo_dn.wait_recv()
        halo_up.wait_send()

    loads[3].wait()
    wide = WQ * ATOM_HEADS
    grow = mask(lax.div(iota((wide, WQ), 0), ATOM_HEADS) == iota((wide, WQ), 1)).astype(BF16)
    fold = mask(iota((WQ, wide), 0) == lax.div(iota((WQ, wide), 1), ATOM_HEADS)).astype(BF16)
    in_head = mask(
        lax.div(iota((wide, LANES), 1), ATOM_HEAD_SIZE) == lax.rem(iota((wide, LANES), 0), ATOM_HEADS)
    )
    slot = iota((wide, WK), 1)
    scores = []
    for w in range(windows):
        q_rows = (dot(grow, query[w * WQ : (w + 1) * WQ]) * in_head).astype(BF16)
        s = dot_nt(q_rows, kv_pad[w * WQ : w * WQ + WK, 0:LANES])
        s = s + bias_v[w * wide : (w + 1) * wide, :].astype(F32)
        if w * WQ < RIM or w * WQ + WK > RIM + atoms:
            spot = tok * atoms + w * WQ - RIM + slot
            s = jnp.where((spot >= 0) & (spot < devs * atoms), s, -1e30)
        scores.append(s)
    probs = []
    for s in scores:
        e = jnp.exp(s - jnp.max(s, axis=-1, keepdims=True))
        probs.append((e * (1.0 / jnp.sum(e, axis=-1, keepdims=True))).astype(BF16))
    mixes = []
    for w in range(windows):
        m = dot(probs[w], kv_pad[w * WQ : w * WQ + WK, LANES:])
        mixes.append(dot(fold, (m * in_head).astype(BF16)).astype(BF16))
    mix = jnp.concatenate(mixes, axis=0)
    a_out = (single + dot(mix, awo_v[...])).astype(BF16)
    atom_out[...] = a_out
    feat = jnp.maximum(dot(a_out, agg_v[...]), 0.0).astype(BF16)

    block = iota((BLOCK_DEVS * here, 1), 0)
    owner_tok = mate(lax.div(block, here)) * here + lax.rem(block, here)
    onehot = mask(owner_tok == name_v[...]).astype(BF16)
    sums = dot(onehot, feat)
    for k in range(1, BLOCK_DEVS):
        sum_s[k] = sums[k * here : (k + 1) * here].astype(BF16)
        remote(
            sum_s.at[k], sum_r.at[BLOCK_DEVS - k], sum_ss, sum_rs, {"tok": mate(k)}
        ).start()
    if len(rounds) > 2:
        learn(1)
        tell(2)

    others = pl.ds(1, BLOCK_DEVS - 1)
    remote(sum_s.at[others], sum_r.at[others], sum_ss, sum_rs, up).wait()
    total = sums[0:here]
    for k in range(1, BLOCK_DEVS):
        total = total + sum_r[k].astype(F32)
    square = iota((here, here), 0) == iota((here, here), 1)
    count = jnp.sum(jnp.where(square, count_v[...].astype(F32), 0.0), axis=1, keepdims=True)
    token_mid = tok_v[...].astype(F32) + total / count
    normed_t = normalize(token_mid).astype(BF16)
    parts = dot(normed_t, proj_v[...])
    t_query = (parts[:, 0:LANES] * (1.0 / math.sqrt(HEAD_SIZE))).astype(BF16)
    kv_all[z, x, c] = parts[:, LANES : 3 * LANES].astype(BF16)
    gate = jax.nn.sigmoid(parts[:, 3 * LANES :])
    residual = from_owner(token_mid, 0)

    if rounds:
        learn(len(rounds) - 1)
    for k in range(1, zs):
        block_k = kv_all.at[z, x, c]
        remote(block_k, block_k, z_s, z_r, {"tok": tok_of(lax.rem(z + k, zs), x, c)}).start()

    two = pl.ds(1, 2)
    remote(weights.at[two], weights.at[two], w_s, w_r.at[0], up).wait_recv()
    r32 = iota((CHUNK, heads), 0)

    def reach_of(sender, k):
        head = y_at(k) * HL + lax.div(r32, ROWS)
        sel = mask(iota((CHUNK, heads), 1) == head).astype(BF16)
        chosen = dot(sel, weights[sender])
        return jnp.maximum(PAIR_HALF * jnp.sum(jnp.abs(chosen), axis=1, keepdims=True), 1e-20)

    step = 1.0 / CODE_MAX
    legs = []
    for kind, out, hold, src, k, to in (
        (OPP_UP, fwd_up_s, hold_up, opp_up_r, 1, FWD_UP),
        (OPP_DN, fwd_dn_s, hold_dn, opp_dn_r, 3, FWD_DN),
    ):
        theirs = reach_of(Y - k, k)
        legs.append((kind, out, hold, src, to, theirs * step, CODE_MAX / (theirs + reach_of(0, k))))
    r_up, r_dn = reach_of(1, 0), reach_of(3, 0)
    s_up, s_dn = r_up * step, r_dn * step

    early = half - sub if half > sub else half
    last_parts = [(0, early), (early, half - early)] if early < half else [(0, half)]

    def forward(g, last):
        for kind, out, hold, src, to, theirs, scale in legs:
            out[g] = coded(src[g].astype(F32) * theirs + hold[g], scale)
            if not last:
                piece(to, g).start()
        if last:
            for at, width in last_parts:
                for to in (FWD_UP, FWD_DN):
                    part_of(to, g, at, width, landed_last(to, at)).start()

    def forward_two(i, last=False):
        for kind in (OPP_UP, OPP_DN):
            pieces(kind, 2 * i, 2).wait_recv()
        forward(2 * i, False)
        forward(2 * i + 1, last)

    forward_two(0)

    if zs > 1:
        others_z = kv_all.at[pl.ds(0, zs - 1), x, c]
        remote(others_z, others_z, z_s, z_r, {"tok": tok}).wait_recv()

    def column(k):
        return kv_all.at[:, x_at(k), c]

    def send(ref, s_sem, r_sem, device):
        copy = remote(ref, ref, s_sem, r_sem, device)
        copy.start()
        return copy

    x_up, x_dn = {"tok": tok_of(z, x_at(1), c)}, {"tok": tok_of(z, x_at(xs - 1), c)}
    other = {"tok": tok_of(z, x, 1 - c)}
    send(column(0), x_s, x_r.at[0], x_up)
    if xs > 2:
        send(column(0), x_s, x_r.at[1], x_dn)
    send(column(0), c_s, c_r, other)

    forward_two(1)

    def arrived(ref, sem):
        remote(ref, ref, x_s, sem, other).wait_recv()

    arrived(column(xs - 1), x_r.at[0])
    if xs > 2:
        lower, upper = pl.ds(0, zs // 2), pl.ds(zs // 2, zs - zs // 2)
        send(kv_all.at[lower, x_at(xs - 1), c], x_s, x_r.at[2], x_up)
        arrived(column(1), x_r.at[1])
        send(kv_all.at[upper, x_at(1), c], x_s, x_r.at[2], x_dn)
        send(column(1), c_s, c_r, other)
    send(column(xs - 1), c_s, c_r, other)

    forward_two(2, True)

    if xs > 2:
        arrived(column(2), x_r.at[2])
        send(column(2), c_s, c_r, other)
    arrived(kv_all.at[:, :, 1 - c], c_r)

    rows = groups * CHUNK
    rr = iota((rows, here), 0)
    pick_row = lax.div(rr, CHUNK) * ROWS + lax.rem(rr, ROWS) == iota((rows, here), 1)
    rl = iota((rows, LANES), 0)
    of_head = mask(
        lax.div(iota((rows, LANES), 1), HEAD_SIZE) == lax.rem(lax.div(rl, ROWS), HL)
    )
    q_rows = (dot(mask(pick_row).astype(BF16), t_query) * of_head).astype(BF16)
    key_rows = kv_all[..., 0:LANES].reshape(keys, LANES)
    for at in range(0, keys, 2 * sub):
        s = dot_nt(q_rows, key_rows[at : at + 2 * sub])
        score[:, :, at : at + 2 * sub] = s.reshape(groups, CHUNK, 2 * sub)

    for kind in (DIR_UP, DIR_DN):
        pieces(kind, 0, groups).wait_recv()

    def direct(g, carry):
        for side, (ref, scale) in enumerate(((dir_dn_r, s_up), (dir_up_r, s_dn))):
            for at in range(0, half, sub):
                cols = slice(side * half + at, side * half + at + sub)
                got = ref[g, :, at : at + sub].astype(F32) * scale
                score[g, :, cols] = score[g, :, cols] + (own[g, :, cols] + got)
        return carry

    lax.fori_loop(0, groups, direct, 0)

    head_mask = of_head[0:CHUNK]

    weights_copy(2).wait_recv()
    r_opp = reach_of(2, 0)
    s_up2, s_dn2 = (r_up + r_opp) * step, (r_dn + r_opp) * step

    def attend_part(g, at_first, width, state):
        spans = []
        peak = state[0] if state else None
        for side, (ref, scale) in enumerate(((fwd_up_r, s_dn2), (fwd_dn_r, s_up2))):
            for at in range(at_first, at_first + width, sub):
                cols = slice(side * half + at, side * half + at + sub)
                s = score[g, :, cols] + ref[g, :, at : at + sub].astype(F32) * scale
                score[g, :, cols] = s
                spans.append(cols)
                high = jnp.max(s, axis=-1, keepdims=True)
                peak = high if peak is None else jnp.maximum(peak, high)
        if state:
            shrink = jnp.exp(state[0] - peak)
            norm, acc = state[1] * shrink, state[2] * shrink
        else:
            norm, acc = jnp.zeros((CHUNK, 1), F32), jnp.zeros((CHUNK, LANES), F32)
        value_rows = kv_all[..., LANES:].reshape(keys, LANES)
        for cols in spans:
            e = jnp.exp(score[g, :, cols] - peak)
            norm = norm + jnp.sum(e, axis=-1, keepdims=True)
            acc = acc + dot(e.astype(BF16), value_rows[cols])
        return peak, norm, acc

    def finish(g, state):
        acc = state[2] * head_mask / state[1]
        mixed[g] = jnp.sum(acc.reshape(HL, ROWS, LANES), axis=0)

    def attend(g, carry):
        finish(g, attend_part(g, 0, half, None))
        return carry

    for g in range(0, groups - 2, 2):
        for kind in (FWD_UP, FWD_DN):
            pieces(kind, g, 2).wait_recv()
        lax.fori_loop(g, g + 2, attend, 0)
    for kind in (FWD_UP, FWD_DN):
        piece(kind, groups - 2).wait_recv()
    attend(groups - 2, 0)
    state = None
    for at, width in last_parts:
        for kind in (FWD_UP, FWD_DN):
            part_of(kind, groups - 1, at, width, landed_last(kind, at)).wait_recv()
        state = attend_part(groups - 1, at, width, state)
    finish(groups - 1, state)

    out_rows = (mixed[...].reshape(here, LANES) * gate).astype(BF16)
    term = dot(out_rows[:, 0:columns], out_v[...])
    for k in range(1, Y):
        fin_s[k] = term[:, k * LANES : (k + 1) * LANES].astype(BF16)
    for i in range(Y - 1):
        target = i + (y <= i).astype(jnp.int32)
        k = lax.rem(target - y + Y, Y)
        remote(fin_s.at[k], fin_r.at[Y - k], fin_ss, fin_rs, {"head": target}).start()
    peers = pl.ds(1, Y - 1)
    remote(codes_s, codes_s, y_s, w_r.at[0], up).wait_send()
    remote(weights.at[peers], weights.at[peers], w_s, w_r.at[0], up).wait_send()
    if zs > 1:
        remote(others_z, others_z, z_s, z_r, other).wait_send()
    x_sent = kv_all.at[:, pl.ds(0, 3 if xs > 2 else 1), c]
    remote(x_sent, x_sent, x_s, x_r.at[0], other).wait_send()
    remote(kv_all.at[:, :, c], kv_all.at[:, :, c], c_s, c_r, other).wait_send()
    result = residual + term[:, 0:LANES]
    remote(fin_s.at[peers], fin_r.at[peers], fin_ss, fin_rs, up).wait()
    for k in range(1, Y):
        result = result + fin_r[k].astype(F32)
    token_out[...] = result[:, 0:columns].astype(BF16)


def hand_over(a, b, a_out, b_out, sems):
    copies = [
        pltpu.make_async_copy(a, a_out, sems.at[0]),
        pltpu.make_async_copy(b, b_out, sems.at[1]),
    ]
    for copy in copies:
        copy.start()
    for copy in copies:
        copy.wait()


def per_device(
    atom_single,
    atom_bias,
    atom_token,
    atom_count,
    token_single,
    pair,
    atom_qkv,
    atom_wo,
    atom_agg,
    token_qkvg,
    pair_weight,
    token_wo,
):
    devs = lax.axis_size("tok")
    xs = 4 if devs % 32 == 0 else 2
    zs = devs // (xs * CORES)
    atoms, width = atom_single.shape
    here, width_t = token_single.shape
    keys = pair.shape[2]
    groups = here // ROWS
    half = keys // 2
    columns = width_t // Y
    depth = ROWS * CH
    anywhere = pl.BlockSpec(memory_space=pl.ANY)
    vmem = pl.BlockSpec(memory_space=pltpu.VMEM)
    dma = pltpu.SemaphoreType.DMA
    code = pltpu.VMEM((groups, CHUNK, half), I16)
    operands = (
        atom_single,
        atom_bias.reshape(atoms * ATOM_HEADS, WK),
        atom_token.reshape(1, atoms),
        atom_count.reshape(1, here),
        token_single,
        pair.reshape(here * CH, keys),
        jnp.transpose(atom_qkv, (1, 0, 2)),
        atom_wo,
        atom_agg,
        token_qkvg,
        jnp.transpose(pair_weight),
        token_wo,
    )
    scratch = [
        pltpu.VMEM((atoms, width), BF16),
        pltpu.VMEM((atoms * ATOM_HEADS, WK), BF16),
        pltpu.VMEM((1, atoms), jnp.int32),
        pltpu.VMEM((1, here), jnp.int32),
        pltpu.VMEM((here, width_t), BF16),
        pltpu.VMEM((groups, depth, keys), BF16),
        pltpu.VMEM((3, width, width), BF16),
        pltpu.VMEM(atom_wo.shape, BF16),
        pltpu.VMEM(atom_agg.shape, BF16),
        pltpu.VMEM(token_qkvg.shape, BF16),
        pltpu.VMEM(token_wo.shape, BF16),
        pltpu.VMEM((atoms + 2 * RIM, 2 * width), BF16),
        pltpu.VMEM((Y, Y * HL, CH), BF16),
        pltpu.VMEM((groups, CHUNK, keys), F32),
        pltpu.VMEM((groups, CHUNK, half), F32),
        pltpu.VMEM((groups, CHUNK, half), F32),
        pltpu.VMEM((6, groups, CHUNK, half), I16),
        *([code] * 6),
        pltpu.VMEM((BLOCK_DEVS, here, width_t), BF16),
        pltpu.VMEM((BLOCK_DEVS, here, width_t), BF16),
        pltpu.VMEM((zs, xs, CORES, here, 2 * LANES), BF16),
        pltpu.VMEM((groups, CHUNK, keys), F32),
        pltpu.VMEM((groups, ROWS, LANES), F32),
        pltpu.VMEM((Y, here, LANES), BF16),
        pltpu.VMEM((Y, here, LANES), BF16),
        pltpu.VMEM((width_t, 4 * LANES), BF16),
        pltpu.VMEM((columns, Y * LANES), BF16),
        dma((11,)),
        dma((6,)),
        dma((2,)),
        dma((2,)),
        dma,
        dma((2,)),
        dma,
        dma((2, groups // 2)),
        dma((2,)),
        dma((2, groups // 2 + 2)),
        dma,
        dma,
        dma,
        dma,
        dma,
        dma((3,)),
        dma,
        dma,
        dma,
        dma,
        pltpu.SemaphoreType.REGULAR((3,)),
        pltpu.SemaphoreType.REGULAR,
        pltpu.SemaphoreType.REGULAR,
    ]
    outs = (
        pltpu.VMEM((atoms, width), BF16),
        pltpu.VMEM((here, columns), BF16),
    )
    results = pl.pallas_call(
        functools.partial(fused, zs, xs),
        out_shape=outs,
        in_specs=[anywhere] * len(operands),
        out_specs=(vmem, vmem),
        scratch_shapes=scratch,
        compiler_params=pltpu.CompilerParams(
            collective_id=0, has_side_effects=True, vmem_limit_bytes=56 * 2**20
        ),
    )(*operands)
    results = [pltpu.with_memory_space_constraint(r, pltpu.VMEM) for r in results]
    return pl.pallas_call(
        hand_over,
        out_shape=tuple(pltpu.HBM(r.shape, r.dtype) for r in results),
        in_specs=[anywhere, anywhere],
        out_specs=(anywhere, anywhere),
        scratch_shapes=[dma((2,))],
    )(*results)


def solution(mesh):
    in_specs = (
        P("tok", None),
        P("tok", None, None),
        P("tok"),
        P("tok"),
        P("tok", None),
        P("tok", "head", None),
        P(),
        P(),
        P(),
        P(),
        P("head", None),
        P("head", None),
    )
    out_specs = (P("tok", None), P("tok", "head"))
    return jax.shard_map(
        per_device, mesh=mesh, in_specs=in_specs, out_specs=out_specs, check_vma=False
    )
```

```python
import functools
import math

import jax
import jax.numpy as jnp
from jax import lax
from jax.experimental import pallas as pl
from jax.experimental.pallas import tpu as pltpu
from jax.sharding import PartitionSpec as P

ATOM_HEADS = 4
WQ = 32
WK = 128
RIM = (WK - WQ) // 2
BLOCK_DEVS = 4
HEAD_SIZE = 24
ATOM_HEAD_SIZE = 32
EPS = 1e-05

Y = 4
CORES = 2
ROWS = 8
CH = 32
HL = 4
CHUNK = HL * ROWS
LANES = 128

PAIR_MID = 9.5
PAIR_HALF = 14.5
CODE_MAX = 32700.0

F32 = jnp.float32
BF16 = jnp.bfloat16
I16 = jnp.int16
MESH = pl.DeviceIdType.MESH

OPP_UP, OPP_DN, DIR_UP, DIR_DN, FWD_UP, FWD_DN = range(6)


def iota(shape, dim):
    return lax.broadcasted_iota(jnp.int32, shape, dim)


def dot(a, b):
    return jnp.dot(a, b, preferred_element_type=F32)


def dot_nt(a, b):
    return lax.dot_general(a, b, (((1,), (1,)), ((), ())), preferred_element_type=F32)


def mask(cond):
    return jnp.where(cond, 1.0, 0.0).astype(F32)


def normalize(rows):
    mean = jnp.mean(rows, axis=-1, keepdims=True)
    centered = rows - mean
    spread = jnp.mean(centered * centered, axis=-1, keepdims=True)
    return centered * lax.rsqrt(spread + EPS)


def fused(
    zs,
    xs,
    atom_single,
    atom_bias,
    atom_token,
    atom_count,
    token_single,
    pair,
    atom_qkv,
    atom_wo,
    atom_agg,
    token_qkvg,
    pair_weight,
    token_wo,
    atom_out,
    token_out,
    single_v,
    bias_v,
    name_v,
    count_v,
    tok_v,
    pair_v,
    aqkv_v,
    awo_v,
    agg_v,
    qkvg_v,
    two_v,
    kv_pad,
    weights,
    own,
    hold_up,
    hold_dn,
    codes_s,
    opp_up_r,
    opp_dn_r,
    dir_up_r,
    dir_dn_r,
    fwd_up_r,
    fwd_dn_r,
    sum_s,
    sum_r,
    kv_all,
    score,
    mixed,
    fin_s,
    fin_r,
    proj_v,
    out_v,
    in_sem,
    pair_sem,
    halo_s,
    halo_r,
    w_s,
    w_r,
    y_s,
    opp_r,
    dir_r,
    fwd_r,
    sum_ss,
    sum_rs,
    z_s,
    z_r,
    x_s,
    x_r,
    c_s,
    c_r,
    fin_ss,
    fin_rs,
    known,
    near,
    opposite,
):
    tok = lax.axis_index("tok")
    y = lax.axis_index("head")
    devs = zs * xs * CORES
    z = lax.div(tok, xs * CORES)
    x = lax.rem(lax.div(tok, CORES), xs)
    c = lax.rem(tok, CORES)
    place = lax.rem(tok, BLOCK_DEVS)
    groups, depth, keys = pair_v.shape
    half = keys // 2
    here = tok_v.shape[0]
    atoms = single_v.shape[0]
    windows = atoms // WQ
    sub = half // 3 if half % 3 == 0 else half
    columns = HL * HEAD_SIZE
    paired = groups // 2

    def tok_of(z_, x_, c_):
        return (z_ * xs + x_) * CORES + c_

    def y_at(k):
        return lax.rem(y + k, Y)

    def x_at(k):
        return lax.rem(x + k, xs)

    def mate(k):
        return tok - place + lax.rem(place + k, BLOCK_DEVS)

    up, dn = {"head": y_at(1)}, {"head": y_at(3)}

    def remote(src, dst, send, recv, device):
        return pltpu.make_async_remote_copy(
            src_ref=src,
            dst_ref=dst,
            send_sem=send,
            recv_sem=recv,
            device_id=device,
            device_id_type=MESH,
        )

    def signal(sem, device):
        pl.semaphore_signal(sem, inc=1, device_id=device, device_id_type=MESH)

    barrier = pltpu.get_barrier_semaphore()
    for device in (up, dn):
        signal(barrier, device)

    opp_up_s, opp_dn_s, dir_up_s, dir_dn_s, fwd_up_s, fwd_dn_s = (codes_s.at[i] for i in range(6))

    loads = [
        (pair_weight, weights.at[0]),
        (atom_single, single_v),
        (atom_qkv, aqkv_v),
        (atom_bias, bias_v),
        (atom_wo, awo_v),
        (atom_agg, agg_v),
        (atom_token, name_v),
        (atom_count, count_v),
        (token_qkvg, qkvg_v),
        (token_single, tok_v),
        (token_wo, two_v),
    ]
    loads = [pltpu.make_async_copy(a, b, in_sem.at[i]) for i, (a, b) in enumerate(loads)]

    def pair_load(g):
        return pltpu.make_async_copy(
            pair.at[pl.ds(pl.multiple_of(g * depth, depth), depth), :],
            pair_v.at[g],
            pair_sem.at[5 if g == 1 else g // 2],
        )

    head_loads = [
        pltpu.make_async_copy(
            pair.at[pl.ds(0, depth), pl.ds(at, width)],
            pair_v.at[0, :, pl.ds(at, width)],
            pair_sem.at[sem],
        )
        for at, width, sem in ((0, sub, 0), (sub, half - sub, 3), (half, half, 4))
        if width
    ]
    loads[0].start()
    for load in head_loads:
        load.start()
    loads[1].start()
    loads[2].start()
    for g in range(1, groups):
        pair_load(g).start()
    for load in loads[3:]:
        load.start()

    first_core = c == 0
    edges = []
    for k in range(1, BLOCK_DEVS):
        same = lax.div(place, CORES) == lax.div(lax.rem(place + k, BLOCK_DEVS), CORES)
        edges.append((None, jnp.where(same, first_core, place + k >= BLOCK_DEVS), mate(k)))
    for k in sorted({1, xs - 1}):
        edges.append((None, x + k >= xs, tok_of(z, x_at(k), c)))
    edges.append((None, first_core, tok_of(z, x, 1 - c)))
    edges.append((tok > 0, first_core, tok - 1))
    edges.append((tok < devs - 1, first_core, tok + 1))
    edges.append((z > 0, True, tok - xs * CORES))
    edges.append((z < zs - 1, False, tok + xs * CORES))

    def both(a, b):
        return b if a is None else a if b is True else jnp.logical_and(a, b)

    waited, waiting, expected, back = [], [], 2, 0
    for there, waits, other in edges:
        if waits is not False:
            waited.append((both(there, waits), other))
            expected = expected + waited[-1][0].astype(jnp.int32)
        if waits is not True:
            waiting.append((both(there, True if waits is False else jnp.logical_not(waits)), other))
            back = back + waiting[-1][0].astype(jnp.int32)

    def signal_all(sem, group):
        for there, other in group:

            @pl.when(there)
            def _():
                signal(sem, {"tok": other})

    signal_all(barrier, waiting)

    heads = weights.shape[1]
    row = iota((Y * CHUNK, heads), 0)
    owner = lax.rem(y + lax.div(row, CHUNK), Y)
    pick = iota((Y * CHUNK, heads), 1) == owner * HL + lax.rem(lax.div(row, ROWS), HL)
    pick = mask(pick).astype(BF16)
    diag = lax.div(iota((Y * CHUNK, depth), 1), CH) == lax.rem(iota((Y * CHUNK, depth), 0), ROWS)
    diag = mask(diag)
    loads[0].wait()
    tiled = jnp.concatenate([weights[0]] * ROWS, axis=1)
    picked_f = dot(pick, tiled)
    lhs = (picked_f * diag).astype(BF16)
    picked_f = picked_f[:, 0:CH]
    mid = PAIR_MID * jnp.sum(picked_f, axis=1, keepdims=True)
    reach = jnp.maximum(PAIR_HALF * jnp.sum(jnp.abs(picked_f), axis=1, keepdims=True), 1e-20)
    inv = CODE_MAX / reach

    buffers = {
        OPP_UP: (opp_up_s, opp_up_r, up),
        OPP_DN: (opp_dn_s, opp_dn_r, dn),
        DIR_UP: (dir_up_s, dir_up_r, up),
        DIR_DN: (dir_dn_s, dir_dn_r, dn),
        FWD_UP: (fwd_up_s, fwd_up_r, up),
        FWD_DN: (fwd_dn_s, fwd_dn_r, dn),
    }

    def landed(kind, g):
        if kind in (OPP_UP, OPP_DN):
            return opp_r.at[kind - OPP_UP, lax.div(g, 2)]
        if kind in (DIR_UP, DIR_DN):
            return dir_r.at[kind - DIR_UP]
        return fwd_r.at[kind - FWD_UP, jnp.maximum(lax.div(g, 2), g - (groups - 1) + paired)]

    def landed_last(kind, at):
        return fwd_r.at[kind - FWD_UP, paired + (1 if at else 0)]

    def piece(kind, g):
        src, dst, device = buffers[kind]
        return remote(src.at[g], dst.at[g], y_s, landed(kind, g), device)

    def part_of(kind, g, at, width, sem):
        src, dst, device = buffers[kind]
        cols = pl.ds(at, width)
        return remote(src.at[g, :, cols], dst.at[g, :, cols], y_s, sem, device)

    def pieces(kind, g, n):
        src, dst, device = buffers[kind]
        some = pl.ds(g, n)
        return remote(src.at[some], dst.at[some], y_s, landed(kind, g), device)

    def coded(value, scale):
        return jnp.round(value * scale).astype(jnp.int32).astype(I16)

    def produce(g, sides, ats):
        for side in sides:
            for at in ats:
                cols = slice(side * half + at, side * half + at + sub)
                into = slice(at, at + sub)
                part = dot(lhs, pair_v[g, :, cols])
                own[g, :, cols] = part[0:CHUNK]
                part = part[CHUNK:] - mid[CHUNK:]
                to_up, to_opp, to_dn = (part[i * CHUNK : (i + 1) * CHUNK] for i in range(3))
                i_up, i_opp, i_dn = (inv[i * CHUNK : (i + 1) * CHUNK] for i in range(1, Y))
                if side == 0:
                    opp_up_s[g, :, into] = coded(to_opp, i_opp)
                    hold_up[g, :, into] = to_up
                    dir_dn_s[g, :, into] = coded(to_dn, i_dn)
                else:
                    opp_dn_s[g, :, into] = coded(to_opp, i_opp)
                    hold_dn[g, :, into] = to_dn
                    dir_up_s[g, :, into] = coded(to_up, i_up)

    ats = tuple(range(0, half, sub))
    head_loads[0].wait()
    produce(0, (0,), ats[:1])

    pl.semaphore_wait(barrier, expected)

    def weights_copy(k):
        to = {"head": y_at(k)}
        return remote(weights.at[0], weights.at[Y - k], w_s, w_r.at[1 if k == 2 else 0], to)

    for side in range(2):
        for at in ats:
            if side or at:
                if at == ats[1 - side]:
                    head_loads[1 + side].wait()
                produce(0, (side,), (at,))
            for kind in (OPP_DN, DIR_UP) if side else (OPP_UP, DIR_DN):
                part_of(kind, 0, at, sub, landed(kind, 0)).start()
    weights_copy(1).start()
    weights_copy(3).start()
    signal(opposite, up)
    signal_all(near, waited)

    rounds = [d for d in (1, 2, 4) if d < zs]

    def tell(r):
        for present, other in (
            (z >= rounds[r], tok - rounds[r] * xs * CORES),
            (z < zs - rounds[r], tok + rounds[r] * xs * CORES),
        ):

            @pl.when(present)
            def _():
                signal(known.at[r], {"tok": other})

    def learn(r):
        amount = (z >= rounds[r]).astype(jnp.int32) + (z < zs - rounds[r]).astype(jnp.int32)
        pl.semaphore_wait(known.at[r], amount)

    loads[1].wait()
    loads[2].wait()
    single = single_v[...].astype(F32)
    normed = normalize(single).astype(BF16)
    query = (dot(normed, aqkv_v[0]) * (1.0 / math.sqrt(ATOM_HEAD_SIZE))).astype(BF16)
    kv_pad[RIM : RIM + atoms, 0:LANES] = dot(normed, aqkv_v[1]).astype(BF16)
    kv_pad[RIM : RIM + atoms, LANES:] = dot(normed, aqkv_v[2]).astype(BF16)
    halo_up = remote(
        kv_pad.at[pl.ds(atoms, RIM), :],
        kv_pad.at[pl.ds(0, RIM), :],
        halo_s.at[0],
        halo_r.at[0],
        {"tok": lax.rem(tok + 1, devs)},
    )
    halo_dn = remote(
        kv_pad.at[pl.ds(RIM, RIM), :],
        kv_pad.at[pl.ds(atoms + RIM, RIM), :],
        halo_s.at[1],
        halo_r.at[1],
        {"tok": lax.rem(tok + devs - 1, devs)},
    )

    def rest(g, carry):
        produce(g, (0, 1), ats)
        for kind in (OPP_UP, OPP_DN, DIR_UP, DIR_DN):
            piece(kind, g).start()
        return carry

    pair_load(1).wait()
    rest(1, 0)
    for g in range(2, groups, 2):
        two_groups = pair_v.at[pl.ds(g, 2)]
        pltpu.make_async_copy(two_groups, two_groups, pair_sem.at[g // 2]).wait()
        lax.fori_loop(g, g + 2, rest, 0)

    @pl.when(back > 0)
    def _():
        pl.semaphore_wait(near, back)

    pl.semaphore_wait(opposite, 1)
    weights_copy(2).start()
    if len(rounds) > 0:
        tell(0)
    first, last = tok == 0, tok == devs - 1

    @pl.when(jnp.logical_not(last))
    def _():
        halo_up.start()

    @pl.when(jnp.logical_not(first))
    def _():
        halo_dn.start()

    def from_owner(value, k):
        shift = lax.rem((2 * Y - y - k) * columns, Y * columns)
        return pltpu.roll(value, shift, 1)[:, 0:LANES]

    for load in loads[4:]:
        load.wait()
    for i in range(4):
        proj_v[:, i * LANES : (i + 1) * LANES] = from_owner(
            qkvg_v[:, i, :].astype(F32), 0
        ).astype(BF16)
    for k in range(Y):
        out_v[:, k * LANES : (k + 1) * LANES] = from_owner(two_v[...].astype(F32), k).astype(BF16)
    if len(rounds) > 1:
        learn(0)
        tell(1)

    @pl.when(first)
    def _():
        kv_pad[0:RIM, :] = jnp.zeros((RIM, 2 * LANES), BF16)

    @pl.when(jnp.logical_not(first))
    def _():
        halo_up.wait_recv()
        halo_dn.wait_send()

    @pl.when(last)
    def _():
        kv_pad[atoms + RIM : atoms + 2 * RIM, :] = jnp.zeros((RIM, 2 * LANES), BF16)

    @pl.when(jnp.logical_not(last))
    def _():
        halo_dn.wait_recv()
        halo_up.wait_send()

    loads[3].wait()
    wide = WQ * ATOM_HEADS
    grow = mask(lax.div(iota((wide, WQ), 0), ATOM_HEADS) == iota((wide, WQ), 1)).astype(BF16)
    fold = mask(iota((WQ, wide), 0) == lax.div(iota((WQ, wide), 1), ATOM_HEADS)).astype(BF16)
    in_head = mask(
        lax.div(iota((wide, LANES), 1), ATOM_HEAD_SIZE) == lax.rem(iota((wide, LANES), 0), ATOM_HEADS)
    )
    slot = iota((wide, WK), 1)
    scores = []
    for w in range(windows):
        q_rows = (dot(grow, query[w * WQ : (w + 1) * WQ]) * in_head).astype(BF16)
        s = dot_nt(q_rows, kv_pad[w * WQ : w * WQ + WK, 0:LANES])
        s = s + bias_v[w * wide : (w + 1) * wide, :].astype(F32)
        if w * WQ < RIM or w * WQ + WK > RIM + atoms:
            spot = tok * atoms + w * WQ - RIM + slot
            s = jnp.where((spot >= 0) & (spot < devs * atoms), s, -1e30)
        scores.append(s)
    probs = []
    for s in scores:
        e = jnp.exp(s - jnp.max(s, axis=-1, keepdims=True))
        probs.append((e * (1.0 / jnp.sum(e, axis=-1, keepdims=True))).astype(BF16))
    mixes = []
    for w in range(windows):
        m = dot(probs[w], kv_pad[w * WQ : w * WQ + WK, LANES:])
        mixes.append(dot(fold, (m * in_head).astype(BF16)).astype(BF16))
    mix = jnp.concatenate(mixes, axis=0)
    a_out = (single + dot(mix, awo_v[...])).astype(BF16)
    atom_out[...] = a_out
    feat = jnp.maximum(dot(a_out, agg_v[...]), 0.0).astype(BF16)

    block = iota((BLOCK_DEVS * here, 1), 0)
    owner_tok = mate(lax.div(block, here)) * here + lax.rem(block, here)
    onehot = mask(owner_tok == name_v[...]).astype(BF16)
    sums = dot(onehot, feat)
    for k in range(1, BLOCK_DEVS):
        sum_s[k] = sums[k * here : (k + 1) * here].astype(BF16)
        remote(
            sum_s.at[k], sum_r.at[BLOCK_DEVS - k], sum_ss, sum_rs, {"tok": mate(k)}
        ).start()
    if len(rounds) > 2:
        learn(1)
        tell(2)

    others = pl.ds(1, BLOCK_DEVS - 1)
    remote(sum_s.at[others], sum_r.at[others], sum_ss, sum_rs, up).wait()
    total = sums[0:here]
    for k in range(1, BLOCK_DEVS):
        total = total + sum_r[k].astype(F32)
    square = iota((here, here), 0) == iota((here, here), 1)
    count = jnp.sum(jnp.where(square, count_v[...].astype(F32), 0.0), axis=1, keepdims=True)
    token_mid = tok_v[...].astype(F32) + total / count
    normed_t = normalize(token_mid).astype(BF16)
    parts = dot(normed_t, proj_v[...])
    t_query = (parts[:, 0:LANES] * (1.0 / math.sqrt(HEAD_SIZE))).astype(BF16)
    kv_all[z, x, c] = parts[:, LANES : 3 * LANES].astype(BF16)
    gate = jax.nn.sigmoid(parts[:, 3 * LANES :])
    residual = from_owner(token_mid, 0)

    if rounds:
        learn(len(rounds) - 1)
    for k in range(1, zs):
        block_k = kv_all.at[z, x, c]
        remote(block_k, block_k, z_s, z_r, {"tok": tok_of(lax.rem(z + k, zs), x, c)}).start()

    two = pl.ds(1, 2)
    remote(weights.at[two], weights.at[two], w_s, w_r.at[0], up).wait_recv()
    r32 = iota((CHUNK, heads), 0)

    def reach_of(sender, k):
        head = y_at(k) * HL + lax.div(r32, ROWS)
        sel = mask(iota((CHUNK, heads), 1) == head).astype(BF16)
        chosen = dot(sel, weights[sender])
        return jnp.maximum(PAIR_HALF * jnp.sum(jnp.abs(chosen), axis=1, keepdims=True), 1e-20)

    step = 1.0 / CODE_MAX
    legs = []
    for kind, out, hold, src, k, to in (
        (OPP_UP, fwd_up_s, hold_up, opp_up_r, 1, FWD_UP),
        (OPP_DN, fwd_dn_s, hold_dn, opp_dn_r, 3, FWD_DN),
    ):
        theirs = reach_of(Y - k, k)
        legs.append((kind, out, hold, src, to, theirs * step, CODE_MAX / (theirs + reach_of(0, k))))
    r_up, r_dn = reach_of(1, 0), reach_of(3, 0)
    s_up, s_dn = r_up * step, r_dn * step

    early = half - sub if half > sub else half
    last_parts = [(0, early), (early, half - early)] if early < half else [(0, half)]

    def forward(g, last):
        for kind, out, hold, src, to, theirs, scale in legs:
            out[g] = coded(src[g].astype(F32) * theirs + hold[g], scale)
            if not last:
                piece(to, g).start()
        if last:
            for at, width in last_parts:
                for to in (FWD_UP, FWD_DN):
                    part_of(to, g, at, width, landed_last(to, at)).start()

    def forward_two(i, last=False):
        for kind in (OPP_UP, OPP_DN):
            pieces(kind, 2 * i, 2).wait_recv()
        forward(2 * i, False)
        forward(2 * i + 1, last)

    forward_two(0)

    if zs > 1:
        others_z = kv_all.at[pl.ds(0, zs - 1), x, c]
        remote(others_z, others_z, z_s, z_r, {"tok": tok}).wait_recv()

    def column(k):
        return kv_all.at[:, x_at(k), c]

    def send(ref, s_sem, r_sem, device):
        copy = remote(ref, ref, s_sem, r_sem, device)
        copy.start()
        return copy

    x_up, x_dn = {"tok": tok_of(z, x_at(1), c)}, {"tok": tok_of(z, x_at(xs - 1), c)}
    other = {"tok": tok_of(z, x, 1 - c)}
    send(column(0), x_s, x_r.at[0], x_up)
    if xs > 2:
        send(column(0), x_s, x_r.at[1], x_dn)
    send(column(0), c_s, c_r, other)

    forward_two(1)

    def arrived(ref, sem):
        remote(ref, ref, x_s, sem, other).wait_recv()

    arrived(column(xs - 1), x_r.at[0])
    if xs > 2:
        lower, upper = pl.ds(0, zs // 2), pl.ds(zs // 2, zs - zs // 2)
        send(kv_all.at[lower, x_at(xs - 1), c], x_s, x_r.at[2], x_up)
        arrived(column(1), x_r.at[1])
        send(kv_all.at[upper, x_at(1), c], x_s, x_r.at[2], x_dn)
        send(column(1), c_s, c_r, other)
    send(column(xs - 1), c_s, c_r, other)

    forward_two(2, True)

    if xs > 2:
        arrived(column(2), x_r.at[2])
        send(column(2), c_s, c_r, other)
    arrived(kv_all.at[:, :, 1 - c], c_r)

    rows = groups * CHUNK
    rr = iota((rows, here), 0)
    pick_row = lax.div(rr, CHUNK) * ROWS + lax.rem(rr, ROWS) == iota((rows, here), 1)
    rl = iota((rows, LANES), 0)
    of_head = mask(
        lax.div(iota((rows, LANES), 1), HEAD_SIZE) == lax.rem(lax.div(rl, ROWS), HL)
    )
    q_rows = (dot(mask(pick_row).astype(BF16), t_query) * of_head).astype(BF16)
    key_rows = kv_all[..., 0:LANES].reshape(keys, LANES)
    for at in range(0, keys, 2 * sub):
        s = dot_nt(q_rows, key_rows[at : at + 2 * sub])
        score[:, :, at : at + 2 * sub] = s.reshape(groups, CHUNK, 2 * sub)

    for kind in (DIR_UP, DIR_DN):
        pieces(kind, 0, groups).wait_recv()

    def direct(g, carry):
        for side, (ref, scale) in enumerate(((dir_dn_r, s_up), (dir_up_r, s_dn))):
            for at in range(0, half, sub):
                cols = slice(side * half + at, side * half + at + sub)
                got = ref[g, :, at : at + sub].astype(F32) * scale
                score[g, :, cols] = score[g, :, cols] + (own[g, :, cols] + got)
        return carry

    lax.fori_loop(0, groups, direct, 0)

    head_mask = of_head[0:CHUNK]

    weights_copy(2).wait_recv()
    r_opp = reach_of(2, 0)
    s_up2, s_dn2 = (r_up + r_opp) * step, (r_dn + r_opp) * step

    def attend_part(g, at_first, width, state):
        spans = []
        peak = state[0] if state else None
        for side, (ref, scale) in enumerate(((fwd_up_r, s_dn2), (fwd_dn_r, s_up2))):
            for at in range(at_first, at_first + width, sub):
                cols = slice(side * half + at, side * half + at + sub)
                s = score[g, :, cols] + ref[g, :, at : at + sub].astype(F32) * scale
                score[g, :, cols] = s
                spans.append(cols)
                high = jnp.max(s, axis=-1, keepdims=True)
                peak = high if peak is None else jnp.maximum(peak, high)
        if state:
            shrink = jnp.exp(state[0] - peak)
            norm, acc = state[1] * shrink, state[2] * shrink
        else:
            norm, acc = jnp.zeros((CHUNK, 1), F32), jnp.zeros((CHUNK, LANES), F32)
        value_rows = kv_all[..., LANES:].reshape(keys, LANES)
        for cols in spans:
            e = jnp.exp(score[g, :, cols] - peak)
            norm = norm + jnp.sum(e, axis=-1, keepdims=True)
            acc = acc + dot(e.astype(BF16), value_rows[cols])
        return peak, norm, acc

    def finish(g, state):
        acc = state[2] * head_mask / state[1]
        mixed[g] = jnp.sum(acc.reshape(HL, ROWS, LANES), axis=0)

    def attend(g, carry):
        finish(g, attend_part(g, 0, half, None))
        return carry

    cut = (groups - 2) * ROWS
    out_parts = [(0, cut), (cut, here - cut)]

    def hand_out(i):
        at, n = out_parts[i]
        mix_rows = mixed[at // ROWS : (at + n) // ROWS].reshape(n, LANES)
        out_rows = (mix_rows * gate[at : at + n]).astype(BF16)
        term = dot(out_rows[:, 0:columns], out_v[...])
        for k in range(1, Y):
            fin_s[k, at : at + n] = term[:, k * LANES : (k + 1) * LANES].astype(BF16)
        for j in range(Y - 1):
            target = j + (y <= j).astype(jnp.int32)
            k = lax.rem(target - y + Y, Y)
            some = pl.ds(at, n)
            remote(
                fin_s.at[k, some],
                fin_r.at[Y - k, some],
                fin_ss.at[i],
                fin_rs.at[i],
                {"head": target},
            ).start()
        return residual[at : at + n] + term[:, 0:LANES]

    def take_in(i, result):
        at, n = out_parts[i]
        part = fin_r.at[pl.ds(1, Y - 1), pl.ds(at, n)]
        sent = fin_s.at[pl.ds(1, Y - 1), pl.ds(at, n)]
        remote(sent, part, fin_ss.at[i], fin_rs.at[i], up).wait()
        for k in range(1, Y):
            result = result + fin_r[k, at : at + n].astype(F32)
        token_out[at : at + n] = result[:, 0:columns].astype(BF16)

    for g in range(0, groups - 2, 2):
        for kind in (FWD_UP, FWD_DN):
            pieces(kind, g, 2).wait_recv()
        lax.fori_loop(g, g + 2, attend, 0)
    early_rows = hand_out(0)
    for kind in (FWD_UP, FWD_DN):
        piece(kind, groups - 2).wait_recv()
    attend(groups - 2, 0)
    state = None
    for at, width in last_parts:
        for kind in (FWD_UP, FWD_DN):
            part_of(kind, groups - 1, at, width, landed_last(kind, at)).wait_recv()
        state = attend_part(groups - 1, at, width, state)
    finish(groups - 1, state)

    late_rows = hand_out(1)
    peers = pl.ds(1, Y - 1)
    remote(codes_s, codes_s, y_s, w_r.at[0], up).wait_send()
    remote(weights.at[peers], weights.at[peers], w_s, w_r.at[0], up).wait_send()
    if zs > 1:
        remote(others_z, others_z, z_s, z_r, other).wait_send()
    x_sent = kv_all.at[:, pl.ds(0, 3 if xs > 2 else 1), c]
    remote(x_sent, x_sent, x_s, x_r.at[0], other).wait_send()
    remote(kv_all.at[:, :, c], kv_all.at[:, :, c], c_s, c_r, other).wait_send()
    take_in(0, early_rows)
    take_in(1, late_rows)


def hand_over(a, b, a_out, b_out, sems):
    copies = [
        pltpu.make_async_copy(a, a_out, sems.at[0]),
        pltpu.make_async_copy(b, b_out, sems.at[1]),
    ]
    for copy in copies:
        copy.start()
    for copy in copies:
        copy.wait()


def per_device(
    atom_single,
    atom_bias,
    atom_token,
    atom_count,
    token_single,
    pair,
    atom_qkv,
    atom_wo,
    atom_agg,
    token_qkvg,
    pair_weight,
    token_wo,
):
    devs = lax.axis_size("tok")
    xs = 4 if devs % 32 == 0 else 2
    zs = devs // (xs * CORES)
    atoms, width = atom_single.shape
    here, width_t = token_single.shape
    keys = pair.shape[2]
    groups = here // ROWS
    half = keys // 2
    columns = width_t // Y
    depth = ROWS * CH
    anywhere = pl.BlockSpec(memory_space=pl.ANY)
    vmem = pl.BlockSpec(memory_space=pltpu.VMEM)
    dma = pltpu.SemaphoreType.DMA
    code = pltpu.VMEM((groups, CHUNK, half), I16)
    operands = (
        atom_single,
        atom_bias.reshape(atoms * ATOM_HEADS, WK),
        atom_token.reshape(1, atoms),
        atom_count.reshape(1, here),
        token_single,
        pair.reshape(here * CH, keys),
        jnp.transpose(atom_qkv, (1, 0, 2)),
        atom_wo,
        atom_agg,
        token_qkvg,
        jnp.transpose(pair_weight),
        token_wo,
    )
    scratch = [
        pltpu.VMEM((atoms, width), BF16),
        pltpu.VMEM((atoms * ATOM_HEADS, WK), BF16),
        pltpu.VMEM((1, atoms), jnp.int32),
        pltpu.VMEM((1, here), jnp.int32),
        pltpu.VMEM((here, width_t), BF16),
        pltpu.VMEM((groups, depth, keys), BF16),
        pltpu.VMEM((3, width, width), BF16),
        pltpu.VMEM(atom_wo.shape, BF16),
        pltpu.VMEM(atom_agg.shape, BF16),
        pltpu.VMEM(token_qkvg.shape, BF16),
        pltpu.VMEM(token_wo.shape, BF16),
        pltpu.VMEM((atoms + 2 * RIM, 2 * width), BF16),
        pltpu.VMEM((Y, Y * HL, CH), BF16),
        pltpu.VMEM((groups, CHUNK, keys), F32),
        pltpu.VMEM((groups, CHUNK, half), F32),
        pltpu.VMEM((groups, CHUNK, half), F32),
        pltpu.VMEM((6, groups, CHUNK, half), I16),
        *([code] * 6),
        pltpu.VMEM((BLOCK_DEVS, here, width_t), BF16),
        pltpu.VMEM((BLOCK_DEVS, here, width_t), BF16),
        pltpu.VMEM((zs, xs, CORES, here, 2 * LANES), BF16),
        pltpu.VMEM((groups, CHUNK, keys), F32),
        pltpu.VMEM((groups, ROWS, LANES), F32),
        pltpu.VMEM((Y, here, LANES), BF16),
        pltpu.VMEM((Y, here, LANES), BF16),
        pltpu.VMEM((width_t, 4 * LANES), BF16),
        pltpu.VMEM((columns, Y * LANES), BF16),
        dma((11,)),
        dma((6,)),
        dma((2,)),
        dma((2,)),
        dma,
        dma((2,)),
        dma,
        dma((2, groups // 2)),
        dma((2,)),
        dma((2, groups // 2 + 2)),
        dma,
        dma,
        dma,
        dma,
        dma,
        dma((3,)),
        dma,
        dma,
        dma((2,)),
        dma((2,)),
        pltpu.SemaphoreType.REGULAR((3,)),
        pltpu.SemaphoreType.REGULAR,
        pltpu.SemaphoreType.REGULAR,
    ]
    outs = (
        pltpu.VMEM((atoms, width), BF16),
        pltpu.VMEM((here, columns), BF16),
    )
    results = pl.pallas_call(
        functools.partial(fused, zs, xs),
        out_shape=outs,
        in_specs=[anywhere] * len(operands),
        out_specs=(vmem, vmem),
        scratch_shapes=scratch,
        compiler_params=pltpu.CompilerParams(
            collective_id=0, has_side_effects=True, vmem_limit_bytes=56 * 2**20
        ),
    )(*operands)
    results = [pltpu.with_memory_space_constraint(r, pltpu.VMEM) for r in results]
    return pl.pallas_call(
        hand_over,
        out_shape=tuple(pltpu.HBM(r.shape, r.dtype) for r in results),
        in_specs=[anywhere, anywhere],
        out_specs=(anywhere, anywhere),
        scratch_shapes=[dma((2,))],
    )(*results)


def solution(mesh):
    in_specs = (
        P("tok", None),
        P("tok", None, None),
        P("tok"),
        P("tok"),
        P("tok", None),
        P("tok", "head", None),
        P(),
        P(),
        P(),
        P(),
        P("head", None),
        P("head", None),
    )
    out_specs = (P("tok", None), P("tok", "head"))
    return jax.shard_map(
        per_device, mesh=mesh, in_specs=in_specs, out_specs=out_specs, check_vma=False
    )
```
